32 devices in a mesh: dp: 2 (over y), ctx: 4 (over z), fsdp: 4 (over x, core).
Axes of the slice: x: 2, y: 2, z: 4, core: 2. Of those that a mesh axis runs over, the one named last changes fastest.
Arguments:
- hidden: bfloat16 [8, 512, 2048], P(('dp', 'fsdp'), 'ctx'), may hold values from -6 to 6
- cotangent: bfloat16 [8, 512, 2048], P(('dp', 'fsdp'), 'ctx'), may hold values from -6 to 6
- span_order: int32 [8], replicated, may hold values from 0 to 7, each once
- norm_gains: float32 [2, 2048], P(None, ('dp', 'ctx', 'fsdp')), may hold values from 0.5 to 1.5
- w_qkv: float32 [2048, 3072], P(('dp', 'ctx', 'fsdp')), may hold values from -0.125 to 0.125
- w_out: float32 [2048, 2048], P(('dp', 'ctx', 'fsdp')), may hold values from -1 to 1
- w_gate_up: float32 [2048, 16384], P(('dp', 'ctx', 'fsdp')), may hold values from -0.125 to 0.125
- w_down: float32 [2048, 8192], P(('dp', 'ctx', 'fsdp')), may hold values from -0.0625 to 0.0625
- mom_gains: float32 [2, 2, 2048], P(None, None, ('dp', 'ctx', 'fsdp')), as said below
- mom_qkv: float32 [2, 2048, 3072], P(None, ('dp', 'ctx', 'fsdp')), as said below
- mom_out: float32 [2, 2048, 2048], P(None, ('dp', 'ctx', 'fsdp')), as said below
- mom_gate_up: float32 [2, 2048, 16384], P(None, ('dp', 'ctx', 'fsdp')), as said below
- mom_down: float32 [2, 2048, 8192], P(None, ('dp', 'ctx', 'fsdp')), as said below
Outputs:
- output: bfloat16 [8, 512, 2048], P(('dp', 'fsdp'), 'ctx')
- grad_hidden: bfloat16 [8, 512, 2048], P(('dp', 'fsdp'), 'ctx')
- grad_gains: float32 [2, 2048], P(None, ('dp', 'ctx', 'fsdp'))
- grad_qkv: float32 [2048, 3072], P(('dp', 'ctx', 'fsdp'))
- grad_out: float32 [2048, 2048], P(('dp', 'ctx', 'fsdp'))
- grad_gate_up: float32 [2048, 16384], P(('dp', 'ctx', 'fsdp'))
- grad_down: float32 [2048, 8192], P(('dp', 'ctx', 'fsdp'))
- new_gains: float32 [2, 2048], P(None, ('dp', 'ctx', 'fsdp'))
- new_qkv: float32 [2048, 3072], P(('dp', 'ctx', 'fsdp'))
- new_out: float32 [2048, 2048], P(('dp', 'ctx', 'fsdp'))
- new_gate_up: float32 [2048, 16384], P(('dp', 'ctx', 'fsdp'))
- new_down: float32 [2048, 8192], P(('dp', 'ctx', 'fsdp'))
- new_mom_gains: float32 [2, 2, 2048], P(None, None, ('dp', 'ctx', 'fsdp'))
- new_mom_qkv: float32 [2, 2048, 3072], P(None, ('dp', 'ctx', 'fsdp'))
- new_mom_out: float32 [2, 2048, 2048], P(None, ('dp', 'ctx', 'fsdp'))
- new_mom_gate_up: float32 [2, 2048, 16384], P(None, ('dp', 'ctx', 'fsdp'))
- new_mom_down: float32 [2, 2048, 8192], P(None, ('dp', 'ctx', 'fsdp'))
The draws below stay inside these ranges and needn't reach their ends.
Inputs may be any that keep to these rules, and one draw needn't show every extreme that they name: `span_order`: each span number appears exactly once. `mom_gains`: index 0 of the first dimension holds first moments, index 1 roots of second moments, which are positive. `mom_qkv`: index 0 of the first dimension holds first moments, index 1 roots of second moments, which are positive. `mom_out`: index 0 of the first dimension holds first moments, index 1 roots of second moments, which are positive. `mom_gate_up`: index 0 of the first dimension holds first moments, index 1 roots of second moments, which are positive. `mom_down`: index 0 of the first dimension holds first moments, index 1 roots of second moments, which are positive.
All inputs are finite; a program needn't handle non-finite values.
Results may differ from the reference program's by a relative error of at most 0.015.
Values may be sent and summed in bfloat16 or wider, within the bound.
A program may use at most 768 MiB of HBM per device.

```python
import math
import jax
import jax.numpy as jnp
from jax import lax

D = 2048
H = 32
KV = 8
HD = 64
FF = 8192
CH = 64
SPANS = 8
L = 512
SEQS = 8


def moment_pair(key, shape, grad_square):
    first_key, second_key = jax.random.split(jax.random.fold_in(key, 7))
    grad_size = math.sqrt(grad_square)
    first_mom = 0.1 * grad_size * jax.random.truncated_normal(first_key, -6.0, 6.0, shape, jnp.float32)
    factor = jnp.exp(jax.random.uniform(second_key, shape, jnp.float32, math.log(0.5), math.log(2.0)))
    root_mom = math.sqrt(2.0 * 0.05 / 0.95 * grad_square) * jnp.sqrt(factor)
    return jnp.stack([first_mom, root_mom])


def attention_sum():
    return SEQS * (math.log(L) + 0.6)


def draw_mom_gains(key, part):
    first_rows = moment_pair(jax.random.fold_in(key, 1), (1, D), 96.0 * attention_sum())
    second_rows = moment_pair(jax.random.fold_in(key, 2), (1, D), 0.8 * SEQS * L)
    return jnp.concatenate([first_rows, second_rows], 1)


def draw_mom_qkv(key, part):
    return moment_pair(key, (D, (H + 2 * KV) * HD), 128.0 * attention_sum())


def draw_mom_out(key, part):
    return moment_pair(key, (D, H * HD), 1.2 * attention_sum())


def draw_mom_gate_up(key, part):
    return moment_pair(key, (D, 2 * FF), 0.1 * SEQS * L)


def draw_mom_down(key, part):
    return moment_pair(key, (D, FF), 0.35 * SEQS * L)


def strengthened(values, own_key, source, target, shards_of, factor):
    def block_of(position):
        return (jnp.arange(values.shape[position]) // (values.shape[position] // shards_of)).reshape((-1,) + (1,) * (values.ndim - 1 - position))

    first = jax.random.permutation(own_key, shards_of)[block_of(target)]
    far = (block_of(target) + shards_of // 2) % shards_of
    return jnp.where((block_of(source) == first) | (block_of(source) == far), factor * values, values)


def steps_of(stream_key, dims, pieces, least, top_value):
    def one(axis_at, blocks):
        draws = jax.random.uniform(jax.random.fold_in(jax.random.fold_in(stream_key, 6), axis_at), (blocks,), jnp.float32, least / len(pieces), top_value / len(pieces))
        return jnp.repeat(jnp.exp(draws), dims[axis_at] // blocks).reshape((-1,) + (1,) * (len(dims) - axis_at - 1))

    loudness = one(*pieces[0])
    for cut in pieces[1:]:
        loudness = loudness * one(*cut)
    return loudness


def gaussian(rng, extent, deviation, most, cuts=(), kind=jnp.bfloat16):
    loudness = steps_of(rng, extent, cuts, -0.22, 0.18) if cuts else 1.0
    values = jax.random.normal(rng, extent, jnp.float32) * deviation * loudness
    return jnp.minimum(jnp.maximum(values, -most), most).astype(kind)


def gaussian_with(rng, dims, width, limit, cuts, heavy, kind=jnp.bfloat16):
    array = width * jax.random.normal(rng, dims, jnp.float32)
    if cuts:
        array = array * steps_of(rng, dims, cuts, -0.22, 0.18)
    return jnp.clip(strengthened(array, jax.random.fold_in(rng, 3), *heavy), -limit, limit).astype(kind)


def setup_inputs(seed: int = 0) -> dict:
    key_of = jax.random.split(jax.random.key(seed), 14)
    hidden = gaussian(key_of[0], (SEQS, L, D), 1.0, 6.0, ((0, 8), (1, 4)))
    cotangent = gaussian_with(key_of[1], (SEQS, L, D), 1.0, 6.0, ((0, 8), (1, 4)), (0, 2, 8, 2.0))
    span_order = jax.random.permutation(key_of[2], SPANS).astype(jnp.int32)
    norm_gains = jnp.clip(1.0 + 0.1 * jax.random.normal(key_of[3], (2, D), jnp.float32), 0.5, 1.5)
    w_qkv = gaussian(key_of[4], (D, (H + 2 * KV) * HD), D ** -0.5, 0.125, ((0, 32),), jnp.float32)
    w_out = gaussian(key_of[5], (D, H * HD), (H * HD // 64) ** -0.5, 1.0, ((0, 32),), jnp.float32)
    w_gate_up = gaussian(key_of[6], (D, 2 * FF), D ** -0.5, 0.125, ((0, 32),), jnp.float32)
    w_down = gaussian(key_of[7], (D, FF), FF ** -0.5, 0.0625, ((0, 32),), jnp.float32)
    mom_gains = draw_mom_gains(jax.random.fold_in(key_of[13], 71), 0)
    mom_qkv = draw_mom_qkv(jax.random.fold_in(key_of[13], 71), 0)
    mom_out = draw_mom_out(jax.random.fold_in(key_of[13], 71), 0)
    mom_gate_up = draw_mom_gate_up(jax.random.fold_in(key_of[13], 71), 0)
    mom_down = draw_mom_down(jax.random.fold_in(key_of[13], 71), 0)
    return dict(hidden=hidden, cotangent=cotangent, span_order=span_order, norm_gains=norm_gains, w_qkv=w_qkv, w_out=w_out, w_gate_up=w_gate_up, w_down=w_down, mom_gains=mom_gains, mom_qkv=mom_qkv, mom_out=mom_out, mom_gate_up=mom_gate_up, mom_down=mom_down)


HIGHEST = lax.Precision.HIGHEST
EPS_NORM = 1e-05
NEG_FILL = -1000000000.0
THETA = 500000.0
BETA_ONE = 0.9
BETA_TWO = 0.95
ADAM_EPS = 1e-08
DECAY_MATRIX = 0.1
LR_MATRIX = 0.01
LR_OUTPUT = 0.06
LR_GAIN = 0.3

@jax.custom_vjp
def low(v):
    return lax.optimization_barrier(v.astype(jnp.bfloat16)).astype(jnp.float32)

@jax.custom_vjp
def low_back(v):
    return v

def low_keep(v):
    return (low(v), None)

def low_pass(kept, grad):
    return (grad,)

def back_keep(v):
    return (v, None)

def back_low(kept, grad):
    return (low(grad),)
low.defvjp(low_keep, low_pass)
low_back.defvjp(back_keep, back_low)

def rope_table(positions):
    half_dim = HD // 2
    index_row = jnp.arange(half_dim, dtype=jnp.float32)
    frequency = jnp.exp(-(2.0 * index_row / HD) * math.log(THETA))
    wavelen = 2.0 * math.pi / frequency
    smooth = (8192.0 / wavelen - 1.0) / 3.0
    scaled = jnp.where(wavelen < 2048.0, frequency, jnp.where(wavelen > 8192.0, frequency / 32.0, (1.0 - smooth) * frequency / 32.0 + smooth * frequency))
    angles = positions.astype(jnp.float32)[:, None] * scaled[None, :]
    cosine = jnp.cos(angles)
    sine_part = jnp.sin(angles)
    return (jnp.concatenate([cosine, cosine], 1), jnp.concatenate([sine_part, sine_part], 1))

def rope_apply(values_in, cos_tab, sin_tab):
    half_dim = values_in.shape[-1] // 2
    turned = jnp.concatenate([-values_in[..., half_dim:], values_in[..., :half_dim]], -1)
    return values_in * cos_tab[:, None, :] + turned * sin_tab[:, None, :]

def rms_norm(values_in):
    return values_in * lax.rsqrt(lax.optimization_barrier(jnp.mean(values_in * values_in, -1, keepdims=True)) + EPS_NORM)

def attend(queries, key_rows, value_rows, visible):
    seq_len = queries.shape[0]
    groups = H // KV
    query_groups = queries.reshape(seq_len, KV, groups, HD).transpose(1, 0, 2, 3)
    key_groups = key_rows.transpose(1, 0, 2)
    value_groups = value_rows.transpose(1, 0, 2)

    def one_group(group_items):
        query_h, key_h, value_h = group_items
        scores = low_back(jnp.einsum('tgd,sd->gts', query_h, key_h, precision=HIGHEST) * HD ** (-0.5))
        scores = jnp.where(visible[None], scores, NEG_FILL)
        probability = jax.nn.softmax(scores, axis=-1)
        return jnp.einsum('gts,sd->tgd', low(probability), value_h, precision=HIGHEST)
    outputs = lax.map(jax.checkpoint(one_group), (query_groups, key_groups, value_groups))
    return outputs.transpose(1, 0, 2, 3).reshape(seq_len, H * HD)

def layer(hidden_row, gains, qkv_w, out_w, gate_up_w, down_w, cos_tab, sin_tab, visible):
    gains_c = low(gains)
    qkv_c = low(qkv_w)
    out_c = low(out_w)
    gate_up_c = low(gate_up_w)
    down_c = low(down_w)
    seq_len = hidden_row.shape[0]
    entry_one = low(rms_norm(hidden_row) * gains_c[0])
    projected = low_back(jnp.dot(entry_one, qkv_c, precision=HIGHEST))
    queries = projected[:, :H * HD].reshape(seq_len, H, HD)
    key_rows = projected[:, H * HD:(H + KV) * HD].reshape(seq_len, KV, HD)
    value_rows = projected[:, (H + KV) * HD:].reshape(seq_len, KV, HD)
    attended = attend(low(rope_apply(queries, cos_tab, sin_tab)), low(rope_apply(key_rows, cos_tab, sin_tab)), low(value_rows), visible)
    attended = low(low_back(attended))
    middle = hidden_row + low_back(jnp.dot(attended, out_c.T, precision=HIGHEST))
    entry_two = low(rms_norm(middle) * gains_c[1])
    gate_up = low_back(jnp.dot(entry_two, gate_up_c, precision=HIGHEST))
    activated = low(jax.nn.silu(gate_up[:, :FF]) * gate_up[:, FF:])
    return middle + low_back(jnp.dot(activated, down_c.T, precision=HIGHEST))

def adamw(weight, gradient, states, step_rate, decay_rate):
    first_mom = BETA_ONE * states[0] + (1.0 - BETA_ONE) * gradient
    root_mom = jnp.sqrt(BETA_TWO * states[1] * states[1] + (1.0 - BETA_TWO) * gradient * gradient)
    first_hat = first_mom / (1.0 - BETA_ONE ** 3)
    root_hat = root_mom / math.sqrt(1.0 - BETA_TWO ** 3)
    updated = weight - step_rate * (first_hat / (root_hat + ADAM_EPS) + decay_rate * weight)
    return (updated, jnp.stack([first_mom, root_mom]))

def reference(hidden, cotangent, span_order, norm_gains, w_qkv, w_out, w_gate_up, w_down, mom_gains, mom_qkv, mom_out, mom_gate_up, mom_down):
    positions = (span_order[:, None] * CH + jnp.arange(CH, dtype=jnp.int32)[None, :]).reshape(-1).astype(jnp.int32)
    cos_tab, sin_tab = rope_table(positions)
    visible = positions[None, :] <= positions[:, None]
    params = (norm_gains, w_qkv, w_out, w_gate_up, w_down)

    def layer_fn(hidden_row, gains, qkv_w, out_w, gate_up_w, down_w):
        return layer(hidden_row, gains, qkv_w, out_w, gate_up_w, down_w, cos_tab, sin_tab, visible)

    def per_sequence(totals, seq_pair):
        hidden_row, cot_row = seq_pair
        result, pull_back = jax.vjp(layer_fn, hidden_row.astype(jnp.float32), norm_gains, w_qkv, w_out, w_gate_up, w_down)
        gradients = pull_back(cot_row.astype(jnp.float32))
        totals = tuple((running + gradient for running, gradient in zip(totals, gradients[1:])))
        return (totals, (result.astype(jnp.bfloat16), gradients[0].astype(jnp.bfloat16)))
    start_totals = tuple((jnp.zeros(param_arr.shape, jnp.float32) for param_arr in params))
    totals, (output, grad_hidden) = lax.scan(per_sequence, start_totals, (hidden, cotangent))
    grad_gains, grad_qkv, grad_out, grad_gate_up, grad_down = totals
    new_gains, new_mom_gains = adamw(norm_gains, grad_gains, mom_gains, LR_GAIN, 0.0)
    new_qkv, new_mom_qkv = adamw(w_qkv, grad_qkv, mom_qkv, LR_MATRIX, DECAY_MATRIX)
    new_out, new_mom_out = adamw(w_out, grad_out, mom_out, LR_OUTPUT, DECAY_MATRIX)
    new_gate_up, new_mom_gate_up = adamw(w_gate_up, grad_gate_up, mom_gate_up, LR_MATRIX, DECAY_MATRIX)
    new_down, new_mom_down = adamw(w_down, grad_down, mom_down, LR_MATRIX, DECAY_MATRIX)
    return (output, grad_hidden, grad_gains, grad_qkv, grad_out, grad_gate_up, grad_down, new_gains, new_qkv, new_out, new_gate_up, new_down, new_mom_gains, new_mom_qkv, new_mom_out, new_mom_gate_up, new_mom_down)
```

```python
import functools
import math

import jax
import jax.numpy as jnp
from jax import lax
from jax.experimental import pallas as pl
from jax.experimental.pallas import tpu as pltpu
from jax.sharding import Mesh
from jax.sharding import PartitionSpec as P

MESH = pl.DeviceIdType.MESH
BF = jnp.bfloat16
F32 = jnp.float32
H = 32
KV = 8
HD = 64
FF = 8192


EPS_NORM = 1e-05
NEG_FILL = -1000000000.0
THETA = 500000.0
BETA_ONE = 0.9
BETA_TWO = 0.95
ADAM_EPS = 1e-08
DECAY_MATRIX = 0.1
LR_MATRIX = 0.01
LR_OUTPUT = 0.06
LR_GAIN = 0.3


def rope_table(positions):
    half_dim = HD // 2
    index_row = jnp.arange(half_dim, dtype=jnp.float32)
    frequency = jnp.exp(-(2.0 * index_row / HD) * math.log(THETA))
    wavelen = 2.0 * math.pi / frequency
    smooth = (8192.0 / wavelen - 1.0) / 3.0
    scaled = jnp.where(
        wavelen < 2048.0,
        frequency,
        jnp.where(
            wavelen > 8192.0,
            frequency / 32.0,
            (1.0 - smooth) * frequency / 32.0 + smooth * frequency,
        ),
    )
    angles = positions.astype(jnp.float32)[:, None] * scaled[None, :]
    cosine = jnp.cos(angles)
    sine_part = jnp.sin(angles)
    return (jnp.concatenate([cosine, cosine], 1), jnp.concatenate([sine_part, sine_part], 1))


def adamw(weight, gradient, states, step_rate, decay_rate):
    first_mom = BETA_ONE * states[0] + (1.0 - BETA_ONE) * gradient
    root_mom = jnp.sqrt(BETA_TWO * states[1] * states[1] + (1.0 - BETA_TWO) * gradient * gradient)
    first_hat = first_mom / (1.0 - BETA_ONE**3)
    root_hat = root_mom / math.sqrt(1.0 - BETA_TWO**3)
    updated = weight - step_rate * (first_hat / (root_hat + ADAM_EPS) + decay_rate * weight)
    return (updated, jnp.stack([first_mom, root_mom]))


def contract_rows(left_arr, right_arr):
    return lax.dot_general(
        left_arr, right_arr, (((0,), (0,)), ((), ())), preferred_element_type=jnp.float32
    )


def contract_cols(left_arr, right_arr):
    return lax.dot_general(
        left_arr, right_arr, (((1,), (1,)), ((), ())), preferred_element_type=jnp.float32
    )


def wrap(value, size):
    return lax.rem(value + size, size)


def remote(src, dst, send_sem, recv_sem, **where):
    return pltpu.make_async_remote_copy(
        src_ref=src,
        dst_ref=dst,
        send_sem=send_sem,
        recv_sem=recv_sem,
        device_id=where,
        device_id_type=MESH,
    )


def greet(places):
    barrier = pltpu.get_barrier_semaphore()
    for where in places:
        pl.semaphore_signal(barrier, inc=1, device_id=where, device_id_type=MESH)
    pl.semaphore_wait(barrier, len(places))


def greet_line(line, pair):
    barrier = pltpu.get_barrier_semaphore()
    here = lax.axis_index("ctx")

    @pl.when(here > 0)
    def _():
        pl.semaphore_signal(barrier, inc=1, device_id={"ctx": here - 1}, device_id_type=MESH)

    @pl.when(here < line - 1)
    def _():
        pl.semaphore_signal(barrier, inc=1, device_id={"ctx": here + 1}, device_id_type=MESH)

    if pair > 1:
        pl.semaphore_signal(
            barrier, inc=1, device_id={"core": 1 - lax.axis_index("core")}, device_id_type=MESH
        )
    ends = (here == 0).astype(jnp.int32) + (here == line - 1).astype(jnp.int32)
    pl.semaphore_wait(barrier, 2 - ends + (1 if pair > 1 else 0))


def gather_kernel(line, pair, many, *refs):
    ins, outs = refs[:many], refs[many : 2 * many]
    own_sem, line_send, line_recv, core_send, core_recv = refs[2 * many :]
    here = lax.axis_index("ctx")
    core = lax.axis_index("core")
    greet_line(line, pair)

    def hop(item, way, step, source=None):
        block = here - step if way == 0 else here + step
        target = here + 1 if way == 0 else here - 1
        place = outs[item].at[core, block]
        return remote(
            place if source is None else source,
            place,
            line_send.at[item, way, step],
            line_recv.at[item, way, step],
            ctx=target,
        )

    def arrived(item, way, step):
        block = here - 1 - step if way == 0 else here + 1 + step
        place = outs[item].at[core, block]
        return remote(
            place, place, line_send.at[item, way, step], line_recv.at[item, way, step], ctx=here
        )

    def share(item, way, step, source=None):
        block = here - 1 - step if way == 0 else here + 1 + step
        place = outs[item].at[core, block]
        return remote(
            place if source is None else source,
            place,
            core_send.at[item, way, step + 1],
            core_recv.at[item, way, step + 1],
            core=1 - core,
        )

    def shared(item, way, step):
        block = here - 1 - step if way == 0 else here + 1 + step
        place = outs[item].at[1 - core, block]
        return remote(
            place,
            place,
            core_send.at[item, way, step + 1],
            core_recv.at[item, way, step + 1],
            core=1 - core,
        )

    def sends(way):
        return here < line - 1 if way == 0 else here > 0

    def has(way, step):
        return here - 1 - step >= 0 if way == 0 else here + 1 + step <= line - 1

    for item in range(many):
        for way in range(2):

            @pl.when(sends(way))
            def _(item=item, way=way):
                hop(item, way, 0, ins[item]).start()

        if pair > 1:
            share(item, 0, -1, ins[item]).start()
        pltpu.make_async_copy(ins[item], outs[item].at[core, here], own_sem.at[item]).start()
    for step in range(line - 1):
        for item in range(many):
            for way in range(2):

                @pl.when(has(way, step))
                def _(item=item, way=way, step=step):
                    arrived(item, way, step).wait_recv()
                    if step + 1 < line - 1:

                        @pl.when(sends(way))
                        def _():
                            hop(item, way, step + 1).start()

                    if pair > 1:
                        share(item, way, step).start()

    for item in range(many):
        pltpu.make_async_copy(ins[item], outs[item].at[core, here], own_sem.at[item]).wait()
        if pair > 1:
            share(item, 0, -1, ins[item]).wait_send()
            shared(item, 0, -1).wait_recv()
        for way in range(2):

            @pl.when(sends(way))
            def _(item=item, way=way):
                hop(item, way, 0, ins[item]).wait_send()

            for step in range(line - 1):

                @pl.when(has(way, step))
                def _(item=item, way=way, step=step):
                    if step + 1 < line - 1:

                        @pl.when(sends(way))
                        def _():
                            hop(item, way, step + 1).wait_send()

                    if pair > 1:
                        share(item, way, step).wait_send()
                        shared(item, way, step).wait_recv()


def gather_tokens(sizes, collective_id, *arrays):
    line, pair = sizes["ctx"], sizes["core"]
    many = len(arrays)
    any_spec = pl.BlockSpec(memory_space=pl.ANY)
    outs = pl.pallas_call(
        functools.partial(gather_kernel, line, pair, many),
        out_shape=[jax.ShapeDtypeStruct((pair, line) + a.shape, a.dtype) for a in arrays],
        in_specs=[any_spec] * many,
        out_specs=[any_spec] * many,
        scratch_shapes=[
            pltpu.SemaphoreType.DMA((many,)),
            pltpu.SemaphoreType.DMA((many, 2, line)),
            pltpu.SemaphoreType.DMA((many, 2, line)),
            pltpu.SemaphoreType.DMA((many, 2, line)),
            pltpu.SemaphoreType.DMA((many, 2, line)),
        ],
        compiler_params=pltpu.CompilerParams(collective_id=collective_id, has_side_effects=True),
    )(*arrays)
    return [o.reshape((-1,) + a.shape[1:]) for o, a in zip(outs, arrays)]


def add_rows(rows, out_ref, *parts):
    def one(index, carry):
        at = pl.ds(pl.multiple_of(index * 16, 16), 16)
        total = parts[0][at, :].astype(F32)
        for part in parts[1:]:
            total = total + part[at, :].astype(F32)
        out_ref[at, :] = total.astype(out_ref.dtype)
        return carry

    lax.fori_loop(0, rows // 16, one, 0)


def scatter_kernel(line, pair, part_ref, out_ref, near, mine, going, landed, core_send, core_recv, line_send, line_recv):
    rows = out_ref.shape[0]
    here = lax.axis_index("ctx")
    core = lax.axis_index("core")
    greet_line(line, pair)

    def to_core(block):
        return remote(
            part_ref.at[1 - core, block],
            near.at[block],
            core_send.at[block],
            core_recv.at[block],
            core=1 - core,
        )

    def onward(way, block):
        return remote(
            going.at[way, block],
            landed.at[way, block],
            line_send.at[way, block],
            line_recv.at[way, block],
            ctx=here + 1 if way == 0 else here - 1,
        )

    order = []
    for step in range(line):
        order += [line - 1 - step, step]
    order = list(dict.fromkeys(order))
    if pair > 1:
        for block in order:
            to_core(block).start()
    ready = set()
    for step in range(line):
        for way, block in ((0, line - 1 - step), (1, step)):
            if block not in ready:
                ready.add(block)
                if pair > 1:
                    to_core(block).wait_recv()
            goes = here < block if way == 0 else here > block
            first = here == 0 if way == 0 else here == line - 1

            @pl.when(goes & first)
            def _(way=way, block=block):
                terms = [part_ref.at[core, block]] + ([near.at[block]] if pair > 1 else [])
                add_rows(rows, going.at[way, block], *terms)
                onward(way, block).start()

            @pl.when(goes & jnp.logical_not(first))
            def _(way=way, block=block):
                onward(way, block).wait_recv()
                terms = [part_ref.at[core, block]] + ([near.at[block]] if pair > 1 else [])
                add_rows(rows, going.at[way, block], *terms, landed.at[way, block])
                onward(way, block).start()

    for block in range(line):

        @pl.when(here == block)
        def _(block=block):
            terms = [part_ref.at[core, block]] + ([near.at[block]] if pair > 1 else [])
            if block > 0:
                onward(0, block).wait_recv()
                terms.append(landed.at[0, block])
            if block < line - 1:
                onward(1, block).wait_recv()
                terms.append(landed.at[1, block])
            add_rows(rows, out_ref, *terms)

    for block in range(line):
        if pair > 1:
            to_core(block).wait_send()
        for way in range(2):
            goes = here < block if way == 0 else here > block

            @pl.when(goes)
            def _(way=way, block=block):
                onward(way, block).wait_send()


def scatter_tokens(sizes, collective_id, terms):
    line, pair = sizes["ctx"], sizes["core"]
    columns = terms.shape[1]
    rows = terms.shape[0] // (line * pair)
    vmem = pl.BlockSpec(memory_space=pltpu.VMEM)
    return pl.pallas_call(
        functools.partial(scatter_kernel, line, pair),
        out_shape=jax.ShapeDtypeStruct((rows, columns), F32),
        in_specs=[vmem],
        out_specs=vmem,
        scratch_shapes=[
            pltpu.VMEM((line, rows, columns), BF),
            pltpu.VMEM((8, 128), F32),
            pltpu.VMEM((2, line, rows, columns), BF),
            pltpu.VMEM((2, line, rows, columns), BF),
            pltpu.SemaphoreType.DMA((line,)),
            pltpu.SemaphoreType.DMA((line,)),
            pltpu.SemaphoreType.DMA((2, line)),
            pltpu.SemaphoreType.DMA((2, line)),
        ],
        compiler_params=pltpu.CompilerParams(
            collective_id=collective_id, has_side_effects=True, vmem_limit_bytes=50 * 2**20
        ),
    )(terms.reshape(pair, line, rows, columns))


def blocks_in_order(line, pair):
    away = sorted(range(line), key=lambda d: min(d, line - d))
    return [(dz, dc) for dz in away for dc in range(pair)]


def greet_all(sizes):
    names = ("dp", "ctx", "x", "core")
    at = {name: lax.axis_index(name) for name in names}
    places = []
    for dz, dc in blocks_in_order(sizes["ctx"], sizes["core"]):
        if dz or dc:
            places.append(
                {"ctx": wrap(at["ctx"] + dz, sizes["ctx"]), "core": wrap(at["core"] + dc, sizes["core"])}
            )
    for name in ("dp", "x"):
        for step in range(1, sizes[name]):
            places.append({name: wrap(at[name] + step, sizes[name])})
    greet(places)


def spread_kernel(sizes, w_ref, o_ref, own_sem, f_send, f_recv, a_send, a_recv, b_send, b_recv):
    line, pair = sizes["ctx"], sizes["core"]
    at = {name: lax.axis_index(name) for name in ("dp", "ctx", "x", "core")}
    greet_all(sizes)
    order = blocks_in_order(line, pair)

    def first(index):
        dz, dc = order[index]
        z, c = wrap(at["ctx"] + dz, line), wrap(at["core"] + dc, pair)
        return remote(
            w_ref.at[z * pair + c],
            o_ref.at[at["dp"], at["ctx"], at["x"], at["core"]],
            f_send.at[index],
            f_recv.at[index],
            ctx=z,
            core=c,
        )

    def place(index, moved):
        dz, dc = order[index]
        z, c = wrap(at["ctx"] - dz, line), wrap(at["core"] - dc, pair)
        spot = {name: wrap(at[name] - moved.get(name, 0), sizes[name]) for name in ("dp", "x")}
        return o_ref.at[spot["dp"], z, spot["x"], c]

    def came(index):
        spot = place(index, {})
        return remote(spot, spot, f_send.at[index], f_recv.at[index], core=at["core"])

    def axes(index):
        dz, dc = order[index]
        return ("x", "dp") if (dz + dc) % 2 == 0 else ("dp", "x")

    def hop_one(index, step):
        name = axes(index)[0]
        spot = place(index, {})
        return remote(
            spot,
            spot,
            a_send.at[index, step],
            a_recv.at[index, step],
            **{name: wrap(at[name] + step, sizes[name])},
        )

    def one_came(index, step):
        name = axes(index)[0]
        spot = place(index, {name: step})
        return remote(spot, spot, a_send.at[index, step], a_recv.at[index, step], core=at["core"])

    def hop_two(index, step, far):
        name, other = axes(index)
        spot = place(index, {name: step})
        return remote(
            spot,
            spot,
            b_send.at[index, step, far],
            b_recv.at[index, step, far],
            **{other: wrap(at[other] + far, sizes[other])},
        )

    def two_came(index, step, far):
        name, other = axes(index)
        spot = place(index, {name: step, other: far})
        return remote(
            spot, spot, b_send.at[index, step, far], b_recv.at[index, step, far], core=at["core"]
        )

    own = pltpu.make_async_copy(
        w_ref.at[at["ctx"] * pair + at["core"]],
        o_ref.at[at["dp"], at["ctx"], at["x"], at["core"]],
        own_sem,
    )
    own.start()
    for index in range(1, len(order)):
        first(index).start()
    late = 2
    for tick in range(len(order) + late):
        if tick < len(order):
            if tick == 0:
                own.wait()
            else:
                came(tick).wait_recv()
            name, other = axes(tick)
            for step in range(1, sizes[name]):
                hop_one(tick, step).start()
            for far in range(1, sizes[other]):
                hop_two(tick, 0, far).start()
        if tick >= late:
            index = tick - late
            name, other = axes(index)
            for step in range(1, sizes[name]):
                one_came(index, step).wait_recv()
                for far in range(1, sizes[other]):
                    hop_two(index, step, far).start()
    for index in range(len(order)):
        if index:
            first(index).wait_send()
        name, other = axes(index)
        for step in range(sizes[name]):
            if step:
                hop_one(index, step).wait_send()
            for far in range(1, sizes[other]):
                hop_two(index, step, far).wait_send()
                two_came(index, step, far).wait_recv()


def spread_weights(sizes, collective_id, packed):
    group, rows, columns = packed.shape
    steps = max(sizes["dp"], sizes["x"])
    any_spec = pl.BlockSpec(memory_space=pl.ANY)
    out = pl.pallas_call(
        functools.partial(spread_kernel, sizes),
        out_shape=jax.ShapeDtypeStruct(
            (sizes["dp"], sizes["ctx"], sizes["x"], sizes["core"], rows, columns), packed.dtype
        ),
        in_specs=[any_spec],
        out_specs=any_spec,
        scratch_shapes=[
            pltpu.SemaphoreType.DMA,
            pltpu.SemaphoreType.DMA((group,)),
            pltpu.SemaphoreType.DMA((group,)),
            pltpu.SemaphoreType.DMA((group, steps)),
            pltpu.SemaphoreType.DMA((group, steps)),
            pltpu.SemaphoreType.DMA((group, steps, steps)),
            pltpu.SemaphoreType.DMA((group, steps, steps)),
        ],
        compiler_params=pltpu.CompilerParams(collective_id=collective_id, has_side_effects=True),
    )(packed)
    return out.reshape(-1, columns)


def collect_kernel(
    sizes, g_ref, o_ref, near_a, near_b, part, far_in, done, own_sem, a_send, a_recv, b_send, b_recv, f_send, f_recv
):
    line, pair = sizes["ctx"], sizes["core"]
    rows = o_ref.shape[1]
    at = {name: lax.axis_index(name) for name in ("dp", "ctx", "x", "core")}
    greet_all(sizes)
    order = blocks_in_order(line, pair)[::-1]
    me = at["ctx"] * pair + at["core"]

    def spot_of(index):
        dz, dc = order[index]
        return wrap(at["ctx"] + dz, line), wrap(at["core"] + dc, pair)

    def axes(index):
        dz, dc = order[index]
        return ("dp", "x") if (dz + dc) % 2 == 0 else ("x", "dp")

    def landing(index, step):
        slot = sum(axes(i)[0] == axes(index)[0] for i in range(index))
        return (near_a if axes(index)[0] == "dp" else near_b).at[slot, step - 1]

    def terms(index, first_at):
        z, c = spot_of(index)
        if axes(index)[0] == "dp":
            return g_ref.at[first_at, z, :, c]
        return g_ref.at[:, z, first_at, c]

    def hop_one(index, step):
        name = axes(index)[0]
        to = wrap(at[name] + step, sizes[name])
        return remote(
            terms(index, to), landing(index, step), a_send.at[index, step], a_recv.at[index, step], **{name: to}
        )

    def hop_two(index, far):
        other = axes(index)[1]
        to = wrap(at[other] + far, sizes[other])
        return remote(
            part.at[index, to], far_in.at[index, far - 1], b_send.at[index, far], b_recv.at[index, far], **{other: to}
        )

    def last(index):
        z, c = spot_of(index)
        return remote(done.at[index], o_ref.at[me], f_send.at[index], f_recv.at[index], ctx=z, core=c)

    def last_came(index):
        dz, dc = order[index]
        z, c = wrap(at["ctx"] - dz, line), wrap(at["core"] - dc, pair)
        spot = o_ref.at[z * pair + c]
        return remote(spot, spot, f_send.at[index], f_recv.at[index], core=at["core"])

    own = pltpu.make_async_copy(done.at[len(order) - 1], o_ref.at[me], own_sem)
    for index in range(len(order)):
        name = axes(index)[0]
        for step in range(1, sizes[name]):
            hop_one(index, step).start()
    late = 2
    for tick in range(len(order) + late):
        if tick < len(order):
            name, other = axes(tick)
            for step in range(1, sizes[name]):
                hop_one(tick, step).wait_recv()
            kept = terms(tick, at[name])
            for place in range(sizes[other]):
                add_rows(
                    rows,
                    part.at[tick, place],
                    kept.at[place],
                    *[landing(tick, step).at[place] for step in range(1, sizes[name])],
                )
            for far in range(1, sizes[other]):
                hop_two(tick, far).start()
        if tick >= late:
            index = tick - late
            other = axes(index)[1]
            for far in range(1, sizes[other]):
                hop_two(index, far).wait_recv()
            add_rows(
                rows,
                done.at[index],
                part.at[index, at[other]],
                *[far_in.at[index, far - 1] for far in range(1, sizes[other])],
            )
            if index < len(order) - 1:
                last(index).start()
            else:
                own.start()
    for index in range(len(order)):
        name, other = axes(index)
        for step in range(1, sizes[name]):
            hop_one(index, step).wait_send()
        for far in range(1, sizes[other]):
            hop_two(index, far).wait_send()
        if index < len(order) - 1:
            last(index).wait_send()
            last_came(index).wait_recv()
    own.wait()


def collect_grads(sizes, collective_id, grads):
    columns = grads.shape[1]
    group = sizes["ctx"] * sizes["core"]
    rows = grads.shape[0] // (group * sizes["dp"] * sizes["x"])
    steps = max(sizes["dp"], sizes["x"])
    half = (group + 1) // 2
    return pl.pallas_call(
        functools.partial(collect_kernel, sizes),
        out_shape=jax.ShapeDtypeStruct((group, rows, columns), BF),
        in_specs=[pl.BlockSpec(memory_space=pltpu.VMEM)],
        out_specs=pl.BlockSpec(memory_space=pl.ANY),
        scratch_shapes=[
            pltpu.VMEM((half, max(1, sizes["dp"] - 1), sizes["x"], rows, columns), BF),
            pltpu.VMEM((half, max(1, sizes["x"] - 1), sizes["dp"], rows, columns), BF),
            pltpu.VMEM((group, steps, rows, columns), BF),
            pltpu.VMEM((group, max(1, steps - 1), rows, columns), BF),
            pltpu.VMEM((group, rows, columns), BF),
            pltpu.SemaphoreType.DMA,
            pltpu.SemaphoreType.DMA((group, steps)),
            pltpu.SemaphoreType.DMA((group, steps)),
            pltpu.SemaphoreType.DMA((group, steps)),
            pltpu.SemaphoreType.DMA((group, steps)),
            pltpu.SemaphoreType.DMA((group,)),
            pltpu.SemaphoreType.DMA((group,)),
        ],
        compiler_params=pltpu.CompilerParams(
            collective_id=collective_id, has_side_effects=True, vmem_limit_bytes=58 * 2**20
        ),
    )(grads.reshape(sizes["dp"], sizes["ctx"], sizes["x"], sizes["core"], rows, columns))


def turned(values):
    half_dim = values.shape[-1] // 2
    return jnp.concatenate([-values[..., half_dim:], values[..., :half_dim]], -1)


def turned_back(values):
    half_dim = values.shape[-1] // 2
    return jnp.concatenate([values[..., half_dim:], -values[..., :half_dim]], -1)


def norm_back(grad_entry, normed, inverse, gain):
    grad_gain = jnp.sum(grad_entry * normed, 0)
    grad_normed = grad_entry * gain
    grad_rows = inverse * (grad_normed - normed * jnp.mean(grad_normed * normed, -1, keepdims=True))
    return (grad_rows, grad_gain)


def dot(left, right):
    return jnp.dot(left, right, preferred_element_type=F32)


def split_columns(array, group, sections):
    rows = array.shape[0]
    pieces, start = [], 0
    for width in sections:
        piece = array[:, start : start + width].reshape(rows, group, width // group)
        pieces.append(piece.transpose(1, 0, 2))
        start += width
    return jnp.concatenate(pieces, 2)


def shards(
    sizes,
    hidden,
    cotangent,
    span_order,
    norm_gains,
    w_qkv,
    w_out,
    w_gate_up,
    w_down,
    mom_gains,
    mom_qkv,
    mom_out,
    mom_gate_up,
    mom_down,
):
    everyone = ("dp", "ctx", "x", "core")
    line, pair = sizes["ctx"], sizes["core"]
    group = line * pair
    block_rows, width = hidden.shape[1:]
    total_rows = block_rows * line
    span_rows = total_rows // span_order.shape[0]
    heads, kv_heads = H // group, KV // group
    ratio = heads // kv_heads
    query_cols, kv_cols, unit_cols = heads * HD, kv_heads * HD, FF // group
    scale = HD ** (-0.5)
    key_pos = (
        span_order[:, None] * span_rows + jnp.arange(span_rows, dtype=jnp.int32)[None, :]
    ).reshape(-1)
    visible = key_pos[None, :] <= key_pos[:, None]
    cos_tab, sin_tab = rope_table(key_pos)
    cos_tab, sin_tab = cos_tab[None, :, None, :], sin_tab[None, :, None, :]

    packed = jnp.concatenate(
        [
            split_columns(w_qkv.astype(BF), group, (H * HD, KV * HD, KV * HD)),
            split_columns(w_out.astype(BF), group, (H * HD,)),
            split_columns(w_gate_up.astype(BF), group, (FF, FF)),
            split_columns(w_down.astype(BF), group, (FF,)),
        ],
        2,
    )
    qkv_width = query_cols + 2 * kv_cols
    ends = [qkv_width, qkv_width + query_cols, qkv_width + query_cols + 2 * unit_cols]
    gains_c = lax.all_gather(norm_gains.astype(BF), everyone, axis=1, tiled=True)
    weights = spread_weights(sizes, 0, packed)
    qkv_c = weights[:, : ends[0]]
    out_c = weights[:, ends[0] : ends[1]]
    gate_up_c = weights[:, ends[1] : ends[2]]
    down_c = weights[:, ends[2] :]

    gain_one = gains_c[0].astype(F32)
    gain_two = gains_c[1].astype(F32)
    row_in = hidden[0].astype(F32)
    inv_one = lax.rsqrt(jnp.mean(row_in * row_in, -1, keepdims=True) + EPS_NORM)
    normed_one = row_in * inv_one
    entry_one, cot = gather_tokens(
        sizes, 1, (normed_one * gain_one).astype(BF), cotangent[0]
    )

    projected = dot(entry_one, qkv_c).reshape(pair, total_rows, qkv_width)
    queries = projected[..., :query_cols].reshape(pair, total_rows, heads, HD)
    key_rows = projected[..., query_cols : query_cols + kv_cols].reshape(
        pair, total_rows, kv_heads, HD
    )
    value_rows = projected[..., query_cols + kv_cols :].reshape(pair, total_rows, kv_heads, HD)
    queries = (queries * cos_tab + turned(queries) * sin_tab).astype(BF)
    key_rows = (key_rows * cos_tab + turned(key_rows) * sin_tab).astype(BF)
    value_rows = value_rows.astype(BF)
    queries = queries.reshape(pair, total_rows, kv_heads, ratio, HD)

    def product(spec, left, right):
        return jnp.einsum(spec, left, right, preferred_element_type=F32)

    scores = product("stkgd,sukd->skgtu", queries, key_rows) * scale
    scores = jnp.where(visible, scores, NEG_FILL)
    top_score = jnp.max(scores, -1, keepdims=True)
    exponent = jnp.exp(scores - top_score)
    probability = exponent / jnp.sum(exponent, -1, keepdims=True)
    prob_low = probability.astype(BF)
    attended = product("skgtu,sukd->stkgd", prob_low, value_rows).astype(BF)
    attended = attended.reshape(pair * total_rows, query_cols)

    middle = row_in + scatter_tokens(sizes, 2, contract_cols(attended, out_c).astype(BF))
    inv_two = lax.rsqrt(jnp.mean(middle * middle, -1, keepdims=True) + EPS_NORM)
    normed_two = middle * inv_two
    (entry_two,) = gather_tokens(sizes, 3, (normed_two * gain_two).astype(BF))

    gate_up = dot(entry_two, gate_up_c)
    gate_part = gate_up[:, :unit_cols]
    up_part = gate_up[:, unit_cols:]
    sigmoid_gate = jax.nn.sigmoid(gate_part)
    silu_gate = gate_part * sigmoid_gate
    activated = (silu_gate * up_part).astype(BF)
    summed = scatter_tokens(sizes, 4, contract_cols(activated, down_c).astype(BF))
    output = (middle + summed).astype(BF)[None]
    grad_act = dot(cot, down_c)
    grad_gate = grad_act * up_part * sigmoid_gate * (1.0 + gate_part * (1.0 - sigmoid_gate))
    grad_up = grad_act * silu_gate
    grad_gu = jnp.concatenate([grad_gate, grad_up], 1).astype(BF)
    grad_entry_two = scatter_tokens(sizes, 5, contract_cols(grad_gu, gate_up_c).astype(BF))
    grad_top = cotangent[0].astype(F32)
    grad_mid_norm, grad_gain_two = norm_back(grad_entry_two, normed_two, inv_two, gain_two)
    grad_middle = grad_top + grad_mid_norm
    (grad_branch,) = gather_tokens(sizes, 6, grad_middle.astype(BF))

    grad_attended = dot(grad_branch, out_c).astype(BF)
    grad_heads = grad_attended.reshape(pair, total_rows, kv_heads, ratio, HD)
    grad_prob = product("stkgd,sukd->skgtu", grad_heads, value_rows)
    delta_row = jnp.sum(probability * grad_prob, -1, keepdims=True)
    grad_scores = jnp.where(visible, probability * (grad_prob - delta_row), 0.0).astype(BF)
    grad_queries = product("skgtu,sukd->stkgd", grad_scores, key_rows) * scale
    grad_keys = product("skgtu,stkgd->sukd", grad_scores, queries) * scale
    grad_values = product("skgtu,stkgd->sukd", prob_low, grad_heads)
    grad_queries = grad_queries.reshape(pair, total_rows, heads, HD)
    grad_queries = grad_queries * cos_tab + turned_back(grad_queries * sin_tab)
    grad_keys = grad_keys * cos_tab + turned_back(grad_keys * sin_tab)
    grad_projected = jnp.concatenate(
        [
            grad_queries.reshape(-1, query_cols),
            grad_keys.reshape(-1, kv_cols),
            grad_values.reshape(-1, kv_cols),
        ],
        1,
    ).astype(BF)
    grad_entry_one = scatter_tokens(sizes, 7, contract_cols(grad_projected, qkv_c).astype(BF))
    grad_row_norm, grad_gain_one = norm_back(grad_entry_one, normed_one, inv_one, gain_one)
    grad_hidden = (grad_middle + grad_row_norm).astype(BF)[None]

    terms = jnp.concatenate(
        [
            contract_rows(entry_one, grad_projected).astype(BF),
            contract_rows(grad_branch, attended).astype(BF),
            contract_rows(entry_two, grad_gu).astype(BF),
            contract_rows(cot, activated).astype(BF),
        ],
        1,
    )
    grads = collect_grads(sizes, 8, terms).astype(F32)
    grad_gains = lax.psum_scatter(
        jnp.stack([grad_gain_one, grad_gain_two]), everyone, scatter_dimension=1, tiled=True
    )

    def joined(*bounds):
        return jnp.concatenate(
            [
                grads[:, :, low:high].transpose(1, 0, 2).reshape(grads.shape[1], -1)
                for low, high in zip(bounds[:-1], bounds[1:])
            ],
            1,
        )

    grad_qkv = joined(0, query_cols, query_cols + kv_cols, ends[0])
    grad_out = joined(ends[0], ends[1])
    grad_gate_up = joined(ends[1], ends[1] + unit_cols, ends[2])
    grad_down = joined(ends[2], ends[2] + unit_cols)
    new_gains, new_mom_gains = adamw(norm_gains, grad_gains, mom_gains, LR_GAIN, 0.0)
    new_qkv, new_mom_qkv = adamw(w_qkv, grad_qkv, mom_qkv, LR_MATRIX, DECAY_MATRIX)
    new_out, new_mom_out = adamw(w_out, grad_out, mom_out, LR_OUTPUT, DECAY_MATRIX)
    new_gate_up, new_mom_gate_up = adamw(
        w_gate_up, grad_gate_up, mom_gate_up, LR_MATRIX, DECAY_MATRIX
    )
    new_down, new_mom_down = adamw(w_down, grad_down, mom_down, LR_MATRIX, DECAY_MATRIX)
    return (
        output,
        grad_hidden,
        grad_gains,
        grad_qkv,
        grad_out,
        grad_gate_up,
        grad_down,
        new_gains,
        new_qkv,
        new_out,
        new_gate_up,
        new_down,
        new_mom_gains,
        new_mom_qkv,
        new_mom_out,
        new_mom_gate_up,
        new_mom_down,
    )


def solution(mesh):
    shape = dict(mesh.shape)
    pair = 2 if shape["ctx"] * 2 <= KV and shape["fsdp"] % 2 == 0 else 1
    sizes = {"dp": shape["dp"], "ctx": shape["ctx"], "x": shape["fsdp"] // pair, "core": pair}
    finer = Mesh(mesh.devices.reshape(tuple(sizes.values())), tuple(sizes))
    tokens = P(("dp", "x", "core"), "ctx", None)
    everyone = ("dp", "ctx", "x", "core")
    rows, gains = P(everyone, None), P(None, everyone)
    row_moments, gain_moments = P(None, everyone, None), P(None, None, everyone)
    weights = (gains, rows, rows, rows, rows)
    moments = (gain_moments, row_moments, row_moments, row_moments, row_moments)
    return jax.shard_map(
        functools.partial(shards, sizes),
        mesh=finer,
        in_specs=(tokens, tokens, P()) + weights + moments,
        out_specs=(tokens, tokens) + weights + weights + moments,
        check_vma=False,
    )
```

```python
import functools
import math

import jax
import jax.numpy as jnp
from jax import lax
from jax.experimental import pallas as pl
from jax.experimental.pallas import tpu as pltpu
from jax.sharding import Mesh
from jax.sharding import PartitionSpec as P

MESH = pl.DeviceIdType.MESH
BF = jnp.bfloat16
F32 = jnp.float32
H = 32
KV = 8
HD = 64
FF = 8192


EPS_NORM = 1e-05
NEG_FILL = -1000000000.0
THETA = 500000.0
BETA_ONE = 0.9
BETA_TWO = 0.95
ADAM_EPS = 1e-08
DECAY_MATRIX = 0.1
LR_MATRIX = 0.01
LR_OUTPUT = 0.06
LR_GAIN = 0.3


def rope_table(positions):
    half_dim = HD // 2
    index_row = jnp.arange(half_dim, dtype=jnp.float32)
    frequency = jnp.exp(-(2.0 * index_row / HD) * math.log(THETA))
    wavelen = 2.0 * math.pi / frequency
    smooth = (8192.0 / wavelen - 1.0) / 3.0
    scaled = jnp.where(
        wavelen < 2048.0,
        frequency,
        jnp.where(
            wavelen > 8192.0,
            frequency / 32.0,
            (1.0 - smooth) * frequency / 32.0 + smooth * frequency,
        ),
    )
    angles = positions.astype(jnp.float32)[:, None] * scaled[None, :]
    cosine = jnp.cos(angles)
    sine_part = jnp.sin(angles)
    return (jnp.concatenate([cosine, cosine], 1), jnp.concatenate([sine_part, sine_part], 1))


def adamw(weight, gradient, states, step_rate, decay_rate):
    first_mom = BETA_ONE * states[0] + (1.0 - BETA_ONE) * gradient
    root_mom = jnp.sqrt(BETA_TWO * states[1] * states[1] + (1.0 - BETA_TWO) * gradient * gradient)
    first_hat = first_mom / (1.0 - BETA_ONE**3)
    root_hat = root_mom / math.sqrt(1.0 - BETA_TWO**3)
    updated = weight - step_rate * (first_hat / (root_hat + ADAM_EPS) + decay_rate * weight)
    return (updated, jnp.stack([first_mom, root_mom]))


def contract_rows(left_arr, right_arr):
    return lax.dot_general(
        left_arr, right_arr, (((0,), (0,)), ((), ())), preferred_element_type=jnp.float32
    )


def contract_cols(left_arr, right_arr):
    return lax.dot_general(
        left_arr, right_arr, (((1,), (1,)), ((), ())), preferred_element_type=jnp.float32
    )


def wrap(value, size):
    return lax.rem(value + size, size)


def remote(src, dst, send_sem, recv_sem, **where):
    return pltpu.make_async_remote_copy(
        src_ref=src,
        dst_ref=dst,
        send_sem=send_sem,
        recv_sem=recv_sem,
        device_id=where,
        device_id_type=MESH,
    )


def greet(places):
    barrier = pltpu.get_barrier_semaphore()
    for where in places:
        pl.semaphore_signal(barrier, inc=1, device_id=where, device_id_type=MESH)
    pl.semaphore_wait(barrier, len(places))


def greet_line(line, pair):
    barrier = pltpu.get_barrier_semaphore()
    here = lax.axis_index("ctx")

    @pl.when(here > 0)
    def _():
        pl.semaphore_signal(barrier, inc=1, device_id={"ctx": here - 1}, device_id_type=MESH)

    @pl.when(here < line - 1)
    def _():
        pl.semaphore_signal(barrier, inc=1, device_id={"ctx": here + 1}, device_id_type=MESH)

    if pair > 1:
        pl.semaphore_signal(
            barrier, inc=1, device_id={"core": 1 - lax.axis_index("core")}, device_id_type=MESH
        )
    ends = (here == 0).astype(jnp.int32) + (here == line - 1).astype(jnp.int32)
    pl.semaphore_wait(barrier, 2 - ends + (1 if pair > 1 else 0))


class Travel:
    @staticmethod
    def sems(many, line):
        return [pltpu.SemaphoreType.DMA((many,))] + [pltpu.SemaphoreType.DMA((many, 2, line))] * 4

    def __init__(self, line, pair, ins, outs, own_sem, line_send, line_recv, core_send, core_recv):
        self.line, self.pair, self.ins, self.outs = line, pair, ins, outs
        self.own_sem, self.line_sems, self.core_sems = own_sem, (line_send, line_recv), (core_send, core_recv)
        self.here = lax.axis_index("ctx")
        self.core = lax.axis_index("core")

    def block(self, way, step):
        return self.here - 1 - step if way == 0 else self.here + 1 + step

    def copy(self, sems, at, source, place, **where):
        return remote(place if source is None else source, place, sems[0].at[at], sems[1].at[at], **where)

    def hop(self, item, way, step, source=None):
        place = self.outs[item].at[self.core, self.block(way, step - 1)]
        target = self.here + 1 if way == 0 else self.here - 1
        return self.copy(self.line_sems, (item, way, step), source, place, ctx=target)

    def arrived(self, item, way, step):
        place = self.outs[item].at[self.core, self.block(way, step)]
        return self.copy(self.line_sems, (item, way, step), None, place, ctx=self.here)

    def share(self, item, way, step, source=None):
        place = self.outs[item].at[self.core, self.block(way, step)]
        return self.copy(self.core_sems, (item, way, step + 1), source, place, core=1 - self.core)

    def shared(self, item, way, step):
        place = self.outs[item].at[1 - self.core, self.block(way, step)]
        return self.copy(self.core_sems, (item, way, step + 1), None, place, core=1 - self.core)

    def own(self, item):
        place = self.outs[item].at[self.core, self.here]
        return pltpu.make_async_copy(self.ins[item], place, self.own_sem.at[item])

    def sends(self, way):
        return self.here < self.line - 1 if way == 0 else self.here > 0

    def has(self, way, step):
        return self.block(way, step) >= 0 if way == 0 else self.block(way, step) <= self.line - 1

    def begin(self):
        for item in range(len(self.ins)):
            for way in range(2):

                @pl.when(self.sends(way))
                def _(item=item, way=way):
                    self.hop(item, way, 0, self.ins[item]).start()

            if self.pair > 1:
                self.share(item, 0, -1, self.ins[item]).start()
            self.own(item).start()

    def step(self, step):
        for item in range(len(self.ins)):
            for way in range(2):

                @pl.when(self.has(way, step))
                def _(item=item, way=way):
                    self.arrived(item, way, step).wait_recv()
                    if step + 1 < self.line - 1:

                        @pl.when(self.sends(way))
                        def _():
                            self.hop(item, way, step + 1).start()

                    if self.pair > 1:
                        self.share(item, way, step).start()

    def end(self):
        for item in range(len(self.ins)):
            self.own(item).wait()
            if self.pair > 1:
                self.share(item, 0, -1, self.ins[item]).wait_send()
                self.shared(item, 0, -1).wait_recv()
            for way in range(2):

                @pl.when(self.sends(way))
                def _(item=item, way=way):
                    self.hop(item, way, 0, self.ins[item]).wait_send()

                for step in range(self.line - 1):

                    @pl.when(self.has(way, step))
                    def _(item=item, way=way, step=step):
                        if step + 1 < self.line - 1:

                            @pl.when(self.sends(way))
                            def _():
                                self.hop(item, way, step + 1).wait_send()

                        if self.pair > 1:
                            self.share(item, way, step).wait_send()
                            self.shared(item, way, step).wait_recv()


def gather_kernel(line, pair, many, *refs):
    greet_line(line, pair)
    travel = Travel(line, pair, refs[:many], refs[many : 2 * many], *refs[2 * many :])
    travel.begin()
    for step in range(line - 1):
        travel.step(step)
    travel.end()


def gather_tokens(sizes, collective_id, *arrays):
    line, pair = sizes["ctx"], sizes["core"]
    many = len(arrays)
    any_spec = pl.BlockSpec(memory_space=pl.ANY)
    outs = pl.pallas_call(
        functools.partial(gather_kernel, line, pair, many),
        out_shape=[jax.ShapeDtypeStruct((pair, line) + a.shape, a.dtype) for a in arrays],
        in_specs=[any_spec] * many,
        out_specs=[any_spec] * many,
        scratch_shapes=Travel.sems(many, line),
        compiler_params=pltpu.CompilerParams(collective_id=collective_id, has_side_effects=True),
    )(*arrays)
    return [o.reshape((-1,) + a.shape[1:]) for o, a in zip(outs, arrays)]


def add_rows(rows, out_ref, *parts):
    def one(index, carry):
        at = pl.ds(pl.multiple_of(index * 16, 16), 16)
        total = parts[0][at, :].astype(F32)
        for part in parts[1:]:
            total = total + part[at, :].astype(F32)
        out_ref[at, :] = total.astype(out_ref.dtype)
        return carry

    lax.fori_loop(0, rows // 16, one, 0)


def scatter_kernel(line, pair, part_ref, out_ref, near, mine, going, landed, core_send, core_recv, line_send, line_recv):
    rows = out_ref.shape[0]
    here = lax.axis_index("ctx")
    core = lax.axis_index("core")
    greet_line(line, pair)

    def to_core(block):
        return remote(
            part_ref.at[1 - core, block],
            near.at[block],
            core_send.at[block],
            core_recv.at[block],
            core=1 - core,
        )

    def onward(way, block):
        return remote(
            going.at[way, block],
            landed.at[way, block],
            line_send.at[way, block],
            line_recv.at[way, block],
            ctx=here + 1 if way == 0 else here - 1,
        )

    order = []
    for step in range(line):
        order += [line - 1 - step, step]
    order = list(dict.fromkeys(order))
    if pair > 1:
        for block in order:
            to_core(block).start()
    ready = set()
    for step in range(line):
        for way, block in ((0, line - 1 - step), (1, step)):
            if block not in ready:
                ready.add(block)
                if pair > 1:
                    to_core(block).wait_recv()
            goes = here < block if way == 0 else here > block
            first = here == 0 if way == 0 else here == line - 1

            @pl.when(goes & first)
            def _(way=way, block=block):
                terms = [part_ref.at[core, block]] + ([near.at[block]] if pair > 1 else [])
                add_rows(rows, going.at[way, block], *terms)
                onward(way, block).start()

            @pl.when(goes & jnp.logical_not(first))
            def _(way=way, block=block):
                onward(way, block).wait_recv()
                terms = [part_ref.at[core, block]] + ([near.at[block]] if pair > 1 else [])
                add_rows(rows, going.at[way, block], *terms, landed.at[way, block])
                onward(way, block).start()

    for block in range(line):

        @pl.when(here == block)
        def _(block=block):
            terms = [part_ref.at[core, block]] + ([near.at[block]] if pair > 1 else [])
            if block > 0:
                onward(0, block).wait_recv()
                terms.append(landed.at[0, block])
            if block < line - 1:
                onward(1, block).wait_recv()
                terms.append(landed.at[1, block])
            add_rows(rows, out_ref, *terms)

    for block in range(line):
        if pair > 1:
            to_core(block).wait_send()
        for way in range(2):
            goes = here < block if way == 0 else here > block

            @pl.when(goes)
            def _(way=way, block=block):
                onward(way, block).wait_send()


def scatter_tokens(sizes, collective_id, terms):
    line, pair = sizes["ctx"], sizes["core"]
    columns = terms.shape[1]
    rows = terms.shape[0] // (line * pair)
    vmem = pl.BlockSpec(memory_space=pltpu.VMEM)
    return pl.pallas_call(
        functools.partial(scatter_kernel, line, pair),
        out_shape=jax.ShapeDtypeStruct((rows, columns), F32),
        in_specs=[vmem],
        out_specs=vmem,
        scratch_shapes=[
            pltpu.VMEM((line, rows, columns), BF),
            pltpu.VMEM((8, 128), F32),
            pltpu.VMEM((2, line, rows, columns), BF),
            pltpu.VMEM((2, line, rows, columns), BF),
            pltpu.SemaphoreType.DMA((line,)),
            pltpu.SemaphoreType.DMA((line,)),
            pltpu.SemaphoreType.DMA((2, line)),
            pltpu.SemaphoreType.DMA((2, line)),
        ],
        compiler_params=pltpu.CompilerParams(
            collective_id=collective_id, has_side_effects=True, vmem_limit_bytes=50 * 2**20
        ),
    )(terms.reshape(pair, line, rows, columns))


def blocks_in_order(line, pair):
    away = sorted(range(line), key=lambda d: min(d, line - d))
    return [(dz, dc) for dz in away for dc in range(pair)]


def greet_all(sizes):
    names = ("dp", "ctx", "x", "core")
    at = {name: lax.axis_index(name) for name in names}
    places = []
    for dz, dc in blocks_in_order(sizes["ctx"], sizes["core"]):
        if dz or dc:
            places.append(
                {"ctx": wrap(at["ctx"] + dz, sizes["ctx"]), "core": wrap(at["core"] + dc, sizes["core"])}
            )
    for name in ("dp", "x"):
        for step in range(1, sizes[name]):
            places.append({name: wrap(at[name] + step, sizes[name])})
    greet(places)


def pack_member(refs, member, rows, group, tall, wide):
    qkv_ref, out_ref, gate_up_ref, down_ref, gain_ref = refs
    heads, keys, units = H * HD // group, KV * HD // group, FF // group
    low = lambda values: values.astype(BF)
    tall[member, :, :heads] = low(qkv_ref[:, member * heads : (member + 1) * heads])
    key_at, value_at = H * HD + member * keys, (H + KV) * HD + member * keys
    tall[member, :, heads : heads + 2 * keys] = low(
        jnp.concatenate(
            [qkv_ref[:, key_at : key_at + keys], qkv_ref[:, value_at : value_at + keys]], 1
        )
    )
    tall[member, :, heads + 2 * keys : 2 * heads + 2 * keys] = low(
        out_ref[:, member * heads : (member + 1) * heads]
    )
    tall[member, :, 2 * heads + 2 * keys :] = low(gain_ref[...])
    wide[member, :, :units] = low(gate_up_ref[:, member * units : (member + 1) * units])
    wide[member, :, units : 2 * units] = low(
        gate_up_ref[:, FF + member * units : FF + (member + 1) * units]
    )
    wide[member, :, 2 * units :] = low(down_ref[:, member * units : (member + 1) * units])


def spread_kernel(sizes, *refs):
    weight_refs, hidden_ref = refs[:5], refs[5]
    outs, hidden_out = refs[6:8], refs[8]
    packs = refs[9:11]
    own_sem, f_send, f_recv, a_send, a_recv, b_send, b_recv = refs[11:18]
    travel_sems = refs[18:]
    line, pair = sizes["ctx"], sizes["core"]
    group = line * pair
    rows = packs[0].shape[1]
    at = {name: lax.axis_index(name) for name in ("dp", "ctx", "x", "core")}
    greet_all(sizes)
    order = blocks_in_order(line, pair)
    me = at["ctx"] * pair + at["core"]
    travel = Travel(line, pair, [hidden_ref], [hidden_out], *travel_sems)
    travel.begin()

    def first(kind, index):
        dz, dc = order[index]
        z, c = wrap(at["ctx"] + dz, line), wrap(at["core"] + dc, pair)
        return remote(
            packs[kind].at[z * pair + c],
            outs[kind].at[at["dp"], at["ctx"], at["x"], at["core"]],
            f_send.at[kind, index],
            f_recv.at[kind, index],
            ctx=z,
            core=c,
        )

    def place(kind, index, moved):
        dz, dc = order[index]
        z, c = wrap(at["ctx"] - dz, line), wrap(at["core"] - dc, pair)
        spot = {name: wrap(at[name] - moved.get(name, 0), sizes[name]) for name in ("dp", "x")}
        return outs[kind].at[spot["dp"], z, spot["x"], c]

    def came(kind, index):
        spot = place(kind, index, {})
        return remote(spot, spot, f_send.at[kind, index], f_recv.at[kind, index], core=at["core"])

    def axes(index):
        dz, dc = order[index]
        return ("x", "dp") if (dz + dc) % 2 == 0 else ("dp", "x")

    def hop_one(kind, index, step):
        name = axes(index)[0]
        spot = place(kind, index, {})
        return remote(
            spot,
            spot,
            a_send.at[kind, index, step],
            a_recv.at[kind, index, step],
            **{name: wrap(at[name] + step, sizes[name])},
        )

    def one_came(kind, index, step):
        name = axes(index)[0]
        spot = place(kind, index, {name: step})
        return remote(
            spot, spot, a_send.at[kind, index, step], a_recv.at[kind, index, step], core=at["core"]
        )

    def hop_two(kind, index, step, far):
        name, other = axes(index)
        spot = place(kind, index, {name: step})
        return remote(
            spot,
            spot,
            b_send.at[kind, index, step, far],
            b_recv.at[kind, index, step, far],
            **{other: wrap(at[other] + far, sizes[other])},
        )

    def two_came(kind, index, step, far):
        name, other = axes(index)
        spot = place(kind, index, {name: step, other: far})
        return remote(
            spot,
            spot,
            b_send.at[kind, index, step, far],
            b_recv.at[kind, index, step, far],
            core=at["core"],
        )

    def own(kind):
        return pltpu.make_async_copy(
            packs[kind].at[me],
            outs[kind].at[at["dp"], at["ctx"], at["x"], at["core"]],
            own_sem.at[kind],
        )

    def onward(kind, index):
        name, other = axes(index)
        for step in range(1, sizes[name]):
            hop_one(kind, index, step).start()
        for far in range(1, sizes[other]):
            hop_two(kind, index, 0, far).start()

    def onward_two(kind, index):
        name, other = axes(index)
        for step in range(1, sizes[name]):
            one_came(kind, index, step).wait_recv()
            for far in range(1, sizes[other]):
                hop_two(kind, index, step, far).start()

    for member in range(group):
        pack_member(weight_refs, member, rows, group, *packs)
    ahead, late = 3, 1
    for kind in range(2):
        own(kind).start()
        for index in range(1, 1 + ahead):
            first(kind, index).start()
    for tick in range(group + late):
        if tick < group:
            for kind in range(2):
                if tick == 0:
                    own(kind).wait()
                else:
                    came(kind, tick).wait_recv()
                onward(kind, tick)
                if 1 + ahead <= tick + ahead < group and tick:
                    first(kind, tick + ahead).start()
        if tick % 2 == 1 and tick // 2 < line - 1:
            travel.step(tick // 2)
        if tick >= late:
            for kind in range(2):
                onward_two(kind, tick - late)
    travel.end()
    for kind in range(2):
        for index in range(group):
            if index:
                first(kind, index).wait_send()
            name, other = axes(index)
            for step in range(sizes[name]):
                if step:
                    hop_one(kind, index, step).wait_send()
                for far in range(1, sizes[other]):
                    hop_two(kind, index, step, far).wait_send()
                    two_came(kind, index, step, far).wait_recv()


def spread_weights(sizes, collective_id, hidden, gains, *weights):
    line, pair = sizes["ctx"], sizes["core"]
    group = line * pair
    rows = weights[0].shape[0]
    steps = max(sizes["dp"], sizes["x"])
    tall, wide = (2 * H * HD + 2 * KV * HD) // group + 128, 3 * FF // group
    gain_tile = jnp.pad(gains.T, ((0, 0), (0, 126)))
    any_spec = pl.BlockSpec(memory_space=pl.ANY)
    vmem = pl.BlockSpec(memory_space=pltpu.VMEM)
    everyone = (sizes["dp"], line, sizes["x"], pair, rows)
    low, high, tokens = pl.pallas_call(
        functools.partial(spread_kernel, sizes),
        out_shape=[
            jax.ShapeDtypeStruct(everyone + (tall,), BF),
            jax.ShapeDtypeStruct(everyone + (wide,), BF),
            jax.ShapeDtypeStruct((pair, line) + hidden.shape, BF),
        ],
        in_specs=[vmem] * 5 + [any_spec],
        out_specs=[any_spec] * 3,
        scratch_shapes=[
            pltpu.VMEM((group, rows, tall), BF),
            pltpu.VMEM((group, rows, wide), BF),
            pltpu.SemaphoreType.DMA((2,)),
            pltpu.SemaphoreType.DMA((2, group)),
            pltpu.SemaphoreType.DMA((2, group)),
            pltpu.SemaphoreType.DMA((2, group, steps)),
            pltpu.SemaphoreType.DMA((2, group, steps)),
            pltpu.SemaphoreType.DMA((2, group, steps, steps)),
            pltpu.SemaphoreType.DMA((2, group, steps, steps)),
            *Travel.sems(1, line),
        ],
        compiler_params=pltpu.CompilerParams(
            collective_id=collective_id, has_side_effects=True, vmem_limit_bytes=40 * 2**20
        ),
    )(*weights, gain_tile, hidden)
    return low.reshape(-1, tall), high.reshape(-1, wide), tokens.reshape(-1, hidden.shape[1])


def collect_kernel(sizes, widths, *refs):
    many = len(widths)
    pieces = grad_pieces(sizes)
    lefts, rights = refs[: 2 * many : 2], refs[1 : 2 * many : 2]
    refs = refs[2 * many :]
    outs, refs = refs[: len(pieces)], refs[len(pieces) :]
    held, refs = refs[: 2 * many], refs[2 * many :]
    terms, near, far_in = refs[:3]
    load_sem, own_sem, a_send, a_recv, b_send, b_recv, f_send, f_recv = refs[3:]
    line, pair = sizes["ctx"], sizes["core"]
    rows = terms.shape[-2]
    across = sizes["x"] * pair * rows
    at = {name: lax.axis_index(name) for name in ("dp", "ctx", "x", "core")}
    me = at["ctx"] * pair + at["core"]
    loads = [
        pltpu.make_async_copy(source, target, load_sem.at[i])
        for i, (source, target) in enumerate(zip((r for two in zip(lefts, rights) for r in two), held))
    ]
    for load in loads:
        load.start()
    greet_all(sizes)
    away = sorted(range(line), key=lambda d: -min(d, line - d))
    order = [(dz, dc) for dz in away for dc in range(pair)]

    def spot_of(index):
        dz, dc = order[index]
        return wrap(at["ctx"] + dz, line), wrap(at["core"] + dc, pair)

    def axes(index):
        dz, dc = order[index]
        return ("dp", "x") if (dz + dc) % 2 == 0 else ("x", "dp")

    def multiply(tick):
        z = wrap(at["ctx"] + away[tick], line)
        start = 0
        for item, width in enumerate(widths):
            left, right = held[2 * item], held[2 * item + 1]
            step = math.gcd(width, 512)

            @pl.loop(0, sizes["dp"])
            def _(dp, left=left, right=right, start=start, width=width, step=step):
                lanes = pl.ds(pl.multiple_of((dp * line + z) * across, 128), across)
                left_t = left[:, lanes].T

                @pl.loop(0, width // step)
                def _(part):
                    columns = pl.ds(pl.multiple_of(part * step, 128), step)
                    into = pl.ds(pl.multiple_of(start + part * step, 128), step)
                    product = dot(left_t, right[:, columns]).astype(BF)
                    for x in range(sizes["x"]):
                        for core in range(pair):
                            low = (x * pair + core) * rows
                            terms[tick, dp, x, core, :, into] = product[low : low + rows]

            start += width

    def block_terms(index, first_at, other_at):
        spot = {axes(index)[0]: first_at, axes(index)[1]: other_at}
        return terms.at[index // pair, spot["dp"], spot["x"], spot_of(index)[1]]

    def hop_one(index, step, place):
        name = axes(index)[0]
        to = wrap(at[name] + step, sizes[name])
        return remote(
            block_terms(index, to, place),
            near.at[index, (step - 1) * sizes[axes(index)[1]] + place],
            a_send.at[index, step, place],
            a_recv.at[index, step, place],
            **{name: to},
        )

    def hop_two(index, far):
        name, other = axes(index)
        to = wrap(at[other] + far, sizes[other])
        return remote(
            block_terms(index, at[name], to),
            far_in.at[index, far - 1],
            b_send.at[index, far],
            b_recv.at[index, far],
            **{other: to},
        )

    def done(index):
        name, other = axes(index)
        return block_terms(index, at[name], at[other])

    def piece_at(piece, member):
        _, width, offset = pieces[piece]
        return outs[piece].at[:, pl.ds(pl.multiple_of(member * width, 128), width)]

    def last(index, piece):
        z, c = spot_of(index)
        _, width, offset = pieces[piece]
        source = done(index).at[:, pl.ds(offset, width)]
        target = piece_at(piece, me)
        if index == len(order) - pair:
            return pltpu.make_async_copy(source, target, own_sem.at[piece])
        return remote(
            source, target, f_send.at[index, piece], f_recv.at[index, piece], ctx=z, core=c
        )

    def last_came(index, piece):
        dz, dc = order[index]
        z, c = wrap(at["ctx"] - dz, line), wrap(at["core"] - dc, pair)
        spot = piece_at(piece, z * pair + c)
        return remote(
            spot, spot, f_send.at[index, piece], f_recv.at[index, piece], core=at["core"]
        )

    def sum_one(index):
        name, other = axes(index)
        for far in list(range(1, sizes[other])) + [0]:
            place = wrap(at[other] + far, sizes[other])
            for step in range(1, sizes[name]):
                hop_one(index, step, place).wait_recv()
            kept = block_terms(index, at[name], place)
            add_rows(rows, kept, kept, *[near.at[index, (step - 1) * sizes[other] + place] for step in range(1, sizes[name])])
            if far:
                hop_two(index, far).start()

    def sum_two(index):
        other = axes(index)[1]
        for far in range(1, sizes[other]):
            hop_two(index, far).wait_recv()
        add_rows(
            rows, done(index), done(index), *[far_in.at[index, far - 1] for far in range(1, sizes[other])]
        )
        for piece in range(len(pieces)):
            last(index, piece).start()

    late, later = 1, 2
    for tick in range(line + later):
        if tick < line:
            if tick == 0:
                for load in loads:
                    load.wait()
            multiply(tick)
            for index in range(tick * pair, (tick + 1) * pair):
                name, other = axes(index)
                for far in list(range(1, sizes[other])) + [0]:
                    for step in range(1, sizes[name]):
                        hop_one(index, step, wrap(at[other] + far, sizes[other])).start()
        if late <= tick < line + late:
            for index in range((tick - late) * pair, (tick - late + 1) * pair):
                sum_one(index)
        if tick >= later:
            for index in range((tick - later) * pair, (tick - later + 1) * pair):
                sum_two(index)
    for index in range(len(order)):
        name, other = axes(index)
        for step in range(1, sizes[name]):
            for place in range(sizes[other]):
                hop_one(index, step, place).wait_send()
        for far in range(1, sizes[other]):
            hop_two(index, far).wait_send()
        for piece in range(len(pieces)):
            if index == len(order) - pair:
                last(index, piece).wait()
            else:
                last(index, piece).wait_send()
                last_came(index, piece).wait_recv()


def grad_pieces(sizes):
    group = sizes["ctx"] * sizes["core"]
    heads, keys, units = H * HD // group, KV * HD // group, FF // group
    pieces, offset = [], 0
    for name, width in (
        ("gate", units),
        ("up", units),
        ("down", units),
        ("query", heads),
        ("key_value", 2 * keys),
        ("out", heads),
    ):
        pieces.append((name, width, offset))
        offset += width
    return pieces


def collect_grads(sizes, collective_id, *factors):
    line, pair = sizes["ctx"], sizes["core"]
    group = line * pair
    rows = factors[0].shape[1] // (group * sizes["dp"] * sizes["x"])
    widths = [right.shape[1] for right in factors[1::2]]
    total = sum(widths)
    pieces = grad_pieces(sizes)
    steps = max(sizes["dp"], sizes["x"])
    any_spec = pl.BlockSpec(memory_space=pl.ANY)
    dma = pltpu.SemaphoreType.DMA
    return pl.pallas_call(
        functools.partial(collect_kernel, sizes, widths),
        out_shape=[jax.ShapeDtypeStruct((rows, group * width), BF) for _, width, _ in pieces],
        in_specs=[any_spec] * len(factors),
        out_specs=[any_spec] * len(pieces),
        scratch_shapes=[
            *[pltpu.VMEM(factor.shape, factor.dtype) for factor in factors],
            pltpu.VMEM((line, sizes["dp"], sizes["x"], pair, rows, total), BF),
            pltpu.VMEM((group, sizes["dp"] * sizes["x"] - min(sizes["dp"], sizes["x"]), rows, total), BF),
            pltpu.VMEM((group, steps - 1, rows, total), BF),
            dma((len(factors),)),
            dma((len(pieces),)),
            dma((group, steps, steps)),
            dma((group, steps, steps)),
            dma((group, steps)),
            dma((group, steps)),
            dma((group, len(pieces))),
            dma((group, len(pieces))),
        ],
        compiler_params=pltpu.CompilerParams(
            collective_id=collective_id, has_side_effects=True, vmem_limit_bytes=62 * 2**20
        ),
    )(*factors)


def adamw_kernel(step_rate, decay_rate, grad_ref, weight_ref, state_ref, grad_out, weight_out, state_out):
    gradient = grad_ref[...].astype(F32)
    grad_out[...] = gradient
    updated, states = adamw(weight_ref[...], gradient, state_ref[...], step_rate, decay_rate)
    weight_out[...] = updated
    state_out[...] = states


def adamw_columns(gradient, weight, states, step_rate, decay_rate):
    rows, columns = weight.shape
    step = math.gcd(columns, 1024)
    flat = pl.BlockSpec((rows, step), lambda i: (0, i))
    deep = pl.BlockSpec((2, rows, step), lambda i: (0, 0, i))
    return pl.pallas_call(
        functools.partial(adamw_kernel, step_rate, decay_rate),
        grid=(columns // step,),
        out_shape=[
            jax.ShapeDtypeStruct(weight.shape, F32),
            jax.ShapeDtypeStruct(weight.shape, F32),
            jax.ShapeDtypeStruct(states.shape, F32),
        ],
        in_specs=[flat, flat, deep],
        out_specs=[flat, flat, deep],
    )(gradient, weight, states)


def turned(values):
    half_dim = values.shape[-1] // 2
    return jnp.concatenate([-values[..., half_dim:], values[..., :half_dim]], -1)


def turned_back(values):
    half_dim = values.shape[-1] // 2
    return jnp.concatenate([values[..., half_dim:], -values[..., :half_dim]], -1)


def norm_back(grad_entry, normed, inverse, gain):
    grad_gain = jnp.sum(grad_entry * normed, 0)
    grad_normed = grad_entry * gain
    grad_rows = inverse * (grad_normed - normed * jnp.mean(grad_normed * normed, -1, keepdims=True))
    return (grad_rows, grad_gain)


def dot(left, right):
    return jnp.dot(left, right, preferred_element_type=F32)


def shards(
    sizes,
    hidden,
    cotangent,
    span_order,
    norm_gains,
    w_qkv,
    w_out,
    w_gate_up,
    w_down,
    mom_gains,
    mom_qkv,
    mom_out,
    mom_gate_up,
    mom_down,
):
    everyone = ("dp", "ctx", "x", "core")
    line, pair = sizes["ctx"], sizes["core"]
    group = line * pair
    block_rows, width = hidden.shape[1:]
    total_rows = block_rows * line
    span_rows = total_rows // span_order.shape[0]
    heads, kv_heads = H // group, KV // group
    ratio = heads // kv_heads
    query_cols, kv_cols, unit_cols = heads * HD, kv_heads * HD, FF // group
    scale = HD ** (-0.5)
    key_pos = (
        span_order[:, None] * span_rows + jnp.arange(span_rows, dtype=jnp.int32)[None, :]
    ).reshape(-1)
    visible = key_pos[None, :] <= key_pos[:, None]
    cos_tab, sin_tab = rope_table(key_pos)
    cos_tab, sin_tab = cos_tab[None, :, None, :], sin_tab[None, :, None, :]

    qkv_width = query_cols + 2 * kv_cols
    low, high, hidden_all = spread_weights(
        sizes, 0, hidden[0], norm_gains, w_qkv, w_out, w_gate_up, w_down
    )
    qkv_c = low[:, :qkv_width]
    out_c = low[:, qkv_width : qkv_width + query_cols]
    gains = low[:, qkv_width + query_cols :].astype(F32)[:, :2].T
    gain_one, gain_two = gains[0], gains[1]
    gate_up_c = high[:, : 2 * unit_cols]
    down_c = high[:, 2 * unit_cols :]

    def normed(rows):
        inverse = lax.rsqrt(jnp.mean(rows * rows, -1, keepdims=True) + EPS_NORM)
        return rows * inverse, inverse

    row_in = hidden[0].astype(F32)
    normed_one, inv_one = normed(row_in)
    entry_one = (normed(hidden_all.astype(F32))[0] * gain_one).astype(BF)
    (cot,) = gather_tokens(sizes, 1, cotangent[0])

    projected = dot(entry_one, qkv_c).reshape(pair, total_rows, qkv_width)
    queries = projected[..., :query_cols].reshape(pair, total_rows, heads, HD)
    key_rows = projected[..., query_cols : query_cols + kv_cols].reshape(
        pair, total_rows, kv_heads, HD
    )
    value_rows = projected[..., query_cols + kv_cols :].reshape(pair, total_rows, kv_heads, HD)
    queries = (queries * cos_tab + turned(queries) * sin_tab).astype(BF)
    key_rows = (key_rows * cos_tab + turned(key_rows) * sin_tab).astype(BF)
    value_rows = value_rows.astype(BF)
    queries = queries.reshape(pair, total_rows, kv_heads, ratio, HD)

    def product(spec, left, right):
        return jnp.einsum(spec, left, right, preferred_element_type=F32)

    scores = product("stkgd,sukd->skgtu", queries, key_rows) * scale
    scores = jnp.where(visible, scores, NEG_FILL)
    top_score = jnp.max(scores, -1, keepdims=True)
    exponent = jnp.exp(scores - top_score)
    probability = exponent / jnp.sum(exponent, -1, keepdims=True)
    prob_low = probability.astype(BF)
    attended = product("skgtu,sukd->stkgd", prob_low, value_rows).astype(BF)
    attended = attended.reshape(pair * total_rows, query_cols)

    middle = row_in + scatter_tokens(sizes, 2, contract_cols(attended, out_c).astype(BF))
    normed_two, inv_two = normed(middle)
    (entry_two,) = gather_tokens(sizes, 3, (normed_two * gain_two).astype(BF))

    gate_up = dot(entry_two, gate_up_c)
    gate_part = gate_up[:, :unit_cols]
    up_part = gate_up[:, unit_cols:]
    sigmoid_gate = jax.nn.sigmoid(gate_part)
    silu_gate = gate_part * sigmoid_gate
    activated = (silu_gate * up_part).astype(BF)
    summed = scatter_tokens(sizes, 4, contract_cols(activated, down_c).astype(BF))
    output = (middle + summed).astype(BF)[None]
    grad_act = dot(cot, down_c)
    grad_gate = grad_act * up_part * sigmoid_gate * (1.0 + gate_part * (1.0 - sigmoid_gate))
    grad_up = grad_act * silu_gate
    grad_gu = jnp.concatenate([grad_gate, grad_up], 1).astype(BF)
    grad_entry_two = scatter_tokens(sizes, 5, contract_cols(grad_gu, gate_up_c).astype(BF))
    grad_top = cotangent[0].astype(F32)
    grad_mid_norm, grad_gain_two = norm_back(grad_entry_two, normed_two, inv_two, gain_two)
    grad_middle = grad_top + grad_mid_norm
    (grad_branch,) = gather_tokens(sizes, 6, grad_middle.astype(BF))

    grad_attended = dot(grad_branch, out_c).astype(BF)
    grad_heads = grad_attended.reshape(pair, total_rows, kv_heads, ratio, HD)
    grad_prob = product("stkgd,sukd->skgtu", grad_heads, value_rows)
    delta_row = jnp.sum(probability * grad_prob, -1, keepdims=True)
    grad_scores = jnp.where(visible, probability * (grad_prob - delta_row), 0.0).astype(BF)
    grad_queries = product("skgtu,sukd->stkgd", grad_scores, key_rows) * scale
    grad_keys = product("skgtu,stkgd->sukd", grad_scores, queries) * scale
    grad_values = product("skgtu,stkgd->sukd", prob_low, grad_heads)
    grad_queries = grad_queries.reshape(pair, total_rows, heads, HD)
    grad_queries = grad_queries * cos_tab + turned_back(grad_queries * sin_tab)
    grad_keys = grad_keys * cos_tab + turned_back(grad_keys * sin_tab)
    grad_projected = jnp.concatenate(
        [
            grad_queries.reshape(-1, query_cols),
            grad_keys.reshape(-1, kv_cols),
            grad_values.reshape(-1, kv_cols),
        ],
        1,
    ).astype(BF)
    grad_entry_one = scatter_tokens(sizes, 7, contract_cols(grad_projected, qkv_c).astype(BF))
    grad_row_norm, grad_gain_one = norm_back(grad_entry_one, normed_one, inv_one, gain_one)
    grad_hidden = (grad_middle + grad_row_norm).astype(BF)[None]

    grad_gate, grad_up, grad_down, grad_query, grad_key_value, grad_out = collect_grads(
        sizes, 8, entry_two, grad_gu, cot, activated, entry_one, grad_projected, grad_branch, attended
    )
    grad_gains = lax.psum_scatter(
        jnp.stack([grad_gain_one, grad_gain_two]), everyone, scatter_dimension=1, tiled=True
    )
    rows = w_qkv.shape[0]
    grad_key_value = grad_key_value.reshape(rows, group, 2, kv_cols).transpose(0, 2, 1, 3)
    grad_qkv = jnp.concatenate([grad_query, grad_key_value.reshape(rows, -1)], 1)
    grad_gate_up = jnp.concatenate([grad_gate, grad_up], 1)
    new_gains, new_mom_gains = adamw(norm_gains, grad_gains, mom_gains, LR_GAIN, 0.0)
    grad_qkv, new_qkv, new_mom_qkv = adamw_columns(grad_qkv, w_qkv, mom_qkv, LR_MATRIX, DECAY_MATRIX)
    grad_out, new_out, new_mom_out = adamw_columns(grad_out, w_out, mom_out, LR_OUTPUT, DECAY_MATRIX)
    grad_gate_up, new_gate_up, new_mom_gate_up = adamw_columns(
        grad_gate_up, w_gate_up, mom_gate_up, LR_MATRIX, DECAY_MATRIX
    )
    grad_down, new_down, new_mom_down = adamw_columns(
        grad_down, w_down, mom_down, LR_MATRIX, DECAY_MATRIX
    )
    return (
        output,
        grad_hidden,
        grad_gains,
        grad_qkv,
        grad_out,
        grad_gate_up,
        grad_down,
        new_gains,
        new_qkv,
        new_out,
        new_gate_up,
        new_down,
        new_mom_gains,
        new_mom_qkv,
        new_mom_out,
        new_mom_gate_up,
        new_mom_down,
    )


def solution(mesh):
    shape = dict(mesh.shape)
    pair = 2 if shape["ctx"] * 2 <= KV and shape["fsdp"] % 2 == 0 else 1
    sizes = {"dp": shape["dp"], "ctx": shape["ctx"], "x": shape["fsdp"] // pair, "core": pair}
    finer = Mesh(mesh.devices.reshape(tuple(sizes.values())), tuple(sizes))
    tokens = P(("dp", "x", "core"), "ctx", None)
    everyone = ("dp", "ctx", "x", "core")
    rows, gains = P(everyone, None), P(None, everyone)
    row_moments, gain_moments = P(None, everyone, None), P(None, None, everyone)
    weights = (gains, rows, rows, rows, rows)
    moments = (gain_moments, row_moments, row_moments, row_moments, row_moments)
    return jax.shard_map(
        functools.partial(shards, sizes),
        mesh=finer,
        in_specs=(tokens, tokens, P()) + weights + moments,
        out_specs=(tokens, tokens) + weights + weights + moments,
        check_vma=False,
    )
```

```python
import functools
import math

import jax
import jax.numpy as jnp
from jax import lax
from jax.experimental import pallas as pl
from jax.experimental.pallas import tpu as pltpu
from jax.sharding import Mesh
from jax.sharding import PartitionSpec as P

MESH = pl.DeviceIdType.MESH
BF = jnp.bfloat16
F32 = jnp.float32
H = 32
KV = 8
HD = 64
FF = 8192


EPS_NORM = 1e-05
NEG_FILL = -1000000000.0
THETA = 500000.0
BETA_ONE = 0.9
BETA_TWO = 0.95
ADAM_EPS = 1e-08
DECAY_MATRIX = 0.1
LR_MATRIX = 0.01
LR_OUTPUT = 0.06
LR_GAIN = 0.3


def rope_table(positions):
    half_dim = HD // 2
    index_row = jnp.arange(half_dim, dtype=jnp.float32)
    frequency = jnp.exp(-(2.0 * index_row / HD) * math.log(THETA))
    wavelen = 2.0 * math.pi / frequency
    smooth = (8192.0 / wavelen - 1.0) / 3.0
    scaled = jnp.where(
        wavelen < 2048.0,
        frequency,
        jnp.where(
            wavelen > 8192.0,
            frequency / 32.0,
            (1.0 - smooth) * frequency / 32.0 + smooth * frequency,
        ),
    )
    angles = positions.astype(jnp.float32)[:, None] * scaled[None, :]
    cosine = jnp.cos(angles)
    sine_part = jnp.sin(angles)
    return (jnp.concatenate([cosine, cosine], 1), jnp.concatenate([sine_part, sine_part], 1))


def adamw(weight, gradient, states, step_rate, decay_rate):
    first_mom = BETA_ONE * states[0] + (1.0 - BETA_ONE) * gradient
    root_mom = jnp.sqrt(BETA_TWO * states[1] * states[1] + (1.0 - BETA_TWO) * gradient * gradient)
    first_hat = first_mom / (1.0 - BETA_ONE**3)
    root_hat = root_mom / math.sqrt(1.0 - BETA_TWO**3)
    updated = weight - step_rate * (first_hat / (root_hat + ADAM_EPS) + decay_rate * weight)
    return (updated, jnp.stack([first_mom, root_mom]))


def contract_rows(left_arr, right_arr):
    return lax.dot_general(
        left_arr, right_arr, (((0,), (0,)), ((), ())), preferred_element_type=jnp.float32
    )


def contract_cols(left_arr, right_arr):
    return lax.dot_general(
        left_arr, right_arr, (((1,), (1,)), ((), ())), preferred_element_type=jnp.float32
    )


def wrap(value, size):
    return lax.rem(value + size, size)


def remote(src, dst, send_sem, recv_sem, **where):
    return pltpu.make_async_remote_copy(
        src_ref=src,
        dst_ref=dst,
        send_sem=send_sem,
        recv_sem=recv_sem,
        device_id=where,
        device_id_type=MESH,
    )


def greet(places):
    barrier = pltpu.get_barrier_semaphore()
    for where in places:
        pl.semaphore_signal(barrier, inc=1, device_id=where, device_id_type=MESH)
    pl.semaphore_wait(barrier, len(places))


def greet_line(line, pair):
    barrier = pltpu.get_barrier_semaphore()
    here = lax.axis_index("ctx")

    @pl.when(here > 0)
    def _():
        pl.semaphore_signal(barrier, inc=1, device_id={"ctx": here - 1}, device_id_type=MESH)

    @pl.when(here < line - 1)
    def _():
        pl.semaphore_signal(barrier, inc=1, device_id={"ctx": here + 1}, device_id_type=MESH)

    if pair > 1:
        pl.semaphore_signal(
            barrier, inc=1, device_id={"core": 1 - lax.axis_index("core")}, device_id_type=MESH
        )
    ends = (here == 0).astype(jnp.int32) + (here == line - 1).astype(jnp.int32)
    pl.semaphore_wait(barrier, 2 - ends + (1 if pair > 1 else 0))


class Travel:
    @staticmethod
    def sems(many, line):
        return [pltpu.SemaphoreType.DMA((many,))] + [pltpu.SemaphoreType.DMA((many, 2, line))] * 4

    def __init__(self, line, pair, ins, outs, own_sem, line_send, line_recv, core_send, core_recv):
        self.line, self.pair, self.ins, self.outs = line, pair, ins, outs
        self.own_sem, self.line_sems, self.core_sems = own_sem, (line_send, line_recv), (core_send, core_recv)
        self.here = lax.axis_index("ctx")
        self.core = lax.axis_index("core")

    def block(self, way, step):
        return self.here - 1 - step if way == 0 else self.here + 1 + step

    def copy(self, sems, at, source, place, **where):
        return remote(place if source is None else source, place, sems[0].at[at], sems[1].at[at], **where)

    def hop(self, item, way, step, source=None):
        place = self.outs[item](self.core, self.block(way, step - 1))
        target = self.here + 1 if way == 0 else self.here - 1
        return self.copy(self.line_sems, (item, way, step), source, place, ctx=target)

    def arrived(self, item, way, step):
        place = self.outs[item](self.core, self.block(way, step))
        return self.copy(self.line_sems, (item, way, step), None, place, ctx=self.here)

    def share(self, item, way, step, source=None):
        place = self.outs[item](self.core, self.block(way, step))
        return self.copy(self.core_sems, (item, way, step + 1), source, place, core=1 - self.core)

    def shared(self, item, way, step):
        place = self.outs[item](1 - self.core, self.block(way, step))
        return self.copy(self.core_sems, (item, way, step + 1), None, place, core=1 - self.core)

    def own(self, item):
        place = self.outs[item](self.core, self.here)
        return pltpu.make_async_copy(self.ins[item], place, self.own_sem.at[item])

    def sends(self, way):
        return self.here < self.line - 1 if way == 0 else self.here > 0

    def has(self, way, step):
        return self.block(way, step) >= 0 if way == 0 else self.block(way, step) <= self.line - 1

    def begin(self):
        for item in range(len(self.ins)):
            for way in range(2):

                @pl.when(self.sends(way))
                def _(item=item, way=way):
                    self.hop(item, way, 0, self.ins[item]).start()

            if self.pair > 1:
                self.share(item, 0, -1, self.ins[item]).start()
            if self.ins[item] is not None:
                self.own(item).start()

    def step(self, step):
        for item in range(len(self.ins)):
            for way in range(2):

                @pl.when(self.has(way, step))
                def _(item=item, way=way):
                    self.arrived(item, way, step).wait_recv()
                    if step + 1 < self.line - 1:

                        @pl.when(self.sends(way))
                        def _():
                            self.hop(item, way, step + 1).start()

                    if self.pair > 1:
                        self.share(item, way, step).start()

    def end(self):
        for item in range(len(self.ins)):
            if self.ins[item] is not None:
                self.own(item).wait()
            if self.pair > 1:
                self.share(item, 0, -1, self.ins[item]).wait_send()
                self.shared(item, 0, -1).wait_recv()
            for way in range(2):

                @pl.when(self.sends(way))
                def _(item=item, way=way):
                    self.hop(item, way, 0, self.ins[item]).wait_send()

                for step in range(self.line - 1):

                    @pl.when(self.has(way, step))
                    def _(item=item, way=way, step=step):
                        if step + 1 < self.line - 1:

                            @pl.when(self.sends(way))
                            def _():
                                self.hop(item, way, step + 1).wait_send()

                        if self.pair > 1:
                            self.share(item, way, step).wait_send()
                            self.shared(item, way, step).wait_recv()


def add_rows(rows, out_ref, *parts):
    def one(index, carry):
        at = pl.ds(pl.multiple_of(index * 16, 16), 16)
        total = parts[0][at, :].astype(F32)
        for part in parts[1:]:
            total = total + part[at, :].astype(F32)
        out_ref[at, :] = total.astype(out_ref.dtype)
        return carry

    lax.fori_loop(0, rows // 16, one, 0)


class Reduce:
    @staticmethod
    def sems(*outer):
        dma = pltpu.SemaphoreType.DMA
        return lambda line: [dma(outer), dma(outer), dma(outer + (2, line)), dma(outer + (2, line))]

    @staticmethod
    def room(line, pair, rows, columns, *outer):
        return [
            pltpu.VMEM(outer + (pair, line, rows, columns), BF),
            pltpu.VMEM(outer + (line, rows, columns), BF),
            pltpu.VMEM(outer + (line + 1, rows, columns), BF),
        ]

    def __init__(self, line, pair, part, near, landed, core_send, core_recv, line_send, line_recv, at):
        self.line, self.pair, self.at = line, pair, at
        self.part, self.near, self.landed = part, near, landed
        self.core_sems, self.line_sems = (core_send, core_recv), (line_send, line_recv)
        self.here, self.core = lax.axis_index("ctx"), lax.axis_index("core")
        self.rows = part.shape[-2]

    def mine(self, block):
        return self.part.at[self.at + (self.core, block)]

    def across(self):
        return remote(
            self.part.at[self.at + (1 - self.core,)],
            self.near.at[self.at],
            self.core_sems[0].at[self.at],
            self.core_sems[1].at[self.at],
            core=1 - self.core,
        )

    def slot(self, way, block):
        return self.landed.at[self.at + (block + 1 if way == 0 else block,)]

    def onward(self, way, block, here):
        index = self.at + (way, block)
        return remote(
            self.mine(block),
            self.slot(way, block),
            self.line_sems[0].at[index],
            self.line_sems[1].at[index],
            ctx=here + 1 if way == 0 else here - 1,
        )

    def begin(self):
        if self.pair > 1:
            self.across().start()

    def settle(self):
        if self.pair > 1:
            self.across().wait_recv()

    def terms(self, block):
        return [self.mine(block)] + ([self.near.at[self.at + (block,)]] if self.pair > 1 else [])

    def relay(self, way, block, here):
        @pl.when(self.here == here)
        def _():
            terms = self.terms(block)
            if here != (0 if way == 0 else self.line - 1):
                self.onward(way, block, here).wait_recv()
                terms.append(self.slot(way, block))
            if len(terms) > 1:
                add_rows(self.rows, self.mine(block), *terms)
            self.onward(way, block, here).start()

    def finish(self, here, total_ref):
        @pl.when(self.here == here)
        def _():
            terms = self.terms(here)
            for way, has in ((0, here > 0), (1, here < self.line - 1)):
                if has:
                    self.onward(way, here, here).wait_recv()
                    terms.append(self.slot(way, here))
            add_rows(self.rows, total_ref, *terms)

    def drain(self):
        if self.pair > 1:
            self.across().wait_send()
        for here in range(self.line):

            @pl.when(self.here == here)
            def _(here=here):
                for block in range(self.line):
                    if block != here:
                        self.onward(0 if block > here else 1, block, here).wait_send()

    def plan(self, start, total_ref, after):
        ends, steps = self.line - 1, [(start, self.begin), (start + LAG, self.settle)]
        for way in range(2):
            for block in range(self.line):
                for here in range(self.line):
                    if here < block if way == 0 else here > block:
                        wait = ends - block if way == 0 else block
                        depth = here if way == 0 else ends - here
                        when = start + LAG + wait * SEND + depth * HOP
                        steps.append((when, functools.partial(self.relay, way, block, here)))
        finish = start + LAG + ends * HOP + 0.5
        for here in range(self.line):
            steps.append((finish, functools.partial(self.finish, here, total_ref)))
        steps.append((finish, after))
        return steps, finish


SEND, HOP, LAG = 3.0, 4.5, 2.5


def run_steps(steps):
    for _, step in sorted(steps, key=lambda item: item[0]):
        step()


def scatter_kernel(line, pair, chunks, terms_ref, out_ref, part, near, landed, total, load_sem, *sems):
    rows = part.shape[-2]
    loads = [
        pltpu.make_async_copy(
            terms_ref.at[:, :, pl.ds(chunk * rows, rows)], part.at[chunk], load_sem.at[chunk]
        )
        for chunk in range(chunks)
    ]
    for load in loads:
        load.start()
    greet_line(line, pair)
    sums = [Reduce(line, pair, part, near, landed, *sems, (chunk,)) for chunk in range(chunks)]
    steps = []
    for chunk, one in enumerate(sums):

        def after(chunk=chunk):
            out_ref[chunk * rows : (chunk + 1) * rows, :] = total[...]

        start = chunk * (line - 1) * SEND
        steps.append((start, loads[chunk].wait))
        steps += one.plan(start, total, after)[0]
    run_steps(steps)
    for one in sums:
        one.drain()


def scatter_tokens(sizes, collective_id, terms):
    line, pair = sizes["ctx"], sizes["core"]
    columns = terms.shape[1]
    rows = terms.shape[0] // (line * pair)
    chunks = 4
    return pl.pallas_call(
        functools.partial(scatter_kernel, line, pair, chunks),
        out_shape=jax.ShapeDtypeStruct((rows, columns), F32),
        in_specs=[pl.BlockSpec(memory_space=pl.ANY)],
        out_specs=pl.BlockSpec(memory_space=pltpu.VMEM),
        scratch_shapes=[
            *Reduce.room(line, pair, rows // chunks, columns, chunks),
            pltpu.VMEM((rows // chunks, columns), F32),
            pltpu.SemaphoreType.DMA((chunks,)),
            *Reduce.sems(chunks)(line),
        ],
        compiler_params=pltpu.CompilerParams(
            collective_id=collective_id, has_side_effects=True, vmem_limit_bytes=40 * 2**20
        ),
    )(terms.reshape(pair, line, rows, columns))


def middle_kernel(line, pair, chunks, *refs):
    heads_ref, low_ref, high_ref, hidden_ref, cot_ref, gain_ref = refs[:6]
    output_ref, grad_mid_ref, gain_grad_ref, branch_ref, entry_ref, cots_ref, act_ref, dgu_ref = refs[6:14]
    out_w, ffn_w, part, near, landed, total, middle, branch, load_sem = refs[14:23]
    reduce_sems, travel_sems = refs[23:27], refs[27:]
    width = hidden_ref.shape[1]
    rows = part.shape[-2]
    tokens = pair * line * rows
    query_cols = out_w.shape[1]
    units = ffn_w.shape[1] // 3
    core, here = lax.axis_index("core"), lax.axis_index("ctx")
    first_col = low_ref.shape[1] - 128 - query_cols
    loads = [
        pltpu.make_async_copy(low_ref.at[:, pl.ds(first_col, query_cols)], out_w, load_sem.at[0]),
        pltpu.make_async_copy(high_ref, ffn_w, load_sem.at[1]),
    ]
    for load in loads:
        load.start()
    greet_line(line, pair)
    steps = []
    sums, travels = [], []

    def chunk_rows(chunk):
        return slice(chunk * rows, (chunk + 1) * rows)

    def reducer(kind, chunk):
        one = Reduce(line, pair, part, near, landed, *reduce_sems, (kind, chunk))
        sums.append(one)
        return one

    def traveller(kind, chunk, source, place, start):
        one = Travel(line, pair, [source], [place], *[sem.at[kind, chunk] for sem in travel_sems])
        travels.append(one)
        steps.append((start, one.begin))
        for step in range(line - 1):
            steps.append((start + (step + 1) * HOP, functools.partial(one.step, step)))
        finish = start + line * HOP - 1.0
        steps.append((finish, one.end))
        return finish

    def product(chunk):
        mine = heads_ref[:, :, chunk_rows(chunk), :].reshape(tokens, query_cols)

        @pl.loop(0, width // 512)
        def _(index):
            at = pl.ds(pl.multiple_of(index * 512, 512), 512)
            term = contract_cols(mine, out_w[at, :]).astype(BF)
            part[0, chunk, :, :, :, at] = term.reshape(pair, line, rows, 512)

    def norm_rows(chunk):
        mid = hidden_ref[chunk_rows(chunk), :].astype(F32) + total[...]
        middle[chunk_rows(chunk), :] = mid
        inverse = lax.rsqrt(jnp.mean(mid * mid, -1, keepdims=True) + EPS_NORM)
        entry_ref[chunk, core, here] = (mid * inverse * gain_ref[...]).astype(BF)

    def units_part(chunk, index, count):
        size = units // count
        entry = entry_ref[chunk].reshape(tokens, width)
        low, high = index * size, (index + 1) * size
        gate = dot(entry, ffn_w[:, low:high])
        up = dot(entry, ffn_w[:, units + low : units + high])
        grad_act = dot(cots_ref[chunk].reshape(tokens, width), ffn_w[:, 2 * units + low : 2 * units + high])
        sigmoid = 1.0 / (1.0 + jnp.exp(-gate))
        silu = gate * sigmoid
        act_ref[chunk, :, low:high] = (silu * up).astype(BF)
        dgu_ref[chunk, :, low:high] = (grad_act * up * sigmoid * (1.0 + gate * (1.0 - sigmoid))).astype(BF)
        dgu_ref[chunk, :, units + low : units + high] = (grad_act * silu).astype(BF)

    def back_part(chunk, index, count):
        size = width // count
        at = slice(index * size, (index + 1) * size)
        term = contract_cols(dgu_ref[chunk], ffn_w[at, : 2 * units]).astype(BF)
        part[1, chunk, :, :, :, at] = term.reshape(pair, line, rows, size)

    def down_part(chunk, index, count):
        size = width // count
        at = slice(index * size, (index + 1) * size)
        term = contract_cols(act_ref[chunk], ffn_w[at, 2 * units :]).astype(BF)
        part[2, chunk, :, :, :, at] = term.reshape(pair, line, rows, size)

    def norm_rows_back(chunk):
        mid = middle[chunk_rows(chunk), :]
        inverse = lax.rsqrt(jnp.mean(mid * mid, -1, keepdims=True) + EPS_NORM)
        normed = mid * inverse
        grad_entry = total[...]
        gain_term = jnp.sum(grad_entry * normed, 0, keepdims=True)
        if chunk == 0:
            gain_grad_ref[...] = gain_term
        else:
            gain_grad_ref[...] += gain_term
        grad_normed = grad_entry * gain_ref[...]
        grad_rows = inverse * (
            grad_normed - normed * jnp.mean(grad_normed * normed, -1, keepdims=True)
        )
        grad_mid = cot_ref[chunk_rows(chunk), :].astype(F32) + grad_rows
        grad_mid_ref[chunk_rows(chunk), :] = grad_mid
        branch[chunk] = grad_mid.astype(BF)

    def write_output(chunk):
        output_ref[chunk_rows(chunk), :] = (middle[chunk_rows(chunk), :] + total[...]).astype(BF)

    span = (line - 1) * SEND
    ready_ffn = ready_back = 0.0
    starts = []
    steps.append((0.0, loads[0].wait))
    for chunk in range(chunks):
        cot_done = traveller(
            0, chunk, cot_ref.at[chunk_rows(chunk)], lambda c, z, k=chunk: cots_ref.at[k, c, z], chunk * span
        )
        begin = 1.0 + chunk * span
        steps.append((begin - 0.5, functools.partial(product, chunk)))
        more, finish = reducer(0, chunk).plan(begin, total, functools.partial(norm_rows, chunk))
        steps += more
        arrived = traveller(1, chunk, None, lambda c, z, k=chunk: entry_ref.at[k, c, z], finish)
        begin = max(arrived, cot_done, ready_ffn) + 0.1
        if chunk == 0:
            steps.append((begin, loads[1].wait))
        count = 4
        for index in range(count):
            steps.append((begin + index, functools.partial(units_part, chunk, index, count)))
        for index in range(count):
            steps.append((begin + 4 + 0.8 * index, functools.partial(back_part, chunk, index, count)))
        for index in range(count):
            steps.append((begin + 7.3 + 0.5 * index, functools.partial(down_part, chunk, index, count)))
        ready_ffn = begin + 9.5
        begin = max(begin + 7.25, ready_back)
        ready_back = begin + span
        more, finish = reducer(1, chunk).plan(begin, total, functools.partial(norm_rows_back, chunk))
        steps += more
        traveller(
            2,
            chunk,
            branch.at[chunk],
            lambda c, z, k=chunk: branch_ref.at[c, z, pl.ds(k * rows, rows)],
            finish,
        )
    for chunk in range(chunks):
        begin = ready_back + chunk * span
        steps += reducer(2, chunk).plan(begin, total, functools.partial(write_output, chunk))[0]
    run_steps(steps)
    for one in sums:
        one.drain()


def middle_rows(sizes, collective_id, heads, low, high, hidden, cot, gain):
    line, pair = sizes["ctx"], sizes["core"]
    rows, width = hidden.shape
    chunks = 4
    step = rows // chunks
    tokens = pair * line * step
    units = high.shape[1] // 3
    query_cols = heads.shape[1]
    any_spec = pl.BlockSpec(memory_space=pl.ANY)
    vmem = pl.BlockSpec(memory_space=pltpu.VMEM)
    shape = jax.ShapeDtypeStruct
    dma = pltpu.SemaphoreType.DMA
    outs = pl.pallas_call(
        functools.partial(middle_kernel, line, pair, chunks),
        out_shape=[
            shape((rows, width), BF),
            shape((rows, width), F32),
            shape((1, width), F32),
            shape((pair, line, rows, width), BF),
            shape((chunks, pair, line, step, width), BF),
            shape((chunks, pair, line, step, width), BF),
            shape((chunks, tokens, units), BF),
            shape((chunks, tokens, 2 * units), BF),
        ],
        in_specs=[vmem, any_spec, any_spec, vmem, vmem, vmem],
        out_specs=[vmem, vmem, vmem, any_spec, vmem, vmem, vmem, vmem],
        scratch_shapes=[
            pltpu.VMEM((width, query_cols), BF),
            pltpu.VMEM(high.shape, BF),
            *Reduce.room(line, pair, step, width, 3, chunks),
            pltpu.VMEM((step, width), F32),
            pltpu.VMEM((rows, width), F32),
            pltpu.VMEM((chunks, step, width), BF),
            dma((2,)),
            *Reduce.sems(3, chunks)(line),
            dma((3, chunks, 1)),
            *[dma((3, chunks, 1, 2, line))] * 4,
        ],
        compiler_params=pltpu.CompilerParams(
            collective_id=collective_id, has_side_effects=True, vmem_limit_bytes=63 * 2**20
        ),
    )(heads.reshape(pair, line, rows, query_cols), low, high, hidden, cot, gain)
    return list(outs[:3]) + [out.reshape(-1, out.shape[-1]) for out in outs[3:]]


def blocks_in_order(line, pair):
    away = sorted(range(line), key=lambda d: min(d, line - d))
    return [(dz, dc) for dz in away for dc in range(pair)]


def greet_all(sizes):
    names = ("dp", "ctx", "x", "core")
    at = {name: lax.axis_index(name) for name in names}
    places = []
    for dz, dc in blocks_in_order(sizes["ctx"], sizes["core"]):
        if dz or dc:
            places.append(
                {"ctx": wrap(at["ctx"] + dz, sizes["ctx"]), "core": wrap(at["core"] + dc, sizes["core"])}
            )
    for name in ("dp", "x"):
        for step in range(1, sizes[name]):
            places.append({name: wrap(at[name] + step, sizes[name])})
    greet(places)


def pack_member(refs, member, rows, group, tall, wide):
    qkv_ref, out_ref, gate_up_ref, down_ref, gain_ref = refs
    heads, keys, units = H * HD // group, KV * HD // group, FF // group
    low = lambda values: values.astype(BF)
    tall[member, :, :heads] = low(qkv_ref[:, member * heads : (member + 1) * heads])
    key_at, value_at = H * HD + member * keys, (H + KV) * HD + member * keys
    tall[member, :, heads : heads + 2 * keys] = low(
        jnp.concatenate(
            [qkv_ref[:, key_at : key_at + keys], qkv_ref[:, value_at : value_at + keys]], 1
        )
    )
    tall[member, :, heads + 2 * keys : 2 * heads + 2 * keys] = low(
        out_ref[:, member * heads : (member + 1) * heads]
    )
    tall[member, :, 2 * heads + 2 * keys :] = low(gain_ref[...])
    wide[member, :, :units] = low(gate_up_ref[:, member * units : (member + 1) * units])
    wide[member, :, units : 2 * units] = low(
        gate_up_ref[:, FF + member * units : FF + (member + 1) * units]
    )
    wide[member, :, 2 * units :] = low(down_ref[:, member * units : (member + 1) * units])


def spread_kernel(sizes, *refs):
    weight_refs, hidden_ref = refs[:5], refs[5]
    outs, hidden_out = refs[6:8], refs[8]
    packs = refs[9:11]
    own_sem, f_send, f_recv, a_send, a_recv, b_send, b_recv = refs[11:18]
    travel_sems = refs[18:]
    line, pair = sizes["ctx"], sizes["core"]
    group = line * pair
    rows = packs[0].shape[1]
    at = {name: lax.axis_index(name) for name in ("dp", "ctx", "x", "core")}
    greet_all(sizes)
    order = blocks_in_order(line, pair)
    me = at["ctx"] * pair + at["core"]
    travel = Travel(line, pair, [hidden_ref], [lambda c, z: hidden_out.at[c, z]], *travel_sems)
    travel.begin()

    def first(kind, index):
        dz, dc = order[index]
        z, c = wrap(at["ctx"] + dz, line), wrap(at["core"] + dc, pair)
        return remote(
            packs[kind].at[z * pair + c],
            outs[kind].at[at["dp"], at["ctx"], at["x"], at["core"]],
            f_send.at[kind, index],
            f_recv.at[kind, index],
            ctx=z,
            core=c,
        )

    def place(kind, index, moved):
        dz, dc = order[index]
        z, c = wrap(at["ctx"] - dz, line), wrap(at["core"] - dc, pair)
        spot = {name: wrap(at[name] - moved.get(name, 0), sizes[name]) for name in ("dp", "x")}
        return outs[kind].at[spot["dp"], z, spot["x"], c]

    def came(kind, index):
        spot = place(kind, index, {})
        return remote(spot, spot, f_send.at[kind, index], f_recv.at[kind, index], core=at["core"])

    def axes(index):
        dz, dc = order[index]
        return ("x", "dp") if (dz + dc) % 2 == 0 else ("dp", "x")

    def hop_one(kind, index, step):
        name = axes(index)[0]
        spot = place(kind, index, {})
        return remote(
            spot,
            spot,
            a_send.at[kind, index, step],
            a_recv.at[kind, index, step],
            **{name: wrap(at[name] + step, sizes[name])},
        )

    def one_came(kind, index, step):
        name = axes(index)[0]
        spot = place(kind, index, {name: step})
        return remote(
            spot, spot, a_send.at[kind, index, step], a_recv.at[kind, index, step], core=at["core"]
        )

    def hop_two(kind, index, step, far):
        name, other = axes(index)
        spot = place(kind, index, {name: step})
        return remote(
            spot,
            spot,
            b_send.at[kind, index, step, far],
            b_recv.at[kind, index, step, far],
            **{other: wrap(at[other] + far, sizes[other])},
        )

    def two_came(kind, index, step, far):
        name, other = axes(index)
        spot = place(kind, index, {name: step, other: far})
        return remote(
            spot,
            spot,
            b_send.at[kind, index, step, far],
            b_recv.at[kind, index, step, far],
            core=at["core"],
        )

    def own(kind):
        return pltpu.make_async_copy(
            packs[kind].at[me],
            outs[kind].at[at["dp"], at["ctx"], at["x"], at["core"]],
            own_sem.at[kind],
        )

    def onward(kind, index):
        name, other = axes(index)
        for step in range(1, sizes[name]):
            hop_one(kind, index, step).start()
        for far in range(1, sizes[other]):
            hop_two(kind, index, 0, far).start()

    def onward_two(kind, index):
        name, other = axes(index)
        for step in range(1, sizes[name]):
            one_came(kind, index, step).wait_recv()
            for far in range(1, sizes[other]):
                hop_two(kind, index, step, far).start()

    for member in range(group):
        pack_member(weight_refs, member, rows, group, *packs)
    ahead, late = 3, 1
    for kind in range(2):
        own(kind).start()
        for index in range(1, 1 + ahead):
            first(kind, index).start()
    for tick in range(group + late):
        if tick < group:
            for kind in range(2):
                if tick == 0:
                    own(kind).wait()
                else:
                    came(kind, tick).wait_recv()
                onward(kind, tick)
                if 1 + ahead <= tick + ahead < group and tick:
                    first(kind, tick + ahead).start()
        if tick % 2 == 1 and tick // 2 < line - 1:
            travel.step(tick // 2)
        if tick >= late:
            for kind in range(2):
                onward_two(kind, tick - late)
    travel.end()
    for kind in range(2):
        for index in range(group):
            if index:
                first(kind, index).wait_send()
            name, other = axes(index)
            for step in range(sizes[name]):
                if step:
                    hop_one(kind, index, step).wait_send()
                for far in range(1, sizes[other]):
                    hop_two(kind, index, step, far).wait_send()
                    two_came(kind, index, step, far).wait_recv()


def spread_weights(sizes, collective_id, hidden, gains, *weights):
    line, pair = sizes["ctx"], sizes["core"]
    group = line * pair
    rows = weights[0].shape[0]
    steps = max(sizes["dp"], sizes["x"])
    tall, wide = (2 * H * HD + 2 * KV * HD) // group + 128, 3 * FF // group
    gain_tile = jnp.pad(gains.T, ((0, 0), (0, 126)))
    any_spec = pl.BlockSpec(memory_space=pl.ANY)
    vmem = pl.BlockSpec(memory_space=pltpu.VMEM)
    everyone = (sizes["dp"], line, sizes["x"], pair, rows)
    low, high, tokens = pl.pallas_call(
        functools.partial(spread_kernel, sizes),
        out_shape=[
            jax.ShapeDtypeStruct(everyone + (tall,), BF),
            jax.ShapeDtypeStruct(everyone + (wide,), BF),
            jax.ShapeDtypeStruct((pair, line) + hidden.shape, BF),
        ],
        in_specs=[vmem] * 5 + [any_spec],
        out_specs=[any_spec] * 3,
        scratch_shapes=[
            pltpu.VMEM((group, rows, tall), BF),
            pltpu.VMEM((group, rows, wide), BF),
            pltpu.SemaphoreType.DMA((2,)),
            pltpu.SemaphoreType.DMA((2, group)),
            pltpu.SemaphoreType.DMA((2, group)),
            pltpu.SemaphoreType.DMA((2, group, steps)),
            pltpu.SemaphoreType.DMA((2, group, steps)),
            pltpu.SemaphoreType.DMA((2, group, steps, steps)),
            pltpu.SemaphoreType.DMA((2, group, steps, steps)),
            *Travel.sems(1, line),
        ],
        compiler_params=pltpu.CompilerParams(
            collective_id=collective_id, has_side_effects=True, vmem_limit_bytes=40 * 2**20
        ),
    )(*weights, gain_tile, hidden)
    return low.reshape(-1, tall), high.reshape(-1, wide), tokens.reshape(-1, hidden.shape[1])


def collect_kernel(sizes, widths, *refs):
    many = len(widths)
    pieces = grad_pieces(sizes)
    lefts, rights = refs[: 2 * many : 2], refs[1 : 2 * many : 2]
    refs = refs[2 * many :]
    outs, refs = refs[: len(pieces)], refs[len(pieces) :]
    held, refs = refs[: 2 * many], refs[2 * many :]
    terms, near, far_in = refs[:3]
    load_sem, own_sem, a_send, a_recv, b_send, b_recv, f_send, f_recv = refs[3:]
    line, pair = sizes["ctx"], sizes["core"]
    rows = terms.shape[-2]
    across = sizes["x"] * pair * rows
    at = {name: lax.axis_index(name) for name in ("dp", "ctx", "x", "core")}
    me = at["ctx"] * pair + at["core"]
    loads = [
        pltpu.make_async_copy(source, target, load_sem.at[i])
        for i, (source, target) in enumerate(zip((r for two in zip(lefts, rights) for r in two), held))
    ]
    for load in loads:
        load.start()
    greet_all(sizes)
    away = sorted(range(line), key=lambda d: -min(d, line - d))
    order = [(dz, dc) for dz in away for dc in range(pair)]

    def spot_of(index):
        dz, dc = order[index]
        return wrap(at["ctx"] + dz, line), wrap(at["core"] + dc, pair)

    def axes(index):
        dz, dc = order[index]
        return ("dp", "x") if (dz + dc) % 2 == 0 else ("x", "dp")

    def multiply(tick):
        z = wrap(at["ctx"] + away[tick], line)
        start = 0
        for item, width in enumerate(widths):
            left, right = held[2 * item], held[2 * item + 1]
            step = math.gcd(width, 512)

            @pl.loop(0, sizes["dp"])
            def _(dp, left=left, right=right, start=start, width=width, step=step):
                lanes = pl.ds(pl.multiple_of((dp * line + z) * across, 128), across)
                left_t = left[:, lanes].T

                @pl.loop(0, width // step)
                def _(part):
                    columns = pl.ds(pl.multiple_of(part * step, 128), step)
                    into = pl.ds(pl.multiple_of(start + part * step, 128), step)
                    product = dot(left_t, right[:, columns]).astype(BF)
                    for x in range(sizes["x"]):
                        for core in range(pair):
                            low = (x * pair + core) * rows
                            terms[tick, dp, x, core, :, into] = product[low : low + rows]

            start += width

    def block_terms(index, first_at, other_at):
        spot = {axes(index)[0]: first_at, axes(index)[1]: other_at}
        return terms.at[index // pair, spot["dp"], spot["x"], spot_of(index)[1]]

    def hop_one(index, step, place):
        name = axes(index)[0]
        to = wrap(at[name] + step, sizes[name])
        return remote(
            block_terms(index, to, place),
            near.at[index, (step - 1) * sizes[axes(index)[1]] + place],
            a_send.at[index, step, place],
            a_recv.at[index, step, place],
            **{name: to},
        )

    def hop_two(index, far):
        name, other = axes(index)
        to = wrap(at[other] + far, sizes[other])
        return remote(
            block_terms(index, at[name], to),
            far_in.at[index, far - 1],
            b_send.at[index, far],
            b_recv.at[index, far],
            **{other: to},
        )

    def done(index):
        name, other = axes(index)
        return block_terms(index, at[name], at[other])

    def piece_at(piece, member):
        _, width, offset = pieces[piece]
        return outs[piece].at[:, pl.ds(pl.multiple_of(member * width, 128), width)]

    def last(index, piece):
        z, c = spot_of(index)
        _, width, offset = pieces[piece]
        source = done(index).at[:, pl.ds(offset, width)]
        target = piece_at(piece, me)
        if index == len(order) - pair:
            return pltpu.make_async_copy(source, target, own_sem.at[piece])
        return remote(
            source, target, f_send.at[index, piece], f_recv.at[index, piece], ctx=z, core=c
        )

    def last_came(index, piece):
        dz, dc = order[index]
        z, c = wrap(at["ctx"] - dz, line), wrap(at["core"] - dc, pair)
        spot = piece_at(piece, z * pair + c)
        return remote(
            spot, spot, f_send.at[index, piece], f_recv.at[index, piece], core=at["core"]
        )

    def sum_one(index):
        name, other = axes(index)
        for far in list(range(1, sizes[other])) + [0]:
            place = wrap(at[other] + far, sizes[other])
            for step in range(1, sizes[name]):
                hop_one(index, step, place).wait_recv()
            kept = block_terms(index, at[name], place)
            add_rows(rows, kept, kept, *[near.at[index, (step - 1) * sizes[other] + place] for step in range(1, sizes[name])])
            if far:
                hop_two(index, far).start()

    def sum_two(index):
        other = axes(index)[1]
        for far in range(1, sizes[other]):
            hop_two(index, far).wait_recv()
        add_rows(
            rows, done(index), done(index), *[far_in.at[index, far - 1] for far in range(1, sizes[other])]
        )
        for piece in range(len(pieces)):
            last(index, piece).start()

    late, later = 1, 2
    for tick in range(line + later):
        if tick < line:
            if tick == 0:
                for load in loads:
                    load.wait()
            multiply(tick)
            for index in range(tick * pair, (tick + 1) * pair):
                name, other = axes(index)
                for far in list(range(1, sizes[other])) + [0]:
                    for step in range(1, sizes[name]):
                        hop_one(index, step, wrap(at[other] + far, sizes[other])).start()
        if late <= tick < line + late:
            for index in range((tick - late) * pair, (tick - late + 1) * pair):
                sum_one(index)
        if tick >= later:
            for index in range((tick - later) * pair, (tick - later + 1) * pair):
                sum_two(index)
    for index in range(len(order)):
        name, other = axes(index)
        for step in range(1, sizes[name]):
            for place in range(sizes[other]):
                hop_one(index, step, place).wait_send()
        for far in range(1, sizes[other]):
            hop_two(index, far).wait_send()
        for piece in range(len(pieces)):
            if index == len(order) - pair:
                last(index, piece).wait()
            else:
                last(index, piece).wait_send()
                last_came(index, piece).wait_recv()


def grad_pieces(sizes):
    group = sizes["ctx"] * sizes["core"]
    heads, keys, units = H * HD // group, KV * HD // group, FF // group
    pieces, offset = [], 0
    for name, width in (
        ("gate", units),
        ("up", units),
        ("down", units),
        ("query", heads),
        ("key_value", 2 * keys),
        ("out", heads),
    ):
        pieces.append((name, width, offset))
        offset += width
    return pieces


def collect_grads(sizes, collective_id, *factors):
    line, pair = sizes["ctx"], sizes["core"]
    group = line * pair
    rows = factors[0].shape[1] // (group * sizes["dp"] * sizes["x"])
    widths = [right.shape[1] for right in factors[1::2]]
    total = sum(widths)
    pieces = grad_pieces(sizes)
    steps = max(sizes["dp"], sizes["x"])
    any_spec = pl.BlockSpec(memory_space=pl.ANY)
    dma = pltpu.SemaphoreType.DMA
    return pl.pallas_call(
        functools.partial(collect_kernel, sizes, widths),
        out_shape=[jax.ShapeDtypeStruct((rows, group * width), BF) for _, width, _ in pieces],
        in_specs=[any_spec] * len(factors),
        out_specs=[any_spec] * len(pieces),
        scratch_shapes=[
            *[pltpu.VMEM(factor.shape, factor.dtype) for factor in factors],
            pltpu.VMEM((line, sizes["dp"], sizes["x"], pair, rows, total), BF),
            pltpu.VMEM((group, sizes["dp"] * sizes["x"] - min(sizes["dp"], sizes["x"]), rows, total), BF),
            pltpu.VMEM((group, steps - 1, rows, total), BF),
            dma((len(factors),)),
            dma((len(pieces),)),
            dma((group, steps, steps)),
            dma((group, steps, steps)),
            dma((group, steps)),
            dma((group, steps)),
            dma((group, len(pieces))),
            dma((group, len(pieces))),
        ],
        compiler_params=pltpu.CompilerParams(
            collective_id=collective_id, has_side_effects=True, vmem_limit_bytes=62 * 2**20
        ),
    )(*factors)


def adamw_kernel(step_rate, decay_rate, grad_ref, weight_ref, state_ref, grad_out, weight_out, state_out):
    gradient = grad_ref[...].astype(F32)
    grad_out[...] = gradient
    updated, states = adamw(weight_ref[...], gradient, state_ref[...], step_rate, decay_rate)
    weight_out[...] = updated
    state_out[...] = states


def adamw_columns(gradient, weight, states, step_rate, decay_rate):
    rows, columns = weight.shape
    step = math.gcd(columns, 1024)
    flat = pl.BlockSpec((rows, step), lambda i: (0, i))
    deep = pl.BlockSpec((2, rows, step), lambda i: (0, 0, i))
    return pl.pallas_call(
        functools.partial(adamw_kernel, step_rate, decay_rate),
        grid=(columns // step,),
        out_shape=[
            jax.ShapeDtypeStruct(weight.shape, F32),
            jax.ShapeDtypeStruct(weight.shape, F32),
            jax.ShapeDtypeStruct(states.shape, F32),
        ],
        in_specs=[flat, flat, deep],
        out_specs=[flat, flat, deep],
    )(gradient, weight, states)


def turned(values):
    half_dim = values.shape[-1] // 2
    return jnp.concatenate([-values[..., half_dim:], values[..., :half_dim]], -1)


def turned_back(values):
    half_dim = values.shape[-1] // 2
    return jnp.concatenate([values[..., half_dim:], -values[..., :half_dim]], -1)


def norm_back(grad_entry, normed, inverse, gain):
    grad_gain = jnp.sum(grad_entry * normed, 0)
    grad_normed = grad_entry * gain
    grad_rows = inverse * (grad_normed - normed * jnp.mean(grad_normed * normed, -1, keepdims=True))
    return (grad_rows, grad_gain)


def dot(left, right):
    return jnp.dot(left, right, preferred_element_type=F32)


def shards(
    sizes,
    hidden,
    cotangent,
    span_order,
    norm_gains,
    w_qkv,
    w_out,
    w_gate_up,
    w_down,
    mom_gains,
    mom_qkv,
    mom_out,
    mom_gate_up,
    mom_down,
):
    everyone = ("dp", "ctx", "x", "core")
    line, pair = sizes["ctx"], sizes["core"]
    group = line * pair
    block_rows, width = hidden.shape[1:]
    total_rows = block_rows * line
    span_rows = total_rows // span_order.shape[0]
    heads, kv_heads = H // group, KV // group
    ratio = heads // kv_heads
    query_cols, kv_cols, unit_cols = heads * HD, kv_heads * HD, FF // group
    scale = HD ** (-0.5)
    key_pos = (
        span_order[:, None] * span_rows + jnp.arange(span_rows, dtype=jnp.int32)[None, :]
    ).reshape(-1)
    visible = key_pos[None, :] <= key_pos[:, None]
    cos_tab, sin_tab = rope_table(key_pos)
    cos_tab, sin_tab = cos_tab[None, :, None, :], sin_tab[None, :, None, :]

    qkv_width = query_cols + 2 * kv_cols
    low, high, hidden_all = spread_weights(
        sizes, 0, hidden[0], norm_gains, w_qkv, w_out, w_gate_up, w_down
    )
    qkv_c = low[:, :qkv_width]
    out_c = low[:, qkv_width : qkv_width + query_cols]
    gains = low[:, qkv_width + query_cols :].astype(F32)[:, :2].T
    gain_one, gain_two = gains[0], gains[1]

    def normed(rows):
        inverse = lax.rsqrt(jnp.mean(rows * rows, -1, keepdims=True) + EPS_NORM)
        return rows * inverse, inverse

    row_in = hidden[0].astype(F32)
    normed_one, inv_one = normed(row_in)
    entry_one = (normed(hidden_all.astype(F32))[0] * gain_one).astype(BF)

    projected = dot(entry_one, qkv_c).reshape(pair, total_rows, qkv_width)
    queries = projected[..., :query_cols].reshape(pair, total_rows, heads, HD)
    key_rows = projected[..., query_cols : query_cols + kv_cols].reshape(
        pair, total_rows, kv_heads, HD
    )
    value_rows = projected[..., query_cols + kv_cols :].reshape(pair, total_rows, kv_heads, HD)
    queries = (queries * cos_tab + turned(queries) * sin_tab).astype(BF)
    key_rows = (key_rows * cos_tab + turned(key_rows) * sin_tab).astype(BF)
    value_rows = value_rows.astype(BF)
    queries = queries.reshape(pair, total_rows, kv_heads, ratio, HD)

    def product(spec, left, right):
        return jnp.einsum(spec, left, right, preferred_element_type=F32)

    scores = product("stkgd,sukd->skgtu", queries, key_rows) * scale
    scores = jnp.where(visible, scores, NEG_FILL)
    top_score = jnp.max(scores, -1, keepdims=True)
    exponent = jnp.exp(scores - top_score)
    probability = exponent / jnp.sum(exponent, -1, keepdims=True)
    prob_low = probability.astype(BF)
    attended = product("skgtu,sukd->stkgd", prob_low, value_rows).astype(BF)
    attended = attended.reshape(pair * total_rows, query_cols)

    output, grad_middle, grad_gain_two, grad_branch, entry_two, cot, activated, grad_gu = middle_rows(
        sizes, 1, attended, low, high, hidden[0], cotangent[0], gain_two[None]
    )
    output = output[None]

    grad_attended = dot(grad_branch, out_c).astype(BF)
    grad_heads = grad_attended.reshape(pair, total_rows, kv_heads, ratio, HD)
    grad_prob = product("stkgd,sukd->skgtu", grad_heads, value_rows)
    delta_row = jnp.sum(probability * grad_prob, -1, keepdims=True)
    grad_scores = jnp.where(visible, probability * (grad_prob - delta_row), 0.0).astype(BF)
    grad_queries = product("skgtu,sukd->stkgd", grad_scores, key_rows) * scale
    grad_keys = product("skgtu,stkgd->sukd", grad_scores, queries) * scale
    grad_values = product("skgtu,stkgd->sukd", prob_low, grad_heads)
    grad_queries = grad_queries.reshape(pair, total_rows, heads, HD)
    grad_queries = grad_queries * cos_tab + turned_back(grad_queries * sin_tab)
    grad_keys = grad_keys * cos_tab + turned_back(grad_keys * sin_tab)
    grad_projected = jnp.concatenate(
        [
            grad_queries.reshape(-1, query_cols),
            grad_keys.reshape(-1, kv_cols),
            grad_values.reshape(-1, kv_cols),
        ],
        1,
    ).astype(BF)
    grad_entry_one = scatter_tokens(sizes, 2, contract_cols(grad_projected, qkv_c).astype(BF))
    grad_row_norm, grad_gain_one = norm_back(grad_entry_one, normed_one, inv_one, gain_one)
    grad_hidden = (grad_middle + grad_row_norm).astype(BF)[None]

    grad_gate, grad_up, grad_down, grad_query, grad_key_value, grad_out = collect_grads(
        sizes, 3, entry_two, grad_gu, cot, activated, entry_one, grad_projected, grad_branch, attended
    )
    grad_gains = lax.psum_scatter(
        jnp.stack([grad_gain_one, grad_gain_two[0]]), everyone, scatter_dimension=1, tiled=True
    )
    rows = w_qkv.shape[0]
    grad_key_value = grad_key_value.reshape(rows, group, 2, kv_cols).transpose(0, 2, 1, 3)
    grad_qkv = jnp.concatenate([grad_query, grad_key_value.reshape(rows, -1)], 1)
    grad_gate_up = jnp.concatenate([grad_gate, grad_up], 1)
    new_gains, new_mom_gains = adamw(norm_gains, grad_gains, mom_gains, LR_GAIN, 0.0)
    grad_qkv, new_qkv, new_mom_qkv = adamw_columns(grad_qkv, w_qkv, mom_qkv, LR_MATRIX, DECAY_MATRIX)
    grad_out, new_out, new_mom_out = adamw_columns(grad_out, w_out, mom_out, LR_OUTPUT, DECAY_MATRIX)
    grad_gate_up, new_gate_up, new_mom_gate_up = adamw_columns(
        grad_gate_up, w_gate_up, mom_gate_up, LR_MATRIX, DECAY_MATRIX
    )
    grad_down, new_down, new_mom_down = adamw_columns(
        grad_down, w_down, mom_down, LR_MATRIX, DECAY_MATRIX
    )
    return (
        output,
        grad_hidden,
        grad_gains,
        grad_qkv,
        grad_out,
        grad_gate_up,
        grad_down,
        new_gains,
        new_qkv,
        new_out,
        new_gate_up,
        new_down,
        new_mom_gains,
        new_mom_qkv,
        new_mom_out,
        new_mom_gate_up,
        new_mom_down,
    )


def solution(mesh):
    shape = dict(mesh.shape)
    pair = 2 if shape["ctx"] * 2 <= KV and shape["fsdp"] % 2 == 0 else 1
    sizes = {"dp": shape["dp"], "ctx": shape["ctx"], "x": shape["fsdp"] // pair, "core": pair}
    finer = Mesh(mesh.devices.reshape(tuple(sizes.values())), tuple(sizes))
    tokens = P(("dp", "x", "core"), "ctx", None)
    everyone = ("dp", "ctx", "x", "core")
    rows, gains = P(everyone, None), P(None, everyone)
    row_moments, gain_moments = P(None, everyone, None), P(None, None, everyone)
    weights = (gains, rows, rows, rows, rows)
    moments = (gain_moments, row_moments, row_moments, row_moments, row_moments)
    return jax.shard_map(
        functools.partial(shards, sizes),
        mesh=finer,
        in_specs=(tokens, tokens, P()) + weights + moments,
        out_specs=(tokens, tokens) + weights + weights + moments,
        check_vma=False,
    )
```

```python
import functools
import math

import jax
import jax.numpy as jnp
from jax import lax
from jax.experimental import pallas as pl
from jax.experimental.pallas import tpu as pltpu
from jax.sharding import Mesh
from jax.sharding import PartitionSpec as P

MESH = pl.DeviceIdType.MESH
BF = jnp.bfloat16
F32 = jnp.float32
H = 32
KV = 8
HD = 64
FF = 8192


EPS_NORM = 1e-05
NEG_FILL = -1000000000.0
THETA = 500000.0
BETA_ONE = 0.9
BETA_TWO = 0.95
ADAM_EPS = 1e-08
DECAY_MATRIX = 0.1
LR_MATRIX = 0.01
LR_OUTPUT = 0.06
LR_GAIN = 0.3


def rope_table(positions):
    half_dim = HD // 2
    index_row = jnp.arange(half_dim, dtype=jnp.float32)
    frequency = jnp.exp(-(2.0 * index_row / HD) * math.log(THETA))
    wavelen = 2.0 * math.pi / frequency
    smooth = (8192.0 / wavelen - 1.0) / 3.0
    scaled = jnp.where(
        wavelen < 2048.0,
        frequency,
        jnp.where(
            wavelen > 8192.0,
            frequency / 32.0,
            (1.0 - smooth) * frequency / 32.0 + smooth * frequency,
        ),
    )
    angles = positions.astype(jnp.float32)[:, None] * scaled[None, :]
    cosine = jnp.cos(angles)
    sine_part = jnp.sin(angles)
    return (jnp.concatenate([cosine, cosine], 1), jnp.concatenate([sine_part, sine_part], 1))


def adamw(weight, gradient, states, step_rate, decay_rate):
    first_mom = BETA_ONE * states[0] + (1.0 - BETA_ONE) * gradient
    root_mom = jnp.sqrt(BETA_TWO * states[1] * states[1] + (1.0 - BETA_TWO) * gradient * gradient)
    first_hat = first_mom / (1.0 - BETA_ONE**3)
    root_hat = root_mom / math.sqrt(1.0 - BETA_TWO**3)
    updated = weight - step_rate * (first_hat / (root_hat + ADAM_EPS) + decay_rate * weight)
    return (updated, jnp.stack([first_mom, root_mom]))


def contract_rows(left_arr, right_arr):
    return lax.dot_general(
        left_arr, right_arr, (((0,), (0,)), ((), ())), preferred_element_type=jnp.float32
    )


def contract_cols(left_arr, right_arr):
    return lax.dot_general(
        left_arr, right_arr, (((1,), (1,)), ((), ())), preferred_element_type=jnp.float32
    )


def wrap(value, size):
    return lax.rem(value + size, size)


def remote(src, dst, send_sem, recv_sem, **where):
    return pltpu.make_async_remote_copy(
        src_ref=src,
        dst_ref=dst,
        send_sem=send_sem,
        recv_sem=recv_sem,
        device_id=where,
        device_id_type=MESH,
    )


def greet(places):
    barrier = pltpu.get_barrier_semaphore()
    for where in places:
        pl.semaphore_signal(barrier, inc=1, device_id=where, device_id_type=MESH)
    pl.semaphore_wait(barrier, len(places))


def greet_line(line, pair):
    barrier = pltpu.get_barrier_semaphore()
    here = lax.axis_index("ctx")

    @pl.when(here > 0)
    def _():
        pl.semaphore_signal(barrier, inc=1, device_id={"ctx": here - 1}, device_id_type=MESH)

    @pl.when(here < line - 1)
    def _():
        pl.semaphore_signal(barrier, inc=1, device_id={"ctx": here + 1}, device_id_type=MESH)

    if pair > 1:
        pl.semaphore_signal(
            barrier, inc=1, device_id={"core": 1 - lax.axis_index("core")}, device_id_type=MESH
        )
    ends = (here == 0).astype(jnp.int32) + (here == line - 1).astype(jnp.int32)
    pl.semaphore_wait(barrier, 2 - ends + (1 if pair > 1 else 0))


class Travel:
    @staticmethod
    def sems(many, line):
        return [pltpu.SemaphoreType.DMA((many,))] + [pltpu.SemaphoreType.DMA((many, 2, line))] * 4

    def __init__(self, line, pair, ins, outs, own_sem, line_send, line_recv, core_send, core_recv):
        self.line, self.pair, self.ins, self.outs = line, pair, ins, outs
        self.own_sem, self.line_sems, self.core_sems = own_sem, (line_send, line_recv), (core_send, core_recv)
        self.here = lax.axis_index("ctx")
        self.core = lax.axis_index("core")

    def block(self, way, step):
        return self.here - 1 - step if way == 0 else self.here + 1 + step

    def copy(self, sems, at, source, place, **where):
        return remote(place if source is None else source, place, sems[0].at[at], sems[1].at[at], **where)

    def hop(self, item, way, step, source=None):
        place = self.outs[item](self.core, self.block(way, step - 1))
        target = self.here + 1 if way == 0 else self.here - 1
        return self.copy(self.line_sems, (item, way, step), source, place, ctx=target)

    def arrived(self, item, way, step):
        place = self.outs[item](self.core, self.block(way, step))
        return self.copy(self.line_sems, (item, way, step), None, place, ctx=self.here)

    def share(self, item, way, step, source=None):
        place = self.outs[item](self.core, self.block(way, step))
        return self.copy(self.core_sems, (item, way, step + 1), source, place, core=1 - self.core)

    def shared(self, item, way, step):
        place = self.outs[item](1 - self.core, self.block(way, step))
        return self.copy(self.core_sems, (item, way, step + 1), None, place, core=1 - self.core)

    def own(self, item):
        place = self.outs[item](self.core, self.here)
        return pltpu.make_async_copy(self.ins[item], place, self.own_sem.at[item])

    def sends(self, way):
        return self.here < self.line - 1 if way == 0 else self.here > 0

    def has(self, way, step):
        return self.block(way, step) >= 0 if way == 0 else self.block(way, step) <= self.line - 1

    def begin(self):
        for item in range(len(self.ins)):
            for way in range(2):

                @pl.when(self.sends(way))
                def _(item=item, way=way):
                    self.hop(item, way, 0, self.ins[item]).start()

            if self.pair > 1:
                self.share(item, 0, -1, self.ins[item]).start()
            if self.ins[item] is not None:
                self.own(item).start()

    def step(self, step):
        for item in range(len(self.ins)):
            for way in range(2):

                @pl.when(self.has(way, step))
                def _(item=item, way=way):
                    self.arrived(item, way, step).wait_recv()
                    if step + 1 < self.line - 1:

                        @pl.when(self.sends(way))
                        def _():
                            self.hop(item, way, step + 1).start()

                    if self.pair > 1:
                        self.share(item, way, step).start()

    def end(self):
        for item in range(len(self.ins)):
            if self.ins[item] is not None:
                self.own(item).wait()
            if self.pair > 1:
                self.share(item, 0, -1, self.ins[item]).wait_send()
                self.shared(item, 0, -1).wait_recv()
            for way in range(2):

                @pl.when(self.sends(way))
                def _(item=item, way=way):
                    self.hop(item, way, 0, self.ins[item]).wait_send()

                for step in range(self.line - 1):

                    @pl.when(self.has(way, step))
                    def _(item=item, way=way, step=step):
                        if step + 1 < self.line - 1:

                            @pl.when(self.sends(way))
                            def _():
                                self.hop(item, way, step + 1).wait_send()

                        if self.pair > 1:
                            self.share(item, way, step).wait_send()
                            self.shared(item, way, step).wait_recv()


def add_rows(rows, out_ref, *parts):
    def one(index, carry):
        at = pl.ds(pl.multiple_of(index * 16, 16), 16)
        total = parts[0][at, :].astype(F32)
        for part in parts[1:]:
            total = total + part[at, :].astype(F32)
        out_ref[at, :] = total.astype(out_ref.dtype)
        return carry

    lax.fori_loop(0, rows // 16, one, 0)


class Reduce:
    @staticmethod
    def sems(*outer):
        dma = pltpu.SemaphoreType.DMA
        return lambda line: [dma(outer), dma(outer), dma(outer + (2, line)), dma(outer + (2, line))]

    @staticmethod
    def room(line, pair, rows, columns, *outer):
        return [
            pltpu.VMEM(outer + (pair, line, rows, columns), BF),
            pltpu.VMEM(outer + (line, rows, columns), BF),
            pltpu.VMEM(outer + (line + 1, rows, columns), BF),
        ]

    def __init__(self, line, pair, part, near, landed, core_send, core_recv, line_send, line_recv, at):
        self.line, self.pair, self.at = line, pair, at
        self.part, self.near, self.landed = part, near, landed
        self.core_sems, self.line_sems = (core_send, core_recv), (line_send, line_recv)
        self.here, self.core = lax.axis_index("ctx"), lax.axis_index("core")
        self.rows = part.shape[-2]

    def mine(self, block):
        return self.part.at[self.at + (self.core, block)]

    def across(self):
        return remote(
            self.part.at[self.at + (1 - self.core,)],
            self.near.at[self.at],
            self.core_sems[0].at[self.at],
            self.core_sems[1].at[self.at],
            core=1 - self.core,
        )

    def slot(self, way, block):
        return self.landed.at[self.at + (block + 1 if way == 0 else block,)]

    def onward(self, way, block, here):
        index = self.at + (way, block)
        return remote(
            self.mine(block),
            self.slot(way, block),
            self.line_sems[0].at[index],
            self.line_sems[1].at[index],
            ctx=here + 1 if way == 0 else here - 1,
        )

    def begin(self):
        if self.pair > 1:
            self.across().start()

    def settle(self):
        if self.pair > 1:
            self.across().wait_recv()

    def terms(self, block):
        return [self.mine(block)] + ([self.near.at[self.at + (block,)]] if self.pair > 1 else [])

    def relay(self, way, block, here):
        @pl.when(self.here == here)
        def _():
            terms = self.terms(block)
            if here != (0 if way == 0 else self.line - 1):
                self.onward(way, block, here).wait_recv()
                terms.append(self.slot(way, block))
            if len(terms) > 1:
                add_rows(self.rows, self.mine(block), *terms)
            self.onward(way, block, here).start()

    def finish(self, here, total_ref):
        @pl.when(self.here == here)
        def _():
            terms = self.terms(here)
            for way, has in ((0, here > 0), (1, here < self.line - 1)):
                if has:
                    self.onward(way, here, here).wait_recv()
                    terms.append(self.slot(way, here))
            add_rows(self.rows, total_ref, *terms)

    def drain(self):
        if self.pair > 1:
            self.across().wait_send()
        for here in range(self.line):

            @pl.when(self.here == here)
            def _(here=here):
                for block in range(self.line):
                    if block != here:
                        self.onward(0 if block > here else 1, block, here).wait_send()

    def plan(self, start, total_ref, after):
        ends, steps = self.line - 1, [(start, self.begin), (start + LAG, self.settle)]
        for way in range(2):
            for block in range(self.line):
                for here in range(self.line):
                    if here < block if way == 0 else here > block:
                        wait = ends - block if way == 0 else block
                        depth = here if way == 0 else ends - here
                        when = start + LAG + wait * SEND + depth * HOP
                        steps.append((when, functools.partial(self.relay, way, block, here)))
        finish = start + LAG + ends * HOP + 0.5
        for here in range(self.line):
            steps.append((finish, functools.partial(self.finish, here, total_ref)))
        steps.append((finish, after))
        return steps, finish


SEND, HOP, LAG = 3.0, 4.5, 2.5


def run_steps(steps):
    for _, step in sorted(steps, key=lambda item: item[0]):
        step()


def middle_kernel(line, pair, chunks, *refs):
    heads_ref, low_ref, high_ref, hidden_ref, cot_ref, gain_ref = refs[:6]
    output_ref, grad_mid_ref, gain_grad_ref, branch_ref, entry_ref, cots_ref, act_ref, dgu_ref = refs[6:14]
    out_w, ffn_w, part, near, landed, total, middle, branch, load_sem = refs[14:23]
    reduce_sems, travel_sems = refs[23:27], refs[27:]
    width = hidden_ref.shape[1]
    rows = part.shape[-2]
    tokens = pair * line * rows
    query_cols = out_w.shape[1]
    units = ffn_w.shape[1] // 3
    core, here = lax.axis_index("core"), lax.axis_index("ctx")
    first_col = low_ref.shape[1] - 128 - query_cols
    loads = [
        pltpu.make_async_copy(low_ref.at[:, pl.ds(first_col, query_cols)], out_w, load_sem.at[0]),
        pltpu.make_async_copy(high_ref, ffn_w, load_sem.at[1]),
    ]
    for load in loads:
        load.start()
    greet_line(line, pair)
    steps = []
    sums, travels = [], []

    def chunk_rows(chunk):
        return slice(chunk * rows, (chunk + 1) * rows)

    def reducer(kind, chunk):
        one = Reduce(line, pair, part, near, landed, *reduce_sems, (kind, chunk))
        sums.append(one)
        return one

    def traveller(kind, chunk, source, place, start):
        one = Travel(line, pair, [source], [place], *[sem.at[kind, chunk] for sem in travel_sems])
        travels.append(one)
        steps.append((start, one.begin))
        for step in range(line - 1):
            steps.append((start + (step + 1) * HOP, functools.partial(one.step, step)))
        finish = start + line * HOP - 1.0
        steps.append((finish, one.end))
        return finish

    def product(chunk):
        mine = heads_ref[:, :, chunk_rows(chunk), :].reshape(tokens, query_cols)

        @pl.loop(0, width // 512)
        def _(index):
            at = pl.ds(pl.multiple_of(index * 512, 512), 512)
            term = contract_cols(mine, out_w[at, :]).astype(BF)
            part[0, chunk, :, :, :, at] = term.reshape(pair, line, rows, 512)

    def norm_rows(chunk):
        mid = hidden_ref[chunk_rows(chunk), :].astype(F32) + total[...]
        middle[chunk_rows(chunk), :] = mid
        inverse = lax.rsqrt(jnp.mean(mid * mid, -1, keepdims=True) + EPS_NORM)
        entry_ref[chunk, core, here] = (mid * inverse * gain_ref[...]).astype(BF)

    def units_part(chunk, index, count):
        size = units // count
        entry = entry_ref[chunk].reshape(tokens, width)
        low, high = index * size, (index + 1) * size
        gate = dot(entry, ffn_w[:, low:high])
        up = dot(entry, ffn_w[:, units + low : units + high])
        grad_act = dot(cots_ref[chunk].reshape(tokens, width), ffn_w[:, 2 * units + low : 2 * units + high])
        sigmoid = 1.0 / (1.0 + jnp.exp(-gate))
        silu = gate * sigmoid
        act_ref[chunk, :, low:high] = (silu * up).astype(BF)
        dgu_ref[chunk, :, low:high] = (grad_act * up * sigmoid * (1.0 + gate * (1.0 - sigmoid))).astype(BF)
        dgu_ref[chunk, :, units + low : units + high] = (grad_act * silu).astype(BF)

    def back_part(chunk, index, count):
        size = width // count
        at = slice(index * size, (index + 1) * size)
        term = contract_cols(dgu_ref[chunk], ffn_w[at, : 2 * units]).astype(BF)
        part[1, chunk, :, :, :, at] = term.reshape(pair, line, rows, size)

    def down_part(chunk, index, count):
        size = width // count
        at = slice(index * size, (index + 1) * size)
        term = contract_cols(act_ref[chunk], ffn_w[at, 2 * units :]).astype(BF)
        part[2, chunk, :, :, :, at] = term.reshape(pair, line, rows, size)

    def norm_rows_back(chunk):
        mid = middle[chunk_rows(chunk), :]
        inverse = lax.rsqrt(jnp.mean(mid * mid, -1, keepdims=True) + EPS_NORM)
        normed = mid * inverse
        grad_entry = total[...]
        gain_term = jnp.sum(grad_entry * normed, 0, keepdims=True)
        if chunk == 0:
            gain_grad_ref[...] = gain_term
        else:
            gain_grad_ref[...] += gain_term
        grad_normed = grad_entry * gain_ref[...]
        grad_rows = inverse * (
            grad_normed - normed * jnp.mean(grad_normed * normed, -1, keepdims=True)
        )
        grad_mid = cot_ref[chunk_rows(chunk), :].astype(F32) + grad_rows
        grad_mid_ref[chunk_rows(chunk), :] = grad_mid
        branch[chunk] = grad_mid.astype(BF)

    def write_output(chunk):
        output_ref[chunk_rows(chunk), :] = (middle[chunk_rows(chunk), :] + total[...]).astype(BF)

    span = (line - 1) * SEND
    ready_ffn = ready_back = 0.0
    starts = []
    steps.append((0.0, loads[0].wait))
    for chunk in range(chunks):
        cot_done = traveller(
            0, chunk, cot_ref.at[chunk_rows(chunk)], lambda c, z, k=chunk: cots_ref.at[k, c, z], chunk * span
        )
        begin = 1.0 + chunk * span
        steps.append((begin - 0.5, functools.partial(product, chunk)))
        more, finish = reducer(0, chunk).plan(begin, total, functools.partial(norm_rows, chunk))
        steps += more
        arrived = traveller(1, chunk, None, lambda c, z, k=chunk: entry_ref.at[k, c, z], finish)
        begin = max(arrived, cot_done, ready_ffn) + 0.1
        if chunk == 0:
            steps.append((begin, loads[1].wait))
        count = 4
        for index in range(count):
            steps.append((begin + index, functools.partial(units_part, chunk, index, count)))
        for index in range(count):
            steps.append((begin + 4 + 0.8 * index, functools.partial(back_part, chunk, index, count)))
        for index in range(count):
            steps.append((begin + 7.3 + 0.5 * index, functools.partial(down_part, chunk, index, count)))
        ready_ffn = begin + 9.5
        begin = max(begin + 7.25, ready_back)
        ready_back = begin + span
        more, finish = reducer(1, chunk).plan(begin, total, functools.partial(norm_rows_back, chunk))
        steps += more
        traveller(
            2,
            chunk,
            branch.at[chunk],
            lambda c, z, k=chunk: branch_ref.at[c, z, pl.ds(k * rows, rows)],
            finish,
        )
    for chunk in range(chunks):
        begin = ready_back + chunk * span
        steps += reducer(2, chunk).plan(begin, total, functools.partial(write_output, chunk))[0]
    run_steps(steps)
    for one in sums:
        one.drain()


def middle_rows(sizes, collective_id, heads, low, high, hidden, cot, gain):
    line, pair = sizes["ctx"], sizes["core"]
    rows, width = hidden.shape
    chunks = 4
    step = rows // chunks
    tokens = pair * line * step
    units = high.shape[1] // 3
    query_cols = heads.shape[1]
    any_spec = pl.BlockSpec(memory_space=pl.ANY)
    vmem = pl.BlockSpec(memory_space=pltpu.VMEM)
    shape = jax.ShapeDtypeStruct
    dma = pltpu.SemaphoreType.DMA
    outs = pl.pallas_call(
        functools.partial(middle_kernel, line, pair, chunks),
        out_shape=[
            shape((rows, width), BF),
            shape((rows, width), F32),
            shape((1, width), F32),
            shape((pair, line, rows, width), BF),
            shape((chunks, pair, line, step, width), BF),
            shape((chunks, pair, line, step, width), BF),
            shape((chunks, tokens, units), BF),
            shape((chunks, tokens, 2 * units), BF),
        ],
        in_specs=[vmem, any_spec, any_spec, vmem, vmem, vmem],
        out_specs=[vmem, vmem, vmem, any_spec, vmem, vmem, vmem, vmem],
        scratch_shapes=[
            pltpu.VMEM((width, query_cols), BF),
            pltpu.VMEM(high.shape, BF),
            *Reduce.room(line, pair, step, width, 3, chunks),
            pltpu.VMEM((step, width), F32),
            pltpu.VMEM((rows, width), F32),
            pltpu.VMEM((chunks, step, width), BF),
            dma((2,)),
            *Reduce.sems(3, chunks)(line),
            dma((3, chunks, 1)),
            *[dma((3, chunks, 1, 2, line))] * 4,
        ],
        compiler_params=pltpu.CompilerParams(
            collective_id=collective_id, has_side_effects=True, vmem_limit_bytes=63 * 2**20
        ),
    )(heads.reshape(pair, line, rows, query_cols), low, high, hidden, cot, gain)
    return list(outs[:3]) + [out.reshape(-1, out.shape[-1]) for out in outs[3:]]


def blocks_in_order(line, pair):
    away = sorted(range(line), key=lambda d: min(d, line - d))
    return [(dz, dc) for dz in away for dc in range(pair)]


def greet_all(sizes):
    names = ("dp", "ctx", "x", "core")
    at = {name: lax.axis_index(name) for name in names}
    places = []
    for dz, dc in blocks_in_order(sizes["ctx"], sizes["core"]):
        if dz or dc:
            places.append(
                {"ctx": wrap(at["ctx"] + dz, sizes["ctx"]), "core": wrap(at["core"] + dc, sizes["core"])}
            )
    for name in ("dp", "x"):
        for step in range(1, sizes[name]):
            places.append({name: wrap(at[name] + step, sizes[name])})
    greet(places)


def pack_member(refs, member, rows, group, tall, wide):
    qkv_ref, out_ref, gate_up_ref, down_ref, gain_ref = refs
    heads, keys, units = H * HD // group, KV * HD // group, FF // group
    low = lambda values: values.astype(BF)
    tall[member, :, :heads] = low(qkv_ref[:, member * heads : (member + 1) * heads])
    key_at, value_at = H * HD + member * keys, (H + KV) * HD + member * keys
    tall[member, :, heads : heads + 2 * keys] = low(
        jnp.concatenate(
            [qkv_ref[:, key_at : key_at + keys], qkv_ref[:, value_at : value_at + keys]], 1
        )
    )
    tall[member, :, heads + 2 * keys : 2 * heads + 2 * keys] = low(
        out_ref[:, member * heads : (member + 1) * heads]
    )
    tall[member, :, 2 * heads + 2 * keys :] = low(gain_ref[...])
    wide[member, :, :units] = low(gate_up_ref[:, member * units : (member + 1) * units])
    wide[member, :, units : 2 * units] = low(
        gate_up_ref[:, FF + member * units : FF + (member + 1) * units]
    )
    wide[member, :, 2 * units :] = low(down_ref[:, member * units : (member + 1) * units])


def spread_kernel(sizes, *refs):
    weight_refs, hidden_ref = refs[:5], refs[5]
    outs, hidden_out = refs[6:8], refs[8]
    packs = refs[9:11]
    own_sem, f_send, f_recv, a_send, a_recv, b_send, b_recv = refs[11:18]
    travel_sems = refs[18:]
    line, pair = sizes["ctx"], sizes["core"]
    group = line * pair
    rows = packs[0].shape[1]
    at = {name: lax.axis_index(name) for name in ("dp", "ctx", "x", "core")}
    greet_all(sizes)
    order = blocks_in_order(line, pair)
    me = at["ctx"] * pair + at["core"]
    travel = Travel(line, pair, [hidden_ref], [lambda c, z: hidden_out.at[c, z]], *travel_sems)
    travel.begin()

    def first(kind, index):
        dz, dc = order[index]
        z, c = wrap(at["ctx"] + dz, line), wrap(at["core"] + dc, pair)
        return remote(
            packs[kind].at[z * pair + c],
            outs[kind].at[at["dp"], at["ctx"], at["x"], at["core"]],
            f_send.at[kind, index],
            f_recv.at[kind, index],
            ctx=z,
            core=c,
        )

    def place(kind, index, moved):
        dz, dc = order[index]
        z, c = wrap(at["ctx"] - dz, line), wrap(at["core"] - dc, pair)
        spot = {name: wrap(at[name] - moved.get(name, 0), sizes[name]) for name in ("dp", "x")}
        return outs[kind].at[spot["dp"], z, spot["x"], c]

    def came(kind, index):
        spot = place(kind, index, {})
        return remote(spot, spot, f_send.at[kind, index], f_recv.at[kind, index], core=at["core"])

    def axes(index):
        dz, dc = order[index]
        return ("x", "dp") if (dz + dc) % 2 == 0 else ("dp", "x")

    def hop_one(kind, index, step):
        name = axes(index)[0]
        spot = place(kind, index, {})
        return remote(
            spot,
            spot,
            a_send.at[kind, index, step],
            a_recv.at[kind, index, step],
            **{name: wrap(at[name] + step, sizes[name])},
        )

    def one_came(kind, index, step):
        name = axes(index)[0]
        spot = place(kind, index, {name: step})
        return remote(
            spot, spot, a_send.at[kind, index, step], a_recv.at[kind, index, step], core=at["core"]
        )

    def hop_two(kind, index, step, far):
        name, other = axes(index)
        spot = place(kind, index, {name: step})
        return remote(
            spot,
            spot,
            b_send.at[kind, index, step, far],
            b_recv.at[kind, index, step, far],
            **{other: wrap(at[other] + far, sizes[other])},
        )

    def two_came(kind, index, step, far):
        name, other = axes(index)
        spot = place(kind, index, {name: step, other: far})
        return remote(
            spot,
            spot,
            b_send.at[kind, index, step, far],
            b_recv.at[kind, index, step, far],
            core=at["core"],
        )

    def own(kind):
        return pltpu.make_async_copy(
            packs[kind].at[me],
            outs[kind].at[at["dp"], at["ctx"], at["x"], at["core"]],
            own_sem.at[kind],
        )

    def onward(kind, index):
        name, other = axes(index)
        for step in range(1, sizes[name]):
            hop_one(kind, index, step).start()
        for far in range(1, sizes[other]):
            hop_two(kind, index, 0, far).start()

    def onward_two(kind, index):
        name, other = axes(index)
        for step in range(1, sizes[name]):
            one_came(kind, index, step).wait_recv()
            for far in range(1, sizes[other]):
                hop_two(kind, index, step, far).start()

    for member in range(group):
        pack_member(weight_refs, member, rows, group, *packs)
    ahead, late = 3, 1
    for kind in range(2):
        own(kind).start()
        for index in range(1, 1 + ahead):
            first(kind, index).start()
    for tick in range(group + late):
        if tick < group:
            for kind in range(2):
                if tick == 0:
                    own(kind).wait()
                else:
                    came(kind, tick).wait_recv()
                onward(kind, tick)
                if 1 + ahead <= tick + ahead < group and tick:
                    first(kind, tick + ahead).start()
        if tick % 2 == 1 and tick // 2 < line - 1:
            travel.step(tick // 2)
        if tick >= late:
            for kind in range(2):
                onward_two(kind, tick - late)
    travel.end()
    for kind in range(2):
        for index in range(group):
            if index:
                first(kind, index).wait_send()
            name, other = axes(index)
            for step in range(sizes[name]):
                if step:
                    hop_one(kind, index, step).wait_send()
                for far in range(1, sizes[other]):
                    hop_two(kind, index, step, far).wait_send()
                    two_came(kind, index, step, far).wait_recv()


def spread_weights(sizes, collective_id, hidden, gains, *weights):
    line, pair = sizes["ctx"], sizes["core"]
    group = line * pair
    rows = weights[0].shape[0]
    steps = max(sizes["dp"], sizes["x"])
    tall, wide = (2 * H * HD + 2 * KV * HD) // group + 128, 3 * FF // group
    gain_tile = jnp.pad(gains.T, ((0, 0), (0, 126)))
    any_spec = pl.BlockSpec(memory_space=pl.ANY)
    vmem = pl.BlockSpec(memory_space=pltpu.VMEM)
    everyone = (sizes["dp"], line, sizes["x"], pair, rows)
    low, high, tokens = pl.pallas_call(
        functools.partial(spread_kernel, sizes),
        out_shape=[
            jax.ShapeDtypeStruct(everyone + (tall,), BF),
            jax.ShapeDtypeStruct(everyone + (wide,), BF),
            jax.ShapeDtypeStruct((pair, line) + hidden.shape, BF),
        ],
        in_specs=[vmem] * 5 + [any_spec],
        out_specs=[any_spec] * 3,
        scratch_shapes=[
            pltpu.VMEM((group, rows, tall), BF),
            pltpu.VMEM((group, rows, wide), BF),
            pltpu.SemaphoreType.DMA((2,)),
            pltpu.SemaphoreType.DMA((2, group)),
            pltpu.SemaphoreType.DMA((2, group)),
            pltpu.SemaphoreType.DMA((2, group, steps)),
            pltpu.SemaphoreType.DMA((2, group, steps)),
            pltpu.SemaphoreType.DMA((2, group, steps, steps)),
            pltpu.SemaphoreType.DMA((2, group, steps, steps)),
            *Travel.sems(1, line),
        ],
        compiler_params=pltpu.CompilerParams(
            collective_id=collective_id, has_side_effects=True, vmem_limit_bytes=40 * 2**20
        ),
    )(*weights, gain_tile, hidden)
    return low.reshape(-1, tall), high.reshape(-1, wide), tokens.reshape(-1, hidden.shape[1])


class Collect:
    AXES = (("dp", "x"), ("x", "dp"))

    @staticmethod
    def room(sizes, rows, width):
        room = [pltpu.VMEM((sizes["ctx"], sizes["dp"], sizes["x"], sizes["core"], rows, width), BF)]
        for parity, (name, other) in enumerate(Collect.AXES):
            count = sum((dz + dc) % 2 == parity for dz, dc in blocks_in_order(sizes["ctx"], sizes["core"]))
            room.append(pltpu.VMEM((max(1, count), (sizes[name] - 1) * sizes[other], rows, width), BF))
            room.append(pltpu.VMEM((max(1, count), sizes[other] - 1, rows, width), BF))
        return room

    @staticmethod
    def sems(sizes, pieces):
        dma = pltpu.SemaphoreType.DMA
        group, steps = sizes["ctx"] * sizes["core"], max(sizes["dp"], sizes["x"])
        return (
            [dma((pieces,))]
            + [dma((group, steps, steps))] * 2
            + [dma((group, steps))] * 2
            + [dma((group, pieces))] * 2
        )

    def __init__(self, sizes, widths, pieces, room, sems):
        self.sizes, self.widths, self.pieces = sizes, widths, pieces
        self.terms = room[0]
        self.near, self.far_in = room[1::2], room[2::2]
        self.own_sem, *rest = sems
        self.a_sems, self.b_sems, self.f_sems = rest[0:2], rest[2:4], rest[4:6]
        self.line, self.pair = sizes["ctx"], sizes["core"]
        self.rows = self.terms.shape[-2]
        self.at = {name: lax.axis_index(name) for name in ("dp", "ctx", "x", "core")}
        self.me = self.at["ctx"] * self.pair + self.at["core"]
        self.away = sorted(range(self.line), key=lambda d: -min(d, self.line - d))
        self.order = [(dz, dc) for dz in self.away for dc in range(self.pair)]

    def spot_of(self, index, sign=1):
        dz, dc = self.order[index]
        return wrap(self.at["ctx"] + sign * dz, self.line), wrap(self.at["core"] + sign * dc, self.pair)

    def parity(self, index):
        return sum(self.order[index]) % 2

    def axes(self, index):
        return self.AXES[self.parity(index)]

    def slot(self, index):
        return sum(self.parity(before) == self.parity(index) for before in range(index))

    def indices(self, tick):
        return range(tick * self.pair, (tick + 1) * self.pair)

    def lanes(self, tick, dp):
        across = self.sizes["x"] * self.pair * self.rows
        z = wrap(self.at["ctx"] + self.away[tick], self.line)
        return pl.ds(pl.multiple_of((dp * self.line + z) * across, 128), across)

    def multiply(self, tick, lefts, rights):
        start = 0
        for left, right, width in zip(lefts, rights, self.widths):
            step = math.gcd(width, 512)

            @pl.loop(0, self.sizes["dp"])
            def _(dp, left=left, right=right, start=start, width=width, step=step):
                left_t = left[dp].T

                @pl.loop(0, width // step)
                def _(part):
                    columns = pl.ds(pl.multiple_of(part * step, 128), step)
                    into = pl.ds(pl.multiple_of(start + part * step, 128), step)
                    product = dot(left_t, right[:, columns]).astype(BF)
                    for x in range(self.sizes["x"]):
                        for core in range(self.pair):
                            low = (x * self.pair + core) * self.rows
                            self.terms[tick, dp, x, core, :, into] = product[low : low + self.rows]

            start += width

    def block_terms(self, index, first_at, other_at):
        name, other = self.axes(index)
        spot = {name: first_at, other: other_at}
        return self.terms.at[index // self.pair, spot["dp"], spot["x"], self.spot_of(index)[1]]

    def landing(self, index, step, place):
        at = (step - 1) * self.sizes[self.axes(index)[1]] + place
        return self.near[self.parity(index)].at[self.slot(index), at]

    def far_landing(self, index, far):
        return self.far_in[self.parity(index)].at[self.slot(index), far - 1]

    def hop_one(self, index, step, place):
        name = self.axes(index)[0]
        to = wrap(self.at[name] + step, self.sizes[name])
        sems = [sem.at[index, step, place] for sem in self.a_sems]
        return remote(
            self.block_terms(index, to, place), self.landing(index, step, place), *sems, **{name: to}
        )

    def hop_two(self, index, far):
        name, other = self.axes(index)
        to = wrap(self.at[other] + far, self.sizes[other])
        sems = [sem.at[index, far] for sem in self.b_sems]
        return remote(
            self.block_terms(index, self.at[name], to), self.far_landing(index, far), *sems, **{other: to}
        )

    def done(self, index):
        name, other = self.axes(index)
        return self.block_terms(index, self.at[name], self.at[other])

    def stays(self, index):
        return self.order[index] == (0, 0)

    def piece_at(self, piece, member):
        out, width, _ = self.pieces[piece]
        return out.at[:, pl.ds(pl.multiple_of(member * width, 128), width)]

    def last(self, index, piece):
        z, c = self.spot_of(index)
        _, width, offset = self.pieces[piece]
        source = self.done(index).at[:, pl.ds(offset, width)]
        target = self.piece_at(piece, self.me)
        if self.stays(index):
            return pltpu.make_async_copy(source, target, self.own_sem.at[piece])
        return remote(source, target, *[sem.at[index, piece] for sem in self.f_sems], ctx=z, core=c)

    def last_came(self, index, piece):
        z, c = self.spot_of(index, -1)
        spot = self.piece_at(piece, z * self.pair + c)
        sems = [sem.at[index, piece] for sem in self.f_sems]
        return remote(spot, spot, *sems, core=self.at["core"])

    def places(self, index):
        other = self.axes(index)[1]
        size = self.sizes[other]
        return [(far, wrap(self.at[other] + far, size)) for far in list(range(1, size)) + [0]]

    def send_one(self, tick):
        for index in self.indices(tick):
            for _, place in self.places(index):
                for step in range(1, self.sizes[self.axes(index)[0]]):
                    self.hop_one(index, step, place).start()

    def sum_one(self, tick):
        for index in self.indices(tick):
            name = self.axes(index)[0]
            for far, place in self.places(index):
                steps = range(1, self.sizes[name])
                for step in steps:
                    self.hop_one(index, step, place).wait_recv()
                kept = self.block_terms(index, self.at[name], place)
                add_rows(self.rows, kept, kept, *[self.landing(index, step, place) for step in steps])
                if far:
                    self.hop_two(index, far).start()

    def sum_two(self, tick):
        for index in self.indices(tick):
            fars = range(1, self.sizes[self.axes(index)[1]])
            for far in fars:
                self.hop_two(index, far).wait_recv()
            done = self.done(index)
            add_rows(self.rows, done, done, *[self.far_landing(index, far) for far in fars])
            for piece in range(len(self.pieces)):
                self.last(index, piece).start()

    def drain(self):
        for index in range(len(self.order)):
            name, other = self.axes(index)
            for step in range(1, self.sizes[name]):
                for place in range(self.sizes[other]):
                    self.hop_one(index, step, place).wait_send()
            for far in range(1, self.sizes[other]):
                self.hop_two(index, far).wait_send()
            for piece in range(len(self.pieces)):
                if self.stays(index):
                    self.last(index, piece).wait()
                else:
                    self.last(index, piece).wait_send()
                    self.last_came(index, piece).wait_recv()


def lane_index(shape):
    return lax.broadcasted_iota(jnp.int32, shape, len(shape) - 1)


def turned(values):
    half, columns = HD // 2, values.shape[1]
    ahead = pltpu.roll(values, columns - half, 1)
    behind = pltpu.roll(values, half, 1)
    return jnp.where(lane_index(values.shape) % HD < half, ahead, behind)


def only_head(values, head):
    return jnp.where(lane_index(values.shape) // HD == head, values, jnp.zeros_like(values))


def both_halves(values, head):
    wide = values.astype(F32)
    return jnp.where(lane_index(wide.shape) // HD == head, wide, pltpu.roll(wide, HD, 1)).astype(BF)


def softmax_rows(queries, keys, visible):
    scores = contract_cols(queries, keys) * HD ** (-0.5)
    scores = jnp.where(visible, scores, NEG_FILL)
    exponent = jnp.exp(scores - jnp.max(scores, -1, keepdims=True))
    return exponent / jnp.sum(exponent, -1, keepdims=True)


def query_rows(total_rows):
    return min(total_rows, 2**18 // total_rows)


def each_query_block(total_rows, heads, pos_col, pos_row):
    size = query_rows(total_rows)
    for low in range(0, total_rows, size):
        visible = pos_row[...] <= pos_col[low : low + size, :]
        for lane in range(0, heads * HD, 2 * HD):
            yield low, size, visible, lane


def attend_kernel(
    hidden_ref, low_ref, gain_ref, cos_ref, sin_ref, pos_col, pos_row, entry_ref, qkv_ref, heads_ref, qkv_w, load_sem
):
    load = pltpu.make_async_copy(low_ref.at[:, pl.ds(0, qkv_w.shape[1])], qkv_w, load_sem)
    load.start()
    tokens, total_rows = hidden_ref.shape[0], cos_ref.shape[0]
    query_cols = heads_ref.shape[1]
    step = 256
    load.wait()

    @pl.loop(0, tokens // step)
    def _(index):
        at = pl.ds(pl.multiple_of(index * step, step), step)
        table_at = pl.ds(pl.multiple_of(lax.rem(index * step, total_rows), step), step)
        rows = hidden_ref[at, :].astype(F32)
        inverse = lax.rsqrt(jnp.mean(rows * rows, -1, keepdims=True) + EPS_NORM)
        entry = (rows * inverse * gain_ref[...]).astype(BF)
        entry_ref[at, :] = entry
        projected = dot(entry, qkv_w[...])
        rotated = projected * cos_ref[table_at, :] + turned(projected) * sin_ref[table_at, :]
        qkv_ref[at, :] = rotated.astype(BF)

    @pl.loop(0, tokens // total_rows)
    def _(sequence):
        start = sequence * total_rows
        both = qkv_ref[pl.ds(pl.multiple_of(start, total_rows), total_rows), query_cols:]
        keys, values = both_halves(both, 0), both_halves(both, 1)
        for low, size, visible, lane in each_query_block(total_rows, query_cols // HD, pos_col, pos_row):
            at = pl.ds(pl.multiple_of(start + low, 128), size)
            queries = qkv_ref[at, lane : lane + 2 * HD]
            pair = [
                dot(softmax_rows(only_head(queries, head), keys, visible).astype(BF), values)
                for head in range(2)
            ]
            heads_ref[at, lane : lane + 2 * HD] = jnp.where(
                lane_index(pair[0].shape) < HD, pair[0], pair[1]
            ).astype(BF)


def attend(hidden_all, low, gain, tables):
    tokens, width = hidden_all.shape
    qkv_cols = tables[0].shape[1]
    query_cols = qkv_cols - 2 * HD
    vmem = pl.BlockSpec(memory_space=pltpu.VMEM)
    return pl.pallas_call(
        attend_kernel,
        out_shape=[
            jax.ShapeDtypeStruct((tokens, width), BF),
            jax.ShapeDtypeStruct((tokens, qkv_cols), BF),
            jax.ShapeDtypeStruct((tokens, query_cols), BF),
        ],
        in_specs=[vmem, pl.BlockSpec(memory_space=pl.ANY)] + [vmem] * 5,
        out_specs=[vmem] * 3,
        scratch_shapes=[pltpu.VMEM((width, qkv_cols), BF), pltpu.SemaphoreType.DMA],
        compiler_params=pltpu.CompilerParams(vmem_limit_bytes=56 * 2**20),
    )(hidden_all, low, gain, *tables)


class GainSum:
    @staticmethod
    def room(sizes, width):
        group = sizes["ctx"] * sizes["core"]
        return [
            pltpu.VMEM((8, width), F32),
            pltpu.VMEM((sizes["x"] - 1, 8, width), F32),
            pltpu.VMEM((sizes["dp"] - 1, 8, width), F32),
            pltpu.VMEM((group, 8, 128), F32),
        ]

    @staticmethod
    def sems(sizes):
        group = sizes["ctx"] * sizes["core"]
        counts = (sizes["x"], sizes["x"], sizes["dp"], sizes["dp"], group, group)
        return [pltpu.SemaphoreType.DMA((count,)) for count in counts]

    def __init__(self, sizes, own_rows, out_ref, room, sems):
        self.sizes, self.own_rows, self.out_ref = sizes, own_rows, out_ref
        self.mine, self.over_x, self.over_dp, self.tiles = room
        self.sems_of = {"x": sems[0:2], "dp": sems[2:4], "group": sems[4:6]}
        self.at = {name: lax.axis_index(name) for name in ("dp", "ctx", "x", "core")}
        self.order = blocks_in_order(sizes["ctx"], sizes["core"])

    def hop(self, name, step):
        into = (self.over_x if name == "x" else self.over_dp).at[step - 1]
        sems = [sem.at[step] for sem in self.sems_of[name]]
        return remote(self.mine, into, *sems, **{name: wrap(self.at[name] + step, self.sizes[name])})

    def tile(self, index):
        dz, dc = self.order[index]
        z, c = wrap(self.at["ctx"] + dz, self.sizes["ctx"]), wrap(self.at["core"] + dc, self.sizes["core"])
        place = (self.at["dp"] * self.sizes["ctx"] + z) * self.sizes["x"] + self.at["x"]
        first = (place * self.sizes["core"] + c) * self.own_rows
        source = self.mine.at[:, pl.ds(pl.multiple_of(first // 128 * 128, 128), 128)]
        sems = [sem.at[index] for sem in self.sems_of["group"]]
        if index == 0:
            return source
        return remote(source, self.tiles.at[index], *sems, ctx=z, core=c)

    def begin(self, first, second):
        self.mine[...] = jnp.zeros_like(self.mine)
        self.mine[0:1, :] = first[...]
        self.mine[1:2, :] = second[...]
        self.send("x")

    def send(self, name):
        for step in range(1, self.sizes[name]):
            self.hop(name, step).start()

    def add(self, name):
        for step in range(1, self.sizes[name]):
            self.hop(name, step).wait()
        for step in range(1, self.sizes[name]):
            self.mine[...] += (self.over_x if name == "x" else self.over_dp)[step - 1]

    def second(self):
        self.add("x")
        self.send("dp")

    def third(self):
        self.add("dp")
        for index in range(1, len(self.order)):
            self.tile(index).start()

    def end(self):
        total = self.tile(0)[...]
        for index in range(1, len(self.order)):
            self.tile(index).wait()
            total = total + self.tiles[index]
        self.out_ref[...] = total


def closing_kernel(sizes, chunks, *refs):
    (entry_two, dgu_ref, cot_ref, act_ref, entry_one, branch_ref, qkv_ref, heads_ref, low_ref) = refs[:9]
    hidden_ref, grad_mid_ref, gain_ref, gain_two_ref, cos_ref, sin_ref, pos_col, pos_row = refs[9:17]
    piece_refs, (grad_hidden_ref, gain_sum_ref) = refs[17:23], refs[23:25]
    refs = refs[1:]
    (left_slots, part, act, dqkv, heads, branch_slots, low_w, grad_heads, grad_proj, key_acc, value_acc) = refs[24:35]
    near, landed, total, load_sem, left_sem, branch_sem = refs[35:41]
    ffn_room, att_room = refs[41:46], refs[46:51]
    ffn_sems, att_sems, reduce_sems = refs[51:58], refs[58:65], refs[65:69]
    gain_grad_ref, gain_room, gain_sems = refs[69], refs[70:74], refs[74:80]
    line, pair = sizes["ctx"], sizes["core"]
    rows = part.shape[-2]
    block_rows, width = hidden_ref.shape
    tokens, total_rows = qkv_ref.shape[0], cos_ref.shape[0]
    query_cols = heads.shape[1]
    qkv_cols = dqkv.shape[1]
    loads = {
        "dgu": pltpu.make_async_copy(dgu_ref, part, load_sem.at[0]),
        "act": pltpu.make_async_copy(act_ref, act, load_sem.at[1]),
        "heads": pltpu.make_async_copy(heads_ref, heads, load_sem.at[2]),
        "low": pltpu.make_async_copy(low_ref.at[:, pl.ds(0, low_w.shape[1])], low_w, load_sem.at[3]),
    }
    names = grad_pieces(sizes)
    shift = names[3][2]
    ffn_pieces = [(ref, w, o) for ref, (_, w, o) in zip(piece_refs[:3], names[:3])]
    att_pieces = [(ref, w, o - shift) for ref, (_, w, o) in zip(piece_refs[3:], names[3:])]
    ffn = Collect(sizes, (2 * act.shape[1], act.shape[1]), ffn_pieces, ffn_room, ffn_sems)
    att = Collect(sizes, (qkv_cols, query_cols), att_pieces, att_room, att_sems)
    sums = [
        Reduce(line, pair, part, near, landed, *reduce_sems, (chunk,)) for chunk in range(chunks)
    ]
    gain_sum = GainSum(sizes, ffn.rows, gain_sum_ref, gain_room, gain_sems)

    def left_loads(turn):
        tick, slot = turn % line, turn % 2
        one, sources = (ffn, (entry_two, cot_ref)) if turn < line else (att, (entry_one, branch_ref))
        return [
            pltpu.make_async_copy(
                source.at[:, one.lanes(tick, dp)], left_slots.at[slot, item, dp], left_sem.at[slot, item, dp]
            )
            for item, source in enumerate(sources)
            for dp in range(sizes["dp"])
        ]

    def branch_load(index):
        size = branch_slots.shape[1]
        return pltpu.make_async_copy(
            branch_ref.at[pl.ds(index * size, size)], branch_slots.at[index % 2], branch_sem.at[index % 2]
        )

    for load in left_loads(0):
        load.start()
    for load in loads.values():
        load.start()
    for load in left_loads(1):
        load.start()
    greet_all(sizes)

    def multiply(turn):
        for load in left_loads(turn):
            load.wait()
        lefts = [left_slots.at[turn % 2, item] for item in range(2)]
        if turn < line:
            ffn.multiply(turn, lefts, (part_rows, act))
        else:
            att.multiply(turn - line, lefts, (dqkv, heads))
        if turn + 2 < 2 * line:
            for load in left_loads(turn + 2):
                load.start()

    class PartRows:
        def __getitem__(self, at):
            return part[:, :, :, :, at[1]].reshape(tokens, -1)

    part_rows = PartRows()

    def back_to_heads():
        loads["low"].wait()
        size = branch_slots.shape[1]
        branch_load(0).start()
        for index in range(tokens // size):
            if index + 1 < tokens // size:
                branch_load(index + 1).start()
            branch_load(index).wait()
            grad_heads[index * size : (index + 1) * size, :] = dot(
                branch_slots[index % 2], low_w[:, qkv_cols:]
            ).astype(BF)

    def attention_part(sequence, low, size, lane):
        start = sequence * total_rows
        span = slice(start, start + total_rows)
        at = slice(start + low, start + low + size)
        both = qkv_ref[span, query_cols:]
        keys, values = both_halves(both, 0), both_halves(both, 1)
        visible = pos_row[...] <= pos_col[low : low + size, :]
        queries = qkv_ref[at, lane : lane + 2 * HD]
        grads = grad_heads[at, lane : lane + 2 * HD]
        grad_queries = []
        key_term = value_term = None
        for head in range(2):
            query, grad = only_head(queries, head), only_head(grads, head)
            probability = softmax_rows(query, keys, visible)
            grad_prob = contract_cols(grad, values)
            delta = jnp.sum(probability * grad_prob, -1, keepdims=True)
            grad_scores = jnp.where(visible, probability * (grad_prob - delta), 0.0).astype(BF)
            grad_queries.append(dot(grad_scores, keys))
            key_more = contract_rows(grad_scores, query)
            value_more = contract_rows(probability.astype(BF), grad)
            key_term = key_more if key_term is None else key_term + key_more
            value_term = value_more if value_term is None else value_term + value_more
        scale = HD ** (-0.5)
        grad_proj[low : low + size, lane : lane + 2 * HD] = scale * jnp.where(
            lane_index(grad_queries[0].shape) < HD, grad_queries[0], grad_queries[1]
        )
        if low == 0 and lane == 0:
            key_acc[...] = key_term * scale
            value_acc[...] = value_term
        else:
            key_acc[...] += key_term * scale
            value_acc[...] += value_term

    def rotate_back(sequence):
        keys, values = key_acc[...], value_acc[...]
        grad_proj[:, query_cols:] = jnp.where(
            lane_index(keys.shape) < HD, keys + pltpu.roll(keys, HD, 1), values + pltpu.roll(values, HD, 1)
        )
        for low in range(0, total_rows, 256):
            size = min(256, total_rows - low)
            grads = grad_proj[low : low + size, :]
            back = grads * cos_ref[low : low + size, :] + turned(grads * sin_ref[low : low + size, :])
            at = sequence * total_rows + low
            dqkv[at : at + size, :] = back.astype(BF)

    def entry_terms(chunk):
        mine = jnp.concatenate(
            [
                dqkv[(c * line + z) * block_rows + chunk * rows : (c * line + z) * block_rows + (chunk + 1) * rows, :]
                for c in range(pair)
                for z in range(line)
            ],
            0,
        )
        for low in range(0, width, 512):
            term = contract_cols(mine, low_w[low : low + 512, :qkv_cols]).astype(BF)
            part[chunk, :, :, :, low : low + 512] = term.reshape(pair, line, rows, 512)

    def norm_rows_back(chunk):
        at = slice(chunk * rows, (chunk + 1) * rows)
        values = hidden_ref[at, :].astype(F32)
        inverse = lax.rsqrt(jnp.mean(values * values, -1, keepdims=True) + EPS_NORM)
        normed = values * inverse
        grad_entry = total[...]
        gain_term = jnp.sum(grad_entry * normed, 0, keepdims=True)
        if chunk == 0:
            gain_grad_ref[...] = gain_term
        else:
            gain_grad_ref[...] += gain_term
        grad_normed = grad_entry * gain_ref[...]
        grad_rows = inverse * (
            grad_normed - normed * jnp.mean(grad_normed * normed, -1, keepdims=True)
        )
        grad_hidden_ref[at, :] = (grad_mid_ref[at, :] + grad_rows).astype(BF)

    steps = []

    def step(time, function, *values):
        steps.append((time, functools.partial(function, *values)))

    step(0.0, loads["dgu"].wait)
    step(0.0, loads["act"].wait)
    period, before = 26.0, 24.0
    for tick in range(line):
        arrived = before + period * tick
        issued = 5.0 * (tick + 1) if tick < 2 else before + period * (tick - 2) + 0.5
        step(issued - 5.0 if tick < 2 else issued - 5.5, multiply, tick)
        step(issued, ffn.send_one, tick)
        step(arrived, ffn.sum_one, tick)
        step(arrived + 12.0, ffn.sum_two, tick)
    now = 10.5
    step(now, back_to_heads)
    now += 3.0
    for sequence in range(tokens // total_rows):
        size = query_rows(total_rows)
        for low in range(0, total_rows, size):
            for lane in range(0, query_cols, 2 * HD):
                step(now, attention_part, sequence, low, size, lane)
                now += 6.0
        step(now, rotate_back, sequence)
        now += 0.5
    now = max(now, before + period * (line - 3) + 0.6)
    step(now, loads["heads"].wait)
    for chunk in range(chunks):
        step(now + 0.5 + chunk, entry_terms, chunk)
    begin = now + 1.0
    for chunk, one in enumerate(sums):
        start = begin + chunk * (line - 1) * SEND
        more, finish = one.plan(start, total, functools.partial(norm_rows_back, chunk))
        steps += more
    step(finish + 0.2, gain_sum.begin, gain_grad_ref, gain_two_ref)
    step(finish + 4.0, gain_sum.second)
    step(finish + 8.0, gain_sum.third)
    step(finish + 12.0, gain_sum.end)
    now += 1.0 + chunks
    for tick in range(line):
        step(now + tick, multiply, line + tick)
        step(now + tick + 0.5, att.send_one, tick)
        arrived = max(now + 30.0 + 2.0 * tick, before + period * (line - 2) + 1.0 + 2.0 * tick)
        step(arrived, att.sum_one, tick)
        step(arrived + 12.5, att.sum_two, tick)
    run_steps(steps)
    for one in sums + [ffn, att]:
        one.drain()


def closing(sizes, collective_id, factors, low, hidden, grad_mid, gain, grad_gain_two, tables):
    line, pair = sizes["ctx"], sizes["core"]
    group = line * pair
    block_rows, width = hidden.shape
    tokens = block_rows * group
    chunks = 4
    rows = block_rows // chunks
    own_rows = width // (group * sizes["dp"] * sizes["x"])
    units = factors[3].shape[1]
    qkv_cols, query_cols = factors[6].shape[1], factors[7].shape[1]
    total_rows = tables[0].shape[0]
    pieces = grad_pieces(sizes)
    any_spec = pl.BlockSpec(memory_space=pl.ANY)
    vmem = pl.BlockSpec(memory_space=pltpu.VMEM)
    dma = pltpu.SemaphoreType.DMA
    shape = jax.ShapeDtypeStruct
    across = sizes["x"] * pair * own_rows
    branch_rows = 128
    part_shape = (chunks, pair, line, rows, width)
    factors = list(factors)
    factors[1] = factors[1].reshape(part_shape)
    return pl.pallas_call(
        functools.partial(closing_kernel, sizes, chunks),
        out_shape=[shape((own_rows, group * w), BF) for _, w, _ in pieces]
        + [shape((block_rows, width), BF), shape((8, 128), F32)],
        in_specs=[any_spec] * 6 + [vmem] + [any_spec] * 2 + [vmem] * 8,
        out_specs=[any_spec] * len(pieces) + [vmem] * 2,
        scratch_shapes=[
            pltpu.VMEM((2, 2, sizes["dp"], tokens, across), BF),
            pltpu.VMEM(part_shape, BF),
            pltpu.VMEM((tokens, units), BF),
            pltpu.VMEM((tokens, qkv_cols), BF),
            pltpu.VMEM((tokens, query_cols), BF),
            pltpu.VMEM((2, branch_rows, width), BF),
            pltpu.VMEM((width, qkv_cols + query_cols), BF),
            pltpu.VMEM((tokens, query_cols), BF),
            pltpu.VMEM((total_rows, qkv_cols), F32),
            pltpu.VMEM((total_rows, 2 * HD), F32),
            pltpu.VMEM((total_rows, 2 * HD), F32),
            *Reduce.room(line, pair, rows, width, chunks)[1:],
            pltpu.VMEM((rows, width), F32),
            dma((4,)),
            dma((2, 2, sizes["dp"])),
            dma((2,)),
            *Collect.room(sizes, own_rows, 3 * units),
            *Collect.room(sizes, own_rows, qkv_cols + query_cols),
            *Collect.sems(sizes, 3),
            *Collect.sems(sizes, 3),
            *Reduce.sems(chunks)(line),
            pltpu.VMEM((1, width), F32),
            *GainSum.room(sizes, width),
            *GainSum.sems(sizes),
        ],
        compiler_params=pltpu.CompilerParams(
            collective_id=collective_id, has_side_effects=True, vmem_limit_bytes=63 * 2**20
        ),
    )(*factors, low, hidden, grad_mid, gain, grad_gain_two, *tables)


def grad_pieces(sizes):
    group = sizes["ctx"] * sizes["core"]
    heads, keys, units = H * HD // group, KV * HD // group, FF // group
    pieces, offset = [], 0
    for name, width in (
        ("gate", units),
        ("up", units),
        ("down", units),
        ("query", heads),
        ("key_value", 2 * keys),
        ("out", heads),
    ):
        pieces.append((name, width, offset))
        offset += width
    return pieces


def adamw_kernel(step_rate, decay_rate, grad_ref, weight_ref, state_ref, grad_out, weight_out, state_out):
    gradient = grad_ref[...].astype(F32)
    grad_out[...] = gradient
    updated, states = adamw(weight_ref[...], gradient, state_ref[...], step_rate, decay_rate)
    weight_out[...] = updated
    state_out[...] = states


def adamw_columns(gradient, weight, states, step_rate, decay_rate):
    rows, columns = weight.shape
    step = math.gcd(columns, 1024)
    flat = pl.BlockSpec((rows, step), lambda i: (0, i))
    deep = pl.BlockSpec((2, rows, step), lambda i: (0, 0, i))
    return pl.pallas_call(
        functools.partial(adamw_kernel, step_rate, decay_rate),
        grid=(columns // step,),
        out_shape=[
            jax.ShapeDtypeStruct(weight.shape, F32),
            jax.ShapeDtypeStruct(weight.shape, F32),
            jax.ShapeDtypeStruct(states.shape, F32),
        ],
        in_specs=[flat, flat, deep],
        out_specs=[flat, flat, deep],
    )(gradient, weight, states)


def dot(left, right):
    return jnp.dot(left, right, preferred_element_type=F32)


def shards(
    sizes,
    hidden,
    cotangent,
    span_order,
    norm_gains,
    w_qkv,
    w_out,
    w_gate_up,
    w_down,
    mom_gains,
    mom_qkv,
    mom_out,
    mom_gate_up,
    mom_down,
):
    everyone = ("dp", "ctx", "x", "core")
    line, pair = sizes["ctx"], sizes["core"]
    group = line * pair
    block_rows, width = hidden.shape[1:]
    total_rows = block_rows * line
    span_rows = total_rows // span_order.shape[0]
    heads, kv_heads = H // group, KV // group
    query_cols, kv_cols = heads * HD, kv_heads * HD
    key_pos = (
        span_order[:, None] * span_rows + jnp.arange(span_rows, dtype=jnp.int32)[None, :]
    ).reshape(-1)
    cos_tab, sin_tab = rope_table(key_pos)
    signs = jnp.where(jnp.arange(HD) < HD // 2, -1.0, 1.0)
    cosines = jnp.concatenate([cos_tab] * (heads + kv_heads) + [jnp.ones_like(cos_tab)] * kv_heads, 1)
    sines = jnp.concatenate(
        [sin_tab * signs] * (heads + kv_heads) + [jnp.zeros_like(sin_tab)] * kv_heads, 1
    )
    tables = (cosines, sines, key_pos[:, None], key_pos[None, :])
    low, high, hidden_all = spread_weights(
        sizes, 0, hidden[0], norm_gains, w_qkv, w_out, w_gate_up, w_down
    )
    gains = low[:, 2 * query_cols + 2 * kv_cols :].astype(F32)[:, :2].T
    gain_one, gain_two = gains[:1], gains[1:]
    entry_one, qkv, attended = attend(hidden_all, low, gain_one, tables)
    output, grad_middle, grad_gain_two, grad_branch, entry_two, cot, activated, grad_gu = middle_rows(
        sizes, 1, attended, low, high, hidden[0], cotangent[0], gain_two
    )
    factors = (entry_two, grad_gu, cot, activated, entry_one, grad_branch, qkv, attended)
    *pieces, grad_hidden, gain_sums = closing(
        sizes, 2, factors, low, hidden[0], grad_middle, gain_one, grad_gain_two, tables
    )
    grad_gate, grad_up, grad_down, grad_query, grad_key_value, grad_out = pieces
    output, grad_hidden = output[None], grad_hidden[None]
    rows = w_qkv.shape[0]
    place = lax.axis_index(everyone) * rows
    grad_gains = lax.dynamic_slice(gain_sums, (0, lax.rem(place, 128)), (2, rows))
    grad_key_value = grad_key_value.reshape(rows, group, 2, kv_cols).transpose(0, 2, 1, 3)
    grad_qkv = jnp.concatenate([grad_query, grad_key_value.reshape(rows, -1)], 1)
    grad_gate_up = jnp.concatenate([grad_gate, grad_up], 1)
    new_gains, new_mom_gains = adamw(norm_gains, grad_gains, mom_gains, LR_GAIN, 0.0)
    grad_qkv, new_qkv, new_mom_qkv = adamw_columns(grad_qkv, w_qkv, mom_qkv, LR_MATRIX, DECAY_MATRIX)
    grad_out, new_out, new_mom_out = adamw_columns(grad_out, w_out, mom_out, LR_OUTPUT, DECAY_MATRIX)
    grad_gate_up, new_gate_up, new_mom_gate_up = adamw_columns(
        grad_gate_up, w_gate_up, mom_gate_up, LR_MATRIX, DECAY_MATRIX
    )
    grad_down, new_down, new_mom_down = adamw_columns(
        grad_down, w_down, mom_down, LR_MATRIX, DECAY_MATRIX
    )
    return (
        output,
        grad_hidden,
        grad_gains,
        grad_qkv,
        grad_out,
        grad_gate_up,
        grad_down,
        new_gains,
        new_qkv,
        new_out,
        new_gate_up,
        new_down,
        new_mom_gains,
        new_mom_qkv,
        new_mom_out,
        new_mom_gate_up,
        new_mom_down,
    )


def solution(mesh):
    shape = dict(mesh.shape)
    pair = 2 if shape["ctx"] * 2 <= KV and shape["fsdp"] % 2 == 0 else 1
    sizes = {"dp": shape["dp"], "ctx": shape["ctx"], "x": shape["fsdp"] // pair, "core": pair}
    finer = Mesh(mesh.devices.reshape(tuple(sizes.values())), tuple(sizes))
    tokens = P(("dp", "x", "core"), "ctx", None)
    everyone = ("dp", "ctx", "x", "core")
    rows, gains = P(everyone, None), P(None, everyone)
    row_moments, gain_moments = P(None, everyone, None), P(None, None, everyone)
    weights = (gains, rows, rows, rows, rows)
    moments = (gain_moments, row_moments, row_moments, row_moments, row_moments)
    return jax.shard_map(
        functools.partial(shards, sizes),
        mesh=finer,
        in_specs=(tokens, tokens, P()) + weights + moments,
        out_specs=(tokens, tokens) + weights + weights + moments,
        check_vma=False,
    )
```

```python
import functools
import math

import jax
import jax.numpy as jnp
from jax import lax
from jax.experimental import pallas as pl
from jax.experimental.pallas import tpu as pltpu
from jax.sharding import Mesh
from jax.sharding import PartitionSpec as P

MESH = pl.DeviceIdType.MESH
BF = jnp.bfloat16
F32 = jnp.float32
H = 32
KV = 8
HD = 64
FF = 8192


EPS_NORM = 1e-05
NEG_FILL = -1000000000.0
THETA = 500000.0
BETA_ONE = 0.9
BETA_TWO = 0.95
ADAM_EPS = 1e-08
DECAY_MATRIX = 0.1
LR_MATRIX = 0.01
LR_OUTPUT = 0.06
LR_GAIN = 0.3


def rope_table(positions):
    half_dim = HD // 2
    index_row = jnp.arange(half_dim, dtype=jnp.float32)
    frequency = jnp.exp(-(2.0 * index_row / HD) * math.log(THETA))
    wavelen = 2.0 * math.pi / frequency
    smooth = (8192.0 / wavelen - 1.0) / 3.0
    scaled = jnp.where(
        wavelen < 2048.0,
        frequency,
        jnp.where(
            wavelen > 8192.0,
            frequency / 32.0,
            (1.0 - smooth) * frequency / 32.0 + smooth * frequency,
        ),
    )
    angles = positions.astype(jnp.float32)[:, None] * scaled[None, :]
    cosine = jnp.cos(angles)
    sine_part = jnp.sin(angles)
    return (jnp.concatenate([cosine, cosine], 1), jnp.concatenate([sine_part, sine_part], 1))


def adamw(weight, gradient, states, step_rate, decay_rate):
    first_mom = BETA_ONE * states[0] + (1.0 - BETA_ONE) * gradient
    root_mom = jnp.sqrt(BETA_TWO * states[1] * states[1] + (1.0 - BETA_TWO) * gradient * gradient)
    first_hat = first_mom / (1.0 - BETA_ONE**3)
    root_hat = root_mom / math.sqrt(1.0 - BETA_TWO**3)
    updated = weight - step_rate * (first_hat / (root_hat + ADAM_EPS) + decay_rate * weight)
    return (updated, jnp.stack([first_mom, root_mom]))


def contract_rows(left_arr, right_arr):
    return lax.dot_general(
        left_arr, right_arr, (((0,), (0,)), ((), ())), preferred_element_type=jnp.float32
    )


def contract_cols(left_arr, right_arr):
    return lax.dot_general(
        left_arr, right_arr, (((1,), (1,)), ((), ())), preferred_element_type=jnp.float32
    )


def wrap(value, size):
    return lax.rem(value + size, size)


def remote(src, dst, send_sem, recv_sem, **where):
    return pltpu.make_async_remote_copy(
        src_ref=src,
        dst_ref=dst,
        send_sem=send_sem,
        recv_sem=recv_sem,
        device_id=where,
        device_id_type=MESH,
    )


def greet(places):
    barrier = pltpu.get_barrier_semaphore()
    for where in places:
        pl.semaphore_signal(barrier, inc=1, device_id=where, device_id_type=MESH)
    pl.semaphore_wait(barrier, len(places))


def greet_line(line, pair):
    barrier = pltpu.get_barrier_semaphore()
    here = lax.axis_index("ctx")

    @pl.when(here > 0)
    def _():
        pl.semaphore_signal(barrier, inc=1, device_id={"ctx": here - 1}, device_id_type=MESH)

    @pl.when(here < line - 1)
    def _():
        pl.semaphore_signal(barrier, inc=1, device_id={"ctx": here + 1}, device_id_type=MESH)

    if pair > 1:
        pl.semaphore_signal(
            barrier, inc=1, device_id={"core": 1 - lax.axis_index("core")}, device_id_type=MESH
        )
    ends = (here == 0).astype(jnp.int32) + (here == line - 1).astype(jnp.int32)
    pl.semaphore_wait(barrier, 2 - ends + (1 if pair > 1 else 0))


class Travel:
    @staticmethod
    def sems(many, line):
        return [pltpu.SemaphoreType.DMA((many,))] + [pltpu.SemaphoreType.DMA((many, 2, line))] * 4

    def __init__(self, line, pair, ins, outs, own_sem, line_send, line_recv, core_send, core_recv):
        self.line, self.pair, self.ins, self.outs = line, pair, ins, outs
        self.own_sem, self.line_sems, self.core_sems = own_sem, (line_send, line_recv), (core_send, core_recv)
        self.here = lax.axis_index("ctx")
        self.core = lax.axis_index("core")

    def block(self, way, step):
        return self.here - 1 - step if way == 0 else self.here + 1 + step

    def copy(self, sems, at, source, place, **where):
        return remote(place if source is None else source, place, sems[0].at[at], sems[1].at[at], **where)

    def hop(self, item, way, step, source=None):
        place = self.outs[item](self.core, self.block(way, step - 1))
        target = self.here + 1 if way == 0 else self.here - 1
        return self.copy(self.line_sems, (item, way, step), source, place, ctx=target)

    def arrived(self, item, way, step):
        place = self.outs[item](self.core, self.block(way, step))
        return self.copy(self.line_sems, (item, way, step), None, place, ctx=self.here)

    def share(self, item, way, step, source=None):
        place = self.outs[item](self.core, self.block(way, step))
        return self.copy(self.core_sems, (item, way, step + 1), source, place, core=1 - self.core)

    def shared(self, item, way, step):
        place = self.outs[item](1 - self.core, self.block(way, step))
        return self.copy(self.core_sems, (item, way, step + 1), None, place, core=1 - self.core)

    def own(self, item):
        place = self.outs[item](self.core, self.here)
        return pltpu.make_async_copy(self.ins[item], place, self.own_sem.at[item])

    def sends(self, way):
        return self.here < self.line - 1 if way == 0 else self.here > 0

    def has(self, way, step):
        return self.block(way, step) >= 0 if way == 0 else self.block(way, step) <= self.line - 1

    def begin(self):
        for item in range(len(self.ins)):
            for way in range(2):

                @pl.when(self.sends(way))
                def _(item=item, way=way):
                    self.hop(item, way, 0, self.ins[item]).start()

            if self.pair > 1:
                self.share(item, 0, -1, self.ins[item]).start()
            if self.ins[item] is not None:
                self.own(item).start()

    def step(self, step):
        for item in range(len(self.ins)):
            for way in range(2):

                @pl.when(self.has(way, step))
                def _(item=item, way=way):
                    self.arrived(item, way, step).wait_recv()
                    if step + 1 < self.line - 1:

                        @pl.when(self.sends(way))
                        def _():
                            self.hop(item, way, step + 1).start()

                    if self.pair > 1:
                        self.share(item, way, step).start()

    def end(self):
        for item in range(len(self.ins)):
            if self.ins[item] is not None:
                self.own(item).wait()
            if self.pair > 1:
                self.share(item, 0, -1, self.ins[item]).wait_send()
                self.shared(item, 0, -1).wait_recv()
            for way in range(2):

                @pl.when(self.sends(way))
                def _(item=item, way=way):
                    self.hop(item, way, 0, self.ins[item]).wait_send()

                for step in range(self.line - 1):

                    @pl.when(self.has(way, step))
                    def _(item=item, way=way, step=step):
                        if step + 1 < self.line - 1:

                            @pl.when(self.sends(way))
                            def _():
                                self.hop(item, way, step + 1).wait_send()

                        if self.pair > 1:
                            self.share(item, way, step).wait_send()
                            self.shared(item, way, step).wait_recv()


def add_rows(rows, out_ref, *parts):
    def one(index, carry):
        at = pl.ds(pl.multiple_of(index * 16, 16), 16)
        total = parts[0][at, :].astype(F32)
        for part in parts[1:]:
            total = total + part[at, :].astype(F32)
        out_ref[at, :] = total.astype(out_ref.dtype)
        return carry

    lax.fori_loop(0, rows // 16, one, 0)


class Reduce:
    @staticmethod
    def sems(*outer):
        dma = pltpu.SemaphoreType.DMA
        return lambda line: [dma(outer), dma(outer), dma(outer + (2, line)), dma(outer + (2, line))]

    @staticmethod
    def room(line, pair, rows, columns, *outer):
        return [
            pltpu.VMEM(outer + (pair, line, rows, columns), BF),
            pltpu.VMEM(outer + (line, rows, columns), BF),
            pltpu.VMEM(outer + (line + 1, rows, columns), BF),
        ]

    def __init__(self, line, pair, part, near, landed, core_send, core_recv, line_send, line_recv, at, kind=None):
        self.line, self.pair, self.at = line, pair, at
        self.sem_at = at if kind is None else (kind,) + at[1:]
        self.part, self.near, self.landed = part, near, landed
        self.core_sems, self.line_sems = (core_send, core_recv), (line_send, line_recv)
        self.here, self.core = lax.axis_index("ctx"), lax.axis_index("core")
        self.rows = part.shape[-2]

    def mine(self, block):
        return self.part.at[self.at + (self.core, block)]

    def across(self):
        return remote(
            self.part.at[self.at + (1 - self.core,)],
            self.near.at[self.at],
            self.core_sems[0].at[self.sem_at],
            self.core_sems[1].at[self.sem_at],
            core=1 - self.core,
        )

    def slot(self, way, block):
        return self.landed.at[self.at + (block + 1 if way == 0 else block,)]

    def onward(self, way, block, here):
        index = self.sem_at + (way, block)
        return remote(
            self.mine(block),
            self.slot(way, block),
            self.line_sems[0].at[index],
            self.line_sems[1].at[index],
            ctx=here + 1 if way == 0 else here - 1,
        )

    def begin(self):
        if self.pair > 1:
            self.across().start()

    def settle(self):
        if self.pair > 1:
            self.across().wait_recv()

    def terms(self, block):
        return [self.mine(block)] + ([self.near.at[self.at + (block,)]] if self.pair > 1 else [])

    def relay(self, way, block, here):
        @pl.when(self.here == here)
        def _():
            terms = self.terms(block)
            if here != (0 if way == 0 else self.line - 1):
                self.onward(way, block, here).wait_recv()
                terms.append(self.slot(way, block))
            if len(terms) > 1:
                add_rows(self.rows, self.mine(block), *terms)
            self.onward(way, block, here).start()

    def finish(self, here, total_ref):
        @pl.when(self.here == here)
        def _():
            terms = self.terms(here)
            for way, has in ((0, here > 0), (1, here < self.line - 1)):
                if has:
                    self.onward(way, here, here).wait_recv()
                    terms.append(self.slot(way, here))
            add_rows(self.rows, total_ref, *terms)

    def drain(self):
        if self.pair > 1:
            self.across().wait_send()
        for here in range(self.line):

            @pl.when(self.here == here)
            def _(here=here):
                for block in range(self.line):
                    if block != here:
                        self.onward(0 if block > here else 1, block, here).wait_send()

    def plan(self, start, total_ref, after):
        ends, steps = self.line - 1, [(start, self.begin), (start + LAG, self.settle)]
        for way in range(2):
            for block in range(self.line):
                for here in range(self.line):
                    if here < block if way == 0 else here > block:
                        wait = ends - block if way == 0 else block
                        depth = here if way == 0 else ends - here
                        when = start + LAG + wait * SEND + depth * HOP
                        steps.append((when, functools.partial(self.relay, way, block, here)))
        finish = start + LAG + ends * HOP + 0.5
        for here in range(self.line):
            steps.append((finish, functools.partial(self.finish, here, total_ref)))
        steps.append((finish, after))
        return steps, finish


SEND, HOP, LAG = 3.0, 4.5, 2.5


def run_steps(steps):
    for _, step in sorted(steps, key=lambda item: item[0]):
        step()


def blocks_in_order(line, pair):
    away = sorted(range(line), key=lambda d: min(d, line - d))
    return [(dz, dc) for dz in away for dc in range(pair)]


def greet_all(sizes):
    names = ("dp", "ctx", "x", "core")
    at = {name: lax.axis_index(name) for name in names}
    places = []
    for dz, dc in blocks_in_order(sizes["ctx"], sizes["core"]):
        if dz or dc:
            places.append(
                {"ctx": wrap(at["ctx"] + dz, sizes["ctx"]), "core": wrap(at["core"] + dc, sizes["core"])}
            )
    for name in ("dp", "x"):
        for step in range(1, sizes[name]):
            places.append({name: wrap(at[name] + step, sizes[name])})
    greet(places)


class Spread:
    @staticmethod
    def sems(sizes):
        dma = pltpu.SemaphoreType.DMA
        group, steps = sizes["ctx"] * sizes["core"], max(sizes["dp"], sizes["x"])
        return [dma((1,))] + [dma((group,))] * 2 + [dma((group, steps))] * 2 + [dma((group, steps, steps))] * 2

    def __init__(self, sizes, pack, out, sems):
        self.sizes, self.pack, self.out = sizes, pack, out
        self.own_sem, *rest = sems
        self.f_sems, self.a_sems, self.b_sems = rest[0:2], rest[2:4], rest[4:6]
        self.line, self.pair = sizes["ctx"], sizes["core"]
        self.at = {name: lax.axis_index(name) for name in ("dp", "ctx", "x", "core")}
        self.order = blocks_in_order(self.line, self.pair)

    def spot(self, dp, z, x, c):
        return self.out.at[dp * self.line + z, x * self.pair + c]

    def mine(self):
        return self.spot(*[self.at[name] for name in ("dp", "ctx", "x", "core")])

    def copy(self, sems, at, source, target, **where):
        return remote(source, target, *[sem.at[at] for sem in sems], **where)

    def first(self, index):
        dz, dc = self.order[index]
        z, c = wrap(self.at["ctx"] + dz, self.line), wrap(self.at["core"] + dc, self.pair)
        return self.copy(self.f_sems, index, self.pack.at[z * self.pair + c], self.mine(), ctx=z, core=c)

    def place(self, index, moved):
        dz, dc = self.order[index]
        z, c = wrap(self.at["ctx"] - dz, self.line), wrap(self.at["core"] - dc, self.pair)
        dp, x = [wrap(self.at[name] - moved.get(name, 0), self.sizes[name]) for name in ("dp", "x")]
        return self.spot(dp, z, x, c)

    def axes(self, index):
        return ("x", "dp") if sum(self.order[index]) % 2 == 0 else ("dp", "x")

    def ahead(self, name, step):
        return {name: wrap(self.at[name] + step, self.sizes[name])}

    def came(self, index):
        spot = self.place(index, {})
        return self.copy(self.f_sems, index, spot, spot, core=self.at["core"])

    def hop_one(self, index, step):
        spot = self.place(index, {})
        return self.copy(self.a_sems, (index, step), spot, spot, **self.ahead(self.axes(index)[0], step))

    def one_came(self, index, step):
        spot = self.place(index, {self.axes(index)[0]: step})
        return self.copy(self.a_sems, (index, step), spot, spot, core=self.at["core"])

    def hop_two(self, index, step, far):
        name, other = self.axes(index)
        spot = self.place(index, {name: step})
        return self.copy(self.b_sems, (index, step, far), spot, spot, **self.ahead(other, far))

    def two_came(self, index, step, far):
        name, other = self.axes(index)
        spot = self.place(index, {name: step, other: far})
        return self.copy(self.b_sems, (index, step, far), spot, spot, core=self.at["core"])

    def own(self):
        source = self.pack.at[self.at["ctx"] * self.pair + self.at["core"]]
        return pltpu.make_async_copy(source, self.mine(), self.own_sem.at[0])

    def begin(self, *indices):
        for index in indices:
            if index == 0:
                self.own().start()
            elif index < len(self.order):
                self.first(index).start()

    def onward(self, index, *more):
        if index == 0:
            self.own().wait()
        else:
            self.came(index).wait_recv()
        self.begin(*more)
        name, other = self.axes(index)
        for step in range(1, self.sizes[name]):
            self.hop_one(index, step).start()
        for far in range(1, self.sizes[other]):
            self.hop_two(index, 0, far).start()

    def onward_two(self, index):
        name, other = self.axes(index)
        for step in range(1, self.sizes[name]):
            self.one_came(index, step).wait_recv()
            for far in range(1, self.sizes[other]):
                self.hop_two(index, step, far).start()

    def complete(self, *indices):
        for index in indices:
            name, other = self.axes(index)
            for step in range(self.sizes[name]):
                for far in range(1, self.sizes[other]):
                    self.two_came(index, step, far).wait_recv()

    def drain(self):
        for index in range(len(self.order)):
            name, other = self.axes(index)
            if index:
                self.first(index).wait_send()
            for step in range(self.sizes[name]):
                if step:
                    self.hop_one(index, step).wait_send()
                for far in range(1, self.sizes[other]):
                    self.hop_two(index, step, far).wait_send()


class Collect:
    AXES = (("dp", "x"), ("x", "dp"))

    @staticmethod
    def room(sizes, rows, width):
        room = [pltpu.VMEM((sizes["ctx"], sizes["dp"], sizes["x"], sizes["core"], rows, width), BF)]
        for parity, (name, other) in enumerate(Collect.AXES):
            count = sum((dz + dc) % 2 == parity for dz, dc in blocks_in_order(sizes["ctx"], sizes["core"]))
            room.append(pltpu.VMEM((max(1, count), (sizes[name] - 1) * sizes[other], rows, width), BF))
            room.append(pltpu.VMEM((max(1, count), sizes[other] - 1, rows, width), BF))
        return room

    @staticmethod
    def sems(sizes, pieces):
        dma = pltpu.SemaphoreType.DMA
        group, steps = sizes["ctx"] * sizes["core"], max(sizes["dp"], sizes["x"])
        return (
            [dma((pieces,))]
            + [dma((group, steps, steps))] * 2
            + [dma((group, steps))] * 2
            + [dma((group, pieces))] * 2
        )

    def __init__(self, sizes, widths, pieces, room, sems):
        self.sizes, self.widths, self.pieces = sizes, widths, pieces
        self.terms = room[0]
        self.near, self.far_in = room[1::2], room[2::2]
        self.own_sem, *rest = sems
        self.a_sems, self.b_sems, self.f_sems = rest[0:2], rest[2:4], rest[4:6]
        self.line, self.pair = sizes["ctx"], sizes["core"]
        self.rows = self.terms.shape[-2]
        self.at = {name: lax.axis_index(name) for name in ("dp", "ctx", "x", "core")}
        self.me = self.at["ctx"] * self.pair + self.at["core"]
        self.away = sorted(range(self.line), key=lambda d: -min(d, self.line - d))
        self.order = [(dz, dc) for dz in self.away for dc in range(self.pair)]

    def spot_of(self, index, sign=1):
        dz, dc = self.order[index]
        return wrap(self.at["ctx"] + sign * dz, self.line), wrap(self.at["core"] + sign * dc, self.pair)

    def parity(self, index):
        return sum(self.order[index]) % 2

    def axes(self, index):
        return self.AXES[self.parity(index)]

    def slot(self, index):
        return sum(self.parity(before) == self.parity(index) for before in range(index))

    def indices(self, tick):
        return range(tick * self.pair, (tick + 1) * self.pair)

    def lanes(self, tick, dp):
        across = self.sizes["x"] * self.pair * self.rows
        z = wrap(self.at["ctx"] + self.away[tick], self.line)
        return pl.ds(pl.multiple_of((dp * self.line + z) * across, 128), across)

    def multiply(self, tick, lefts, rights):
        start = 0
        for left, right, width in zip(lefts, rights, self.widths):
            step = math.gcd(width, 512)

            @pl.loop(0, self.sizes["dp"])
            def _(dp, left=left, right=right, start=start, width=width, step=step):
                left_t = left[dp].T

                @pl.loop(0, width // step)
                def _(part):
                    columns = pl.ds(pl.multiple_of(part * step, 128), step)
                    into = pl.ds(pl.multiple_of(start + part * step, 128), step)
                    product = dot(left_t, right[:, columns]).astype(BF)
                    for x in range(self.sizes["x"]):
                        for core in range(self.pair):
                            low = (x * self.pair + core) * self.rows
                            self.terms[tick, dp, x, core, :, into] = product[low : low + self.rows]

            start += width

    def block_terms(self, index, first_at, other_at):
        name, other = self.axes(index)
        spot = {name: first_at, other: other_at}
        return self.terms.at[index // self.pair, spot["dp"], spot["x"], self.spot_of(index)[1]]

    def landing(self, index, step, place):
        at = (step - 1) * self.sizes[self.axes(index)[1]] + place
        return self.near[self.parity(index)].at[self.slot(index), at]

    def far_landing(self, index, far):
        return self.far_in[self.parity(index)].at[self.slot(index), far - 1]

    def hop_one(self, index, step, place):
        name = self.axes(index)[0]
        to = wrap(self.at[name] + step, self.sizes[name])
        sems = [sem.at[index, step, place] for sem in self.a_sems]
        return remote(
            self.block_terms(index, to, place), self.landing(index, step, place), *sems, **{name: to}
        )

    def hop_two(self, index, far):
        name, other = self.axes(index)
        to = wrap(self.at[other] + far, self.sizes[other])
        sems = [sem.at[index, far] for sem in self.b_sems]
        return remote(
            self.block_terms(index, self.at[name], to), self.far_landing(index, far), *sems, **{other: to}
        )

    def done(self, index):
        name, other = self.axes(index)
        return self.block_terms(index, self.at[name], self.at[other])

    def stays(self, index):
        return self.order[index] == (0, 0)

    def piece_at(self, piece, member):
        out, width, _ = self.pieces[piece]
        return out.at[:, pl.ds(pl.multiple_of(member * width, 128), width)]

    def last(self, index, piece):
        z, c = self.spot_of(index)
        _, width, offset = self.pieces[piece]
        source = self.done(index).at[:, pl.ds(offset, width)]
        target = self.piece_at(piece, self.me)
        if self.stays(index):
            return pltpu.make_async_copy(source, target, self.own_sem.at[piece])
        return remote(source, target, *[sem.at[index, piece] for sem in self.f_sems], ctx=z, core=c)

    def last_came(self, index, piece):
        z, c = self.spot_of(index, -1)
        spot = self.piece_at(piece, z * self.pair + c)
        sems = [sem.at[index, piece] for sem in self.f_sems]
        return remote(spot, spot, *sems, core=self.at["core"])

    def places(self, index):
        other = self.axes(index)[1]
        size = self.sizes[other]
        return [(far, wrap(self.at[other] + far, size)) for far in list(range(1, size)) + [0]]

    def send_one(self, tick):
        for index in self.indices(tick):
            for _, place in self.places(index):
                for step in range(1, self.sizes[self.axes(index)[0]]):
                    self.hop_one(index, step, place).start()

    def sum_one(self, tick):
        for index in self.indices(tick):
            name = self.axes(index)[0]
            for far, place in self.places(index):
                steps = range(1, self.sizes[name])
                for step in steps:
                    self.hop_one(index, step, place).wait_recv()
                kept = self.block_terms(index, self.at[name], place)
                add_rows(self.rows, kept, kept, *[self.landing(index, step, place) for step in steps])
                if far:
                    self.hop_two(index, far).start()

    def sum_two(self, tick):
        for index in self.indices(tick):
            fars = range(1, self.sizes[self.axes(index)[1]])
            for far in fars:
                self.hop_two(index, far).wait_recv()
            done = self.done(index)
            add_rows(self.rows, done, done, *[self.far_landing(index, far) for far in fars])
            for piece in range(len(self.pieces)):
                self.last(index, piece).start()

    def drain(self):
        for index in range(len(self.order)):
            name, other = self.axes(index)
            for step in range(1, self.sizes[name]):
                for place in range(self.sizes[other]):
                    self.hop_one(index, step, place).wait_send()
            for far in range(1, self.sizes[other]):
                self.hop_two(index, far).wait_send()
            for piece in range(len(self.pieces)):
                if self.stays(index):
                    self.last(index, piece).wait()
                else:
                    self.last(index, piece).wait_send()
                    self.last_came(index, piece).wait_recv()


def lane_index(shape):
    return lax.broadcasted_iota(jnp.int32, shape, len(shape) - 1)


def turned(values):
    half, columns = HD // 2, values.shape[1]
    ahead = pltpu.roll(values, columns - half, 1)
    behind = pltpu.roll(values, half, 1)
    return jnp.where(lane_index(values.shape) % HD < half, ahead, behind)


def only_head(values, head):
    return jnp.where(lane_index(values.shape) // HD == head, values, jnp.zeros_like(values))


def both_halves(values, head):
    wide = values.astype(F32)
    return jnp.where(lane_index(wide.shape) // HD == head, wide, pltpu.roll(wide, HD, 1)).astype(BF)


def softmax_rows(queries, keys, visible):
    scores = contract_cols(queries, keys) * HD ** (-0.5)
    scores = jnp.where(visible, scores, NEG_FILL)
    exponent = jnp.exp(scores - jnp.max(scores, -1, keepdims=True))
    return exponent / jnp.sum(exponent, -1, keepdims=True)


def query_rows(total_rows):
    return min(total_rows, 2**18 // total_rows)


def opening_kernel(sizes, chunks, *refs):
    line, pair = sizes["ctx"], sizes["core"]
    group = line * pair
    refs = list(refs)

    def take(count):
        taken, refs[:count] = refs[:count], []
        return taken

    qkv_in, out_in, gate_up_in, down_in, gain_in, hidden_ref, cot_ref, cos_ref, sin_ref, pos_col, pos_row = take(11)
    output_ref, grad_mid_ref, gain_grad_ref, gains_ref = take(4)
    low_out, entry_one_out, qkv_out, heads_out, branch_ref, entry_two_out, cots_out, act_out, dgu_out = take(9)
    stage, tall, wide, low_w, ffn_w, rows_in, cots, qkv, heads, act, dgu = take(11)
    part, near, landed, total, middle, branch = take(6)
    stage_sem, out_sem, slot_sem = take(3)
    tall_sems, wide_sems, reduce_sems, hidden_sems, travel_sems = take(7), take(7), take(4), take(5), take(5)

    rows, width = part.shape[-2:]
    own_rows = tall.shape[1]
    block_rows = rows * chunks
    tokens = group * rows
    total_rows = cos_ref.shape[0]
    qkv_cols, query_cols = qkv.shape[1], heads.shape[-1]
    units = ffn_w.shape[-1] // 3
    groups = ffn_w.shape[0]
    core, here = lax.axis_index("core"), lax.axis_index("ctx")
    steps, travels, sums = [], [], []
    low, high = Spread(sizes, tall, low_w, tall_sems), Spread(sizes, wide, ffn_w, wide_sems)
    gain_rows = [gains_ref.at[pl.ds(0, 1)], gains_ref.at[pl.ds(1, 1)]]

    def step(time, function, *values):
        steps.append((time, functools.partial(function, *values)))

    def chunk_rows(chunk):
        return slice(chunk * rows, (chunk + 1) * rows)

    def staged(member):
        slot = member % 2
        sources = (
            gate_up_in.at[:, pl.ds(member * units, units)],
            gate_up_in.at[:, pl.ds(FF + member * units, units)],
            down_in.at[:, pl.ds(member * units, units)],
        )
        return [
            pltpu.make_async_copy(
                source, stage.at[slot, :, pl.ds(index * units, units)], stage_sem.at[slot, index]
            )
            for index, source in enumerate(sources)
        ]

    def pack_low():
        keys = KV * HD // group
        heads_of = H * HD // group
        for member in range(group):
            key_at, value_at = H * HD + member * keys, (H + KV) * HD + member * keys
            tall[member, :, :heads_of] = qkv_in[:, member * heads_of : (member + 1) * heads_of].astype(BF)
            both = jnp.concatenate(
                [qkv_in[:, key_at : key_at + keys], qkv_in[:, value_at : value_at + keys]], 1
            )
            tall[member, :, heads_of:qkv_cols] = both.astype(BF)
            tall[member, :, qkv_cols : qkv_cols + heads_of] = out_in[
                :, member * heads_of : (member + 1) * heads_of
            ].astype(BF)
            tall[member, :, qkv_cols + heads_of :] = gain_in[...].astype(BF)

    def pack_high():
        for member in range(group):
            for load in staged(member):
                load.wait()
            wide[member] = stage[member % 2].astype(BF)
            if member + 2 < group:
                for load in staged(member + 2):
                    load.start()

    def columns_of(weight, first, size):
        return weight[:, :, :, first : first + size].reshape(width, size)

    def rows_of(weight, index, count, first, size):
        each = groups // count
        return weight[index * each : (index + 1) * each, :, :, first : first + size].reshape(-1, size)

    def gains_to_rows():
        columns = columns_of(low_w, qkv_cols + query_cols, 128).astype(F32)
        gains_ref[...] = columns.T[:8, :]

    def project(sequence):
        weight = columns_of(low_w, 0, qkv_cols)

        @pl.loop(0, line)
        def _(z):
            values = rows_in[:, sequence, z].reshape(block_rows, width).astype(F32)
            inverse = lax.rsqrt(jnp.mean(values * values, -1, keepdims=True) + EPS_NORM)
            entry = (values * inverse * gain_rows[0][...]).astype(BF)
            rows_in[:, sequence, z] = entry.reshape(chunks, rows, width)
            projected = dot(entry, weight)
            table_at = pl.ds(pl.multiple_of(z * block_rows, block_rows), block_rows)
            rotated = projected * cos_ref[table_at, :] + turned(projected) * sin_ref[table_at, :]
            at = pl.ds(pl.multiple_of((sequence * line + z) * block_rows, block_rows), block_rows)
            qkv[at, :] = rotated.astype(BF)

    def attention(sequence, first, size, lane):
        start = sequence * total_rows
        both = qkv[start : start + total_rows, query_cols:]
        keys, values = both_halves(both, 0), both_halves(both, 1)
        visible = pos_row[...] <= pos_col[first : first + size, :]
        queries = qkv[start + first : start + first + size, lane : lane + 2 * HD]
        two = [
            dot(softmax_rows(only_head(queries, head), keys, visible).astype(BF), values)
            for head in range(2)
        ]
        merged = jnp.where(lane_index(two[0].shape) < HD, two[0], two[1]).astype(BF)
        from_z, to_z = first // block_rows, (first + size) // block_rows
        heads[sequence, from_z:to_z, :, lane : lane + 2 * HD] = merged.reshape(-1, block_rows, 2 * HD)

    def entry_one_copies():
        return [
            pltpu.make_async_copy(rows_in.at[:, c, z], entry_one_out.at[c, z], out_sem.at[3 + c * line + z])
            for c in range(pair)
            for z in range(line)
        ]

    whole_copies = [
        pltpu.make_async_copy(low_w, low_out, out_sem.at[0]),
        pltpu.make_async_copy(qkv, qkv_out, out_sem.at[1]),
        pltpu.make_async_copy(heads, heads_out, out_sem.at[2]),
    ]

    def chunk_copies(chunk):
        return [
            pltpu.make_async_copy(source, target.at[chunk], slot_sem.at[chunk, index])
            for index, (source, target) in enumerate(
                (
                    (act.at[chunk % 2], act_out),
                    (dgu.at[chunk % 2], dgu_out),
                    (rows_in.at[chunk], entry_two_out),
                    (cots.at[chunk], cots_out),
                )
            )
        ]

    def start_all(copies):
        for copy in copies:
            copy.start()

    def wait_all(copies):
        for copy in copies:
            copy.wait()

    def reducer(kind, chunk):
        one = Reduce(line, pair, part, near, landed, *reduce_sems, (kind // 2, chunk), kind)
        sums.append(one)
        return one

    def traveller(sems, source, place, start, hop):
        one = Travel(line, pair, [source], [place], *sems)
        steps.append((start, one.begin))
        for index in range(line - 1):
            steps.append((start + (index + 1) * hop, functools.partial(one.step, index)))
        finish = start + line * hop - 1.0
        steps.append((finish, one.end))
        return finish

    def product(chunk):
        mine = heads[:, :, chunk_rows(chunk), :].reshape(tokens, query_cols)
        for index in range(4):
            at = slice(index * (width // 4), (index + 1) * (width // 4))
            term = contract_cols(mine, rows_of(low_w, index, 4, qkv_cols, query_cols)).astype(BF)
            part[0, chunk, :, :, :, at] = term.reshape(pair, line, rows, -1)

    def norm_rows(chunk):
        mid = hidden_ref[chunk].astype(F32) + total[...]
        middle[chunk_rows(chunk), :] = mid
        inverse = lax.rsqrt(jnp.mean(mid * mid, -1, keepdims=True) + EPS_NORM)
        rows_in[chunk, core, here] = (mid * inverse * gain_rows[1][...]).astype(BF)

    def units_part(chunk, index, count):
        size = units // count
        slot = chunk % 2
        entry = rows_in[chunk].reshape(tokens, width)
        first, last = index * size, (index + 1) * size
        gate = dot(entry, columns_of(ffn_w, first, size))
        up = dot(entry, columns_of(ffn_w, units + first, size))
        grad_act = dot(cots[chunk].reshape(tokens, width), columns_of(ffn_w, 2 * units + first, size))
        sigmoid = 1.0 / (1.0 + jnp.exp(-gate))
        silu = gate * sigmoid
        act[slot, :, first:last] = (silu * up).astype(BF)
        dgu[slot, :, first:last] = (grad_act * up * sigmoid * (1.0 + gate * (1.0 - sigmoid))).astype(BF)
        dgu[slot, :, units + first : units + last] = (grad_act * silu).astype(BF)

    def back_part(chunk, index, count):
        size = width // count
        at = slice(index * size, (index + 1) * size)
        term = contract_cols(dgu[chunk % 2], rows_of(ffn_w, index, count, 0, 2 * units)).astype(BF)
        part[0, chunk, :, :, :, at] = term.reshape(pair, line, rows, size)

    def down_part(chunk, index, count):
        size = width // count
        at = slice(index * size, (index + 1) * size)
        term = contract_cols(act[chunk % 2], rows_of(ffn_w, index, count, 2 * units, units)).astype(BF)
        part[1, chunk, :, :, :, at] = term.reshape(pair, line, rows, size)

    def norm_rows_back(chunk):
        mid = middle[chunk_rows(chunk), :]
        inverse = lax.rsqrt(jnp.mean(mid * mid, -1, keepdims=True) + EPS_NORM)
        normed = mid * inverse
        grad_entry = total[...]
        gain_term = jnp.sum(grad_entry * normed, 0, keepdims=True)
        if chunk == 0:
            gain_grad_ref[...] = gain_term
        else:
            gain_grad_ref[...] += gain_term
        grad_normed = grad_entry * gain_rows[1][...]
        grad_rows = inverse * (
            grad_normed - normed * jnp.mean(grad_normed * normed, -1, keepdims=True)
        )
        grad_mid = cot_ref[chunk].astype(F32) + grad_rows
        grad_mid_ref[chunk_rows(chunk), :] = grad_mid
        branch[chunk] = grad_mid.astype(BF)

    def write_output(chunk):
        output_ref[chunk_rows(chunk), :] = (middle[chunk_rows(chunk), :] + total[...]).astype(BF)

    for member in range(2):
        start_all(staged(member))
    greet_all(sizes)

    step(0.0, pack_low)
    hidden_done = traveller(
        hidden_sems, hidden_ref, lambda c, z: rows_in.at[:, c, z], 0.0, T_HIDDEN
    )
    step(0.1, low.begin, *range(group))
    step(0.2, pack_high)
    step(0.3, high.begin, *range(min(group, 4)))
    for index in range(group):
        when = 1.0 + T_LOW * (index // 2)
        step(when, low.onward, index)
        step(when + T_LOW + 1.0, low.onward_two, index)
        when = 1.0 + T_HIGH * (index // 2)
        step(when, high.onward, index, *([index + 2] if index >= 2 else []))
        step(when + T_HIGH * 0.6, high.onward_two, index)
    weights_there = 1.0 + T_HIGH * (group // 2) + 8.0

    now = max(hidden_done + 0.2, 1.0 + T_LOW * (group // 2) + 6.0)
    step(now, low.complete, *range(group))
    step(now, gains_to_rows)
    step(now, whole_copies[0].start)
    for sequence in range(pair * line * block_rows // total_rows):
        step(now + 0.1, project, sequence)
        now += 2.5
    step(now, start_all, entry_one_copies())
    step(now, whole_copies[1].start)
    size = query_rows(total_rows) // 2
    for sequence in range(pair * line * block_rows // total_rows):
        for first in range(0, total_rows, size):
            for lane in range(0, query_cols, 2 * HD):
                step(now + 0.1, attention, sequence, first, size, lane)
                now += 1.0
    step(now, whole_copies[2].start)
    step(now, wait_all, entry_one_copies())

    span = (line - 1) * SEND
    ready_ffn, ready_back, base = weights_there, 0.0, now + 0.5
    count = 4
    for chunk in range(chunks):
        cot_done = traveller(
            [sem.at[0, chunk] for sem in travel_sems],
            cot_ref.at[chunk],
            lambda c, z, k=chunk: cots.at[k, c, z],
            base + chunk * span,
            HOP,
        )
        begin = base + 1.0 + chunk * span
        step(begin - 0.5, product, chunk)
        first_sum = reducer(0, chunk)
        more, finish = first_sum.plan(begin, total, functools.partial(norm_rows, chunk))
        steps.extend(more)
        arrived = traveller(
            [sem.at[1, chunk] for sem in travel_sems],
            None,
            lambda c, z, k=chunk: rows_in.at[k, c, z],
            finish,
            HOP,
        )
        begin = max(arrived, cot_done, ready_ffn) + 0.1
        if chunk == 0:
            step(begin, high.complete, *range(group))
        if chunk >= 2:
            step(begin, wait_all, chunk_copies(chunk - 2))
        step(begin, first_sum.drain)
        for index in range(count):
            step(begin + index, units_part, chunk, index, count)
        for index in range(count):
            step(begin + 4 + 0.8 * index, back_part, chunk, index, count)
        for index in range(count):
            step(begin + 7.3 + 0.5 * index, down_part, chunk, index, count)
        step(begin + 4.0, start_all, chunk_copies(chunk))
        ready_ffn = begin + 9.5
        begin = max(begin + 7.25, ready_back)
        ready_back = begin + span
        more, finish = reducer(1, chunk).plan(begin, total, functools.partial(norm_rows_back, chunk))
        steps.extend(more)
        traveller(
            [sem.at[2, chunk] for sem in travel_sems],
            branch.at[chunk],
            lambda c, z, k=chunk: branch_ref.at[c, z, pl.ds(k * rows, rows)],
            finish,
            HOP,
        )
    for chunk in range(chunks):
        begin = ready_back + chunk * span
        steps.extend(reducer(2, chunk).plan(begin, total, functools.partial(write_output, chunk))[0])
    run_steps(steps)
    for one in sums:
        if one.sem_at[0]:
            one.drain()
    low.drain()
    high.drain()
    wait_all(whole_copies)
    for chunk in range(max(0, chunks - 2), chunks):
        wait_all(chunk_copies(chunk))


T_HIDDEN, T_LOW, T_HIGH = 14.0, 7.0, 28.0


def opening(sizes, collective_id, weights, gains, hidden, cot, tables):
    line, pair = sizes["ctx"], sizes["core"]
    group = line * pair
    block_rows, width = hidden.shape
    chunks = 4
    rows = block_rows // chunks
    tokens = group * rows
    own_rows = weights[0].shape[0]
    heads, keys, units = H * HD // group, KV * HD // group, FF // group
    qkv_cols = heads + 2 * keys
    tall, wide = qkv_cols + heads + 128, 3 * units
    blocks = (sizes["dp"] * line, sizes["x"] * pair, own_rows)
    gain_tile = jnp.pad(gains.T, ((0, 0), (0, 126)))
    any_spec = pl.BlockSpec(memory_space=pl.ANY)
    vmem = pl.BlockSpec(memory_space=pltpu.VMEM)
    shape = jax.ShapeDtypeStruct
    dma = pltpu.SemaphoreType.DMA
    by_chunk = (chunks, pair, line, rows, width)
    outs = pl.pallas_call(
        functools.partial(opening_kernel, sizes, chunks),
        out_shape=[
            shape((block_rows, width), BF),
            shape((block_rows, width), F32),
            shape((1, width), F32),
            shape((8, width), F32),
            shape(blocks + (tall,), BF),
            shape((pair, line, chunks, rows, width), BF),
            shape((group * block_rows, qkv_cols), BF),
            shape((pair, line, block_rows, heads), BF),
            shape((pair, line, block_rows, width), BF),
            shape(by_chunk, BF),
            shape(by_chunk, BF),
            shape((chunks, tokens, units), BF),
            shape((chunks, tokens, 2 * units), BF),
        ],
        in_specs=[vmem, vmem, any_spec, any_spec] + [vmem] * 7,
        out_specs=[vmem] * 4 + [any_spec] * 9,
        scratch_shapes=[
            pltpu.VMEM((2, own_rows, wide), F32),
            pltpu.VMEM((group, own_rows, tall), BF),
            pltpu.VMEM((group, own_rows, wide), BF),
            pltpu.VMEM(blocks + (tall,), BF),
            pltpu.VMEM(blocks + (wide,), BF),
            pltpu.VMEM(by_chunk, BF),
            pltpu.VMEM(by_chunk, BF),
            pltpu.VMEM((group * block_rows, qkv_cols), BF),
            pltpu.VMEM((pair, line, block_rows, heads), BF),
            pltpu.VMEM((2, tokens, units), BF),
            pltpu.VMEM((2, tokens, 2 * units), BF),
            *Reduce.room(line, pair, rows, width, 2, chunks),
            pltpu.VMEM((rows, width), F32),
            pltpu.VMEM((block_rows, width), F32),
            pltpu.VMEM((chunks, rows, width), BF),
            dma((2, 3)),
            dma((3 + group,)),
            dma((chunks, 4)),
            *Spread.sems(sizes),
            *Spread.sems(sizes),
            *Reduce.sems(3, chunks)(line),
            *Travel.sems(1, line),
            dma((3, chunks, 1)),
            *[dma((3, chunks, 1, 2, line))] * 4,
        ],
        compiler_params=pltpu.CompilerParams(
            collective_id=collective_id, has_side_effects=True, vmem_limit_bytes=63 * 2**20
        ),
    )(*weights, gain_tile, hidden.reshape(chunks, rows, width), cot.reshape(chunks, rows, width), *tables)
    output, grad_mid, gain_grad, gain_rows, low, *rest = outs
    return output, grad_mid, gain_grad, gain_rows, low.reshape(width, tall), [
        array.reshape(-1, array.shape[-1]) for array in rest
    ]


class GainSum:
    @staticmethod
    def room(sizes, width):
        group = sizes["ctx"] * sizes["core"]
        return [
            pltpu.VMEM((8, width), F32),
            pltpu.VMEM((sizes["x"] - 1, 8, width), F32),
            pltpu.VMEM((sizes["dp"] - 1, 8, width), F32),
            pltpu.VMEM((group, 8, 128), F32),
        ]

    @staticmethod
    def sems(sizes):
        group = sizes["ctx"] * sizes["core"]
        counts = (sizes["x"], sizes["x"], sizes["dp"], sizes["dp"], group, group)
        return [pltpu.SemaphoreType.DMA((count,)) for count in counts]

    def __init__(self, sizes, own_rows, out_ref, room, sems):
        self.sizes, self.own_rows, self.out_ref = sizes, own_rows, out_ref
        self.mine, self.over_x, self.over_dp, self.tiles = room
        self.sems_of = {"x": sems[0:2], "dp": sems[2:4], "group": sems[4:6]}
        self.at = {name: lax.axis_index(name) for name in ("dp", "ctx", "x", "core")}
        self.order = blocks_in_order(sizes["ctx"], sizes["core"])

    def hop(self, name, step):
        into = (self.over_x if name == "x" else self.over_dp).at[step - 1]
        sems = [sem.at[step] for sem in self.sems_of[name]]
        return remote(self.mine, into, *sems, **{name: wrap(self.at[name] + step, self.sizes[name])})

    def tile(self, index):
        dz, dc = self.order[index]
        z, c = wrap(self.at["ctx"] + dz, self.sizes["ctx"]), wrap(self.at["core"] + dc, self.sizes["core"])
        place = (self.at["dp"] * self.sizes["ctx"] + z) * self.sizes["x"] + self.at["x"]
        first = (place * self.sizes["core"] + c) * self.own_rows
        source = self.mine.at[:, pl.ds(pl.multiple_of(first // 128 * 128, 128), 128)]
        sems = [sem.at[index] for sem in self.sems_of["group"]]
        if index == 0:
            return source
        return remote(source, self.tiles.at[index], *sems, ctx=z, core=c)

    def begin(self, first, second):
        self.mine[...] = jnp.zeros_like(self.mine)
        self.mine[0:1, :] = first[...]
        self.mine[1:2, :] = second[...]
        self.send("x")

    def send(self, name):
        for step in range(1, self.sizes[name]):
            self.hop(name, step).start()

    def add(self, name):
        for step in range(1, self.sizes[name]):
            self.hop(name, step).wait()
        for step in range(1, self.sizes[name]):
            self.mine[...] += (self.over_x if name == "x" else self.over_dp)[step - 1]

    def second(self):
        self.add("x")
        self.send("dp")

    def third(self):
        self.add("dp")
        for index in range(1, len(self.order)):
            self.tile(index).start()

    def end(self):
        total = self.tile(0)[...]
        for index in range(1, len(self.order)):
            self.tile(index).wait()
            total = total + self.tiles[index]
        self.out_ref[...] = total


def closing_kernel(sizes, chunks, *refs):
    (entry_two, dgu_ref, cot_ref, act_ref, entry_one, branch_ref, qkv_ref, heads_ref, low_ref) = refs[:9]
    hidden_ref, grad_mid_ref, gain_ref, gain_two_ref, cos_ref, sin_ref, pos_col, pos_row = refs[9:17]
    piece_refs, (grad_hidden_ref, gain_sum_ref) = refs[17:23], refs[23:25]
    refs = refs[1:]
    (left_slots, part, act, dqkv, heads, branch_slots, low_w, grad_heads, grad_proj, key_acc, value_acc) = refs[24:35]
    near, landed, total, load_sem, left_sem, branch_sem = refs[35:41]
    ffn_room, att_room = refs[41:46], refs[46:51]
    ffn_sems, att_sems, reduce_sems = refs[51:58], refs[58:65], refs[65:69]
    gain_grad_ref, gain_room, gain_sems = refs[69], refs[70:74], refs[74:80]
    line, pair = sizes["ctx"], sizes["core"]
    rows = part.shape[-2]
    block_rows, width = hidden_ref.shape
    tokens, total_rows = qkv_ref.shape[0], cos_ref.shape[0]
    query_cols = heads.shape[1]
    qkv_cols = dqkv.shape[1]
    loads = {
        "dgu": pltpu.make_async_copy(dgu_ref, part, load_sem.at[0]),
        "act": pltpu.make_async_copy(act_ref, act, load_sem.at[1]),
        "heads": pltpu.make_async_copy(heads_ref, heads, load_sem.at[2]),
        "low": pltpu.make_async_copy(low_ref.at[:, pl.ds(0, low_w.shape[1])], low_w, load_sem.at[3]),
    }
    names = grad_pieces(sizes)
    shift = names[3][2]
    ffn_pieces = [(ref, w, o) for ref, (_, w, o) in zip(piece_refs[:3], names[:3])]
    att_pieces = [(ref, w, o - shift) for ref, (_, w, o) in zip(piece_refs[3:], names[3:])]
    ffn = Collect(sizes, (2 * act.shape[1], act.shape[1]), ffn_pieces, ffn_room, ffn_sems)
    att = Collect(sizes, (qkv_cols, query_cols), att_pieces, att_room, att_sems)
    sums = [
        Reduce(line, pair, part, near, landed, *reduce_sems, (chunk,)) for chunk in range(chunks)
    ]
    gain_sum = GainSum(sizes, ffn.rows, gain_sum_ref, gain_room, gain_sems)

    def left_loads(turn):
        tick, slot = turn % line, turn % 2
        one, sources = (ffn, (entry_two, cot_ref)) if turn < line else (att, (entry_one, branch_ref))
        return [
            pltpu.make_async_copy(
                source.at[:, one.lanes(tick, dp)], left_slots.at[slot, item, dp], left_sem.at[slot, item, dp]
            )
            for item, source in enumerate(sources)
            for dp in range(sizes["dp"])
        ]

    def branch_load(index):
        size = branch_slots.shape[1]
        return pltpu.make_async_copy(
            branch_ref.at[pl.ds(index * size, size)], branch_slots.at[index % 2], branch_sem.at[index % 2]
        )

    for load in left_loads(0):
        load.start()
    for load in loads.values():
        load.start()
    for load in left_loads(1):
        load.start()
    greet_all(sizes)

    def multiply(turn):
        for load in left_loads(turn):
            load.wait()
        lefts = [left_slots.at[turn % 2, item] for item in range(2)]
        if turn < line:
            ffn.multiply(turn, lefts, (part_rows, act))
        else:
            att.multiply(turn - line, lefts, (dqkv, heads))
        if turn + 2 < 2 * line:
            for load in left_loads(turn + 2):
                load.start()

    class PartRows:
        def __getitem__(self, at):
            return part[:, :, :, :, at[1]].reshape(tokens, -1)

    part_rows = PartRows()

    def back_to_heads():
        loads["low"].wait()
        size = branch_slots.shape[1]
        branch_load(0).start()
        for index in range(tokens // size):
            if index + 1 < tokens // size:
                branch_load(index + 1).start()
            branch_load(index).wait()
            grad_heads[index * size : (index + 1) * size, :] = dot(
                branch_slots[index % 2], low_w[:, qkv_cols:]
            ).astype(BF)

    def attention_part(sequence, low, size, lane):
        start = sequence * total_rows
        span = slice(start, start + total_rows)
        at = slice(start + low, start + low + size)
        both = qkv_ref[span, query_cols:]
        keys, values = both_halves(both, 0), both_halves(both, 1)
        visible = pos_row[...] <= pos_col[low : low + size, :]
        queries = qkv_ref[at, lane : lane + 2 * HD]
        grads = grad_heads[at, lane : lane + 2 * HD]
        grad_queries = []
        key_term = value_term = None
        for head in range(2):
            query, grad = only_head(queries, head), only_head(grads, head)
            probability = softmax_rows(query, keys, visible)
            grad_prob = contract_cols(grad, values)
            delta = jnp.sum(probability * grad_prob, -1, keepdims=True)
            grad_scores = jnp.where(visible, probability * (grad_prob - delta), 0.0).astype(BF)
            grad_queries.append(dot(grad_scores, keys))
            key_more = contract_rows(grad_scores, query)
            value_more = contract_rows(probability.astype(BF), grad)
            key_term = key_more if key_term is None else key_term + key_more
            value_term = value_more if value_term is None else value_term + value_more
        scale = HD ** (-0.5)
        grad_proj[low : low + size, lane : lane + 2 * HD] = scale * jnp.where(
            lane_index(grad_queries[0].shape) < HD, grad_queries[0], grad_queries[1]
        )
        if low == 0 and lane == 0:
            key_acc[...] = key_term * scale
            value_acc[...] = value_term
        else:
            key_acc[...] += key_term * scale
            value_acc[...] += value_term

    def rotate_back(sequence):
        keys, values = key_acc[...], value_acc[...]
        grad_proj[:, query_cols:] = jnp.where(
            lane_index(keys.shape) < HD, keys + pltpu.roll(keys, HD, 1), values + pltpu.roll(values, HD, 1)
        )
        for low in range(0, total_rows, 256):
            size = min(256, total_rows - low)
            grads = grad_proj[low : low + size, :]
            back = grads * cos_ref[low : low + size, :] + turned(grads * sin_ref[low : low + size, :])
            at = sequence * total_rows + low
            dqkv[at : at + size, :] = back.astype(BF)

    def entry_terms(chunk):
        mine = jnp.concatenate(
            [
                dqkv[(c * line + z) * block_rows + chunk * rows : (c * line + z) * block_rows + (chunk + 1) * rows, :]
                for c in range(pair)
                for z in range(line)
            ],
            0,
        )
        for low in range(0, width, 512):
            term = contract_cols(mine, low_w[low : low + 512, :qkv_cols]).astype(BF)
            part[chunk, :, :, :, low : low + 512] = term.reshape(pair, line, rows, 512)

    def norm_rows_back(chunk):
        at = slice(chunk * rows, (chunk + 1) * rows)
        values = hidden_ref[at, :].astype(F32)
        inverse = lax.rsqrt(jnp.mean(values * values, -1, keepdims=True) + EPS_NORM)
        normed = values * inverse
        grad_entry = total[...]
        gain_term = jnp.sum(grad_entry * normed, 0, keepdims=True)
        if chunk == 0:
            gain_grad_ref[...] = gain_term
        else:
            gain_grad_ref[...] += gain_term
        grad_normed = grad_entry * gain_ref[...]
        grad_rows = inverse * (
            grad_normed - normed * jnp.mean(grad_normed * normed, -1, keepdims=True)
        )
        grad_hidden_ref[at, :] = (grad_mid_ref[at, :] + grad_rows).astype(BF)

    steps = []

    def step(time, function, *values):
        steps.append((time, functools.partial(function, *values)))

    step(0.0, loads["dgu"].wait)
    step(0.0, loads["act"].wait)
    period, before = 26.0, 24.0
    for tick in range(line):
        arrived = before + period * tick
        issued = 5.0 * (tick + 1) if tick < 2 else before + period * (tick - 2) + 0.5
        step(issued - 5.0 if tick < 2 else issued - 5.5, multiply, tick)
        step(issued, ffn.send_one, tick)
        step(arrived, ffn.sum_one, tick)
        step(arrived + 12.0, ffn.sum_two, tick)
    now = 10.5
    step(now, back_to_heads)
    now += 3.0
    for sequence in range(tokens // total_rows):
        size = query_rows(total_rows)
        for low in range(0, total_rows, size):
            for lane in range(0, query_cols, 2 * HD):
                step(now, attention_part, sequence, low, size, lane)
                now += 6.0
        step(now, rotate_back, sequence)
        now += 0.5
    now = max(now, before + period * (line - 3) + 0.6)
    step(now, loads["heads"].wait)
    for chunk in range(chunks):
        step(now + 0.5 + chunk, entry_terms, chunk)
    begin = now + 1.0
    for chunk, one in enumerate(sums):
        start = begin + chunk * (line - 1) * SEND
        more, finish = one.plan(start, total, functools.partial(norm_rows_back, chunk))
        steps += more
    step(finish + 0.2, gain_sum.begin, gain_grad_ref, gain_two_ref)
    step(finish + 4.0, gain_sum.second)
    step(finish + 8.0, gain_sum.third)
    step(finish + 12.0, gain_sum.end)
    now += 1.0 + chunks
    for tick in range(line):
        step(now + tick, multiply, line + tick)
        step(now + tick + 0.5, att.send_one, tick)
        arrived = max(now + 30.0 + 2.0 * tick, before + period * (line - 2) + 1.0 + 2.0 * tick)
        step(arrived, att.sum_one, tick)
        step(arrived + 12.5, att.sum_two, tick)
    run_steps(steps)
    for one in sums + [ffn, att]:
        one.drain()


def closing(sizes, collective_id, factors, low, hidden, grad_mid, gain, grad_gain_two, tables):
    line, pair = sizes["ctx"], sizes["core"]
    group = line * pair
    block_rows, width = hidden.shape
    tokens = block_rows * group
    chunks = 4
    rows = block_rows // chunks
    own_rows = width // (group * sizes["dp"] * sizes["x"])
    units = factors[3].shape[1]
    qkv_cols, query_cols = factors[6].shape[1], factors[7].shape[1]
    total_rows = tables[0].shape[0]
    pieces = grad_pieces(sizes)
    any_spec = pl.BlockSpec(memory_space=pl.ANY)
    vmem = pl.BlockSpec(memory_space=pltpu.VMEM)
    dma = pltpu.SemaphoreType.DMA
    shape = jax.ShapeDtypeStruct
    across = sizes["x"] * pair * own_rows
    branch_rows = 128
    part_shape = (chunks, pair, line, rows, width)
    factors = list(factors)
    factors[1] = factors[1].reshape(part_shape)
    return pl.pallas_call(
        functools.partial(closing_kernel, sizes, chunks),
        out_shape=[shape((own_rows, group * w), BF) for _, w, _ in pieces]
        + [shape((block_rows, width), BF), shape((8, 128), F32)],
        in_specs=[any_spec] * 6 + [vmem] + [any_spec] * 2 + [vmem] * 8,
        out_specs=[any_spec] * len(pieces) + [vmem] * 2,
        scratch_shapes=[
            pltpu.VMEM((2, 2, sizes["dp"], tokens, across), BF),
            pltpu.VMEM(part_shape, BF),
            pltpu.VMEM((tokens, units), BF),
            pltpu.VMEM((tokens, qkv_cols), BF),
            pltpu.VMEM((tokens, query_cols), BF),
            pltpu.VMEM((2, branch_rows, width), BF),
            pltpu.VMEM((width, qkv_cols + query_cols), BF),
            pltpu.VMEM((tokens, query_cols), BF),
            pltpu.VMEM((total_rows, qkv_cols), F32),
            pltpu.VMEM((total_rows, 2 * HD), F32),
            pltpu.VMEM((total_rows, 2 * HD), F32),
            *Reduce.room(line, pair, rows, width, chunks)[1:],
            pltpu.VMEM((rows, width), F32),
            dma((4,)),
            dma((2, 2, sizes["dp"])),
            dma((2,)),
            *Collect.room(sizes, own_rows, 3 * units),
            *Collect.room(sizes, own_rows, qkv_cols + query_cols),
            *Collect.sems(sizes, 3),
            *Collect.sems(sizes, 3),
            *Reduce.sems(chunks)(line),
            pltpu.VMEM((1, width), F32),
            *GainSum.room(sizes, width),
            *GainSum.sems(sizes),
        ],
        compiler_params=pltpu.CompilerParams(
            collective_id=collective_id, has_side_effects=True, vmem_limit_bytes=63 * 2**20
        ),
    )(*factors, low, hidden, grad_mid, gain, grad_gain_two, *tables)


def grad_pieces(sizes):
    group = sizes["ctx"] * sizes["core"]
    heads, keys, units = H * HD // group, KV * HD // group, FF // group
    pieces, offset = [], 0
    for name, width in (
        ("gate", units),
        ("up", units),
        ("down", units),
        ("query", heads),
        ("key_value", 2 * keys),
        ("out", heads),
    ):
        pieces.append((name, width, offset))
        offset += width
    return pieces


def adamw_kernel(step_rate, decay_rate, grad_ref, weight_ref, state_ref, grad_out, weight_out, state_out):
    gradient = grad_ref[...].astype(F32)
    grad_out[...] = gradient
    updated, states = adamw(weight_ref[...], gradient, state_ref[...], step_rate, decay_rate)
    weight_out[...] = updated
    state_out[...] = states


def adamw_columns(gradient, weight, states, step_rate, decay_rate):
    rows, columns = weight.shape
    step = math.gcd(columns, 1024)
    flat = pl.BlockSpec((rows, step), lambda i: (0, i))
    deep = pl.BlockSpec((2, rows, step), lambda i: (0, 0, i))
    return pl.pallas_call(
        functools.partial(adamw_kernel, step_rate, decay_rate),
        grid=(columns // step,),
        out_shape=[
            jax.ShapeDtypeStruct(weight.shape, F32),
            jax.ShapeDtypeStruct(weight.shape, F32),
            jax.ShapeDtypeStruct(states.shape, F32),
        ],
        in_specs=[flat, flat, deep],
        out_specs=[flat, flat, deep],
    )(gradient, weight, states)


def dot(left, right):
    return jnp.dot(left, right, preferred_element_type=F32)


def shards(
    sizes,
    hidden,
    cotangent,
    span_order,
    norm_gains,
    w_qkv,
    w_out,
    w_gate_up,
    w_down,
    mom_gains,
    mom_qkv,
    mom_out,
    mom_gate_up,
    mom_down,
):
    everyone = ("dp", "ctx", "x", "core")
    line, pair = sizes["ctx"], sizes["core"]
    group = line * pair
    block_rows, width = hidden.shape[1:]
    total_rows = block_rows * line
    span_rows = total_rows // span_order.shape[0]
    heads, kv_heads = H // group, KV // group
    query_cols, kv_cols = heads * HD, kv_heads * HD
    key_pos = (
        span_order[:, None] * span_rows + jnp.arange(span_rows, dtype=jnp.int32)[None, :]
    ).reshape(-1)
    cos_tab, sin_tab = rope_table(key_pos)
    signs = jnp.where(jnp.arange(HD) < HD // 2, -1.0, 1.0)
    cosines = jnp.concatenate([cos_tab] * (heads + kv_heads) + [jnp.ones_like(cos_tab)] * kv_heads, 1)
    sines = jnp.concatenate(
        [sin_tab * signs] * (heads + kv_heads) + [jnp.zeros_like(sin_tab)] * kv_heads, 1
    )
    tables = (cosines, sines, key_pos[:, None], key_pos[None, :])
    weights = (w_qkv, w_out, w_gate_up, w_down)
    output, grad_middle, grad_gain_two, gains, low, rest = opening(
        sizes, 0, weights, norm_gains, hidden[0], cotangent[0], tables
    )
    entry_one, qkv, attended, grad_branch, entry_two, cot, activated, grad_gu = rest
    gain_one = gains[:1]
    factors = (entry_two, grad_gu, cot, activated, entry_one, grad_branch, qkv, attended)
    *pieces, grad_hidden, gain_sums = closing(
        sizes, 1, factors, low, hidden[0], grad_middle, gain_one, grad_gain_two, tables
    )
    grad_gate, grad_up, grad_down, grad_query, grad_key_value, grad_out = pieces
    output, grad_hidden = output[None], grad_hidden[None]
    rows = w_qkv.shape[0]
    place = lax.axis_index(everyone) * rows
    grad_gains = lax.dynamic_slice(gain_sums, (0, lax.rem(place, 128)), (2, rows))
    grad_key_value = grad_key_value.reshape(rows, group, 2, kv_cols).transpose(0, 2, 1, 3)
    grad_qkv = jnp.concatenate([grad_query, grad_key_value.reshape(rows, -1)], 1)
    grad_gate_up = jnp.concatenate([grad_gate, grad_up], 1)
    new_gains, new_mom_gains = adamw(norm_gains, grad_gains, mom_gains, LR_GAIN, 0.0)
    grad_qkv, new_qkv, new_mom_qkv = adamw_columns(grad_qkv, w_qkv, mom_qkv, LR_MATRIX, DECAY_MATRIX)
    grad_out, new_out, new_mom_out = adamw_columns(grad_out, w_out, mom_out, LR_OUTPUT, DECAY_MATRIX)
    grad_gate_up, new_gate_up, new_mom_gate_up = adamw_columns(
        grad_gate_up, w_gate_up, mom_gate_up, LR_MATRIX, DECAY_MATRIX
    )
    grad_down, new_down, new_mom_down = adamw_columns(
        grad_down, w_down, mom_down, LR_MATRIX, DECAY_MATRIX
    )
    return (
        output,
        grad_hidden,
        grad_gains,
        grad_qkv,
        grad_out,
        grad_gate_up,
        grad_down,
        new_gains,
        new_qkv,
        new_out,
        new_gate_up,
        new_down,
        new_mom_gains,
        new_mom_qkv,
        new_mom_out,
        new_mom_gate_up,
        new_mom_down,
    )


def solution(mesh):
    shape = dict(mesh.shape)
    pair = 2 if shape["ctx"] * 2 <= KV and shape["fsdp"] % 2 == 0 else 1
    sizes = {"dp": shape["dp"], "ctx": shape["ctx"], "x": shape["fsdp"] // pair, "core": pair}
    finer = Mesh(mesh.devices.reshape(tuple(sizes.values())), tuple(sizes))
    tokens = P(("dp", "x", "core"), "ctx", None)
    everyone = ("dp", "ctx", "x", "core")
    rows, gains = P(everyone, None), P(None, everyone)
    row_moments, gain_moments = P(None, everyone, None), P(None, None, everyone)
    weights = (gains, rows, rows, rows, rows)
    moments = (gain_moments, row_moments, row_moments, row_moments, row_moments)
    return jax.shard_map(
        functools.partial(shards, sizes),
        mesh=finer,
        in_specs=(tokens, tokens, P()) + weights + moments,
        out_specs=(tokens, tokens) + weights + weights + moments,
        check_vma=False,
    )
```

```python
import functools
import math

import jax
import jax.numpy as jnp
from jax import lax
from jax.experimental import pallas as pl
from jax.experimental.pallas import tpu as pltpu
from jax.sharding import Mesh
from jax.sharding import PartitionSpec as P

MESH = pl.DeviceIdType.MESH
BF = jnp.bfloat16
F32 = jnp.float32
H = 32
KV = 8
HD = 64
FF = 8192


EPS_NORM = 1e-05
NEG_FILL = -1000000000.0
THETA = 500000.0
BETA_ONE = 0.9
BETA_TWO = 0.95
ADAM_EPS = 1e-08
DECAY_MATRIX = 0.1
LR_MATRIX = 0.01
LR_OUTPUT = 0.06
LR_GAIN = 0.3


def rope_table(positions):
    half_dim = HD // 2
    index_row = jnp.arange(half_dim, dtype=jnp.float32)
    frequency = jnp.exp(-(2.0 * index_row / HD) * math.log(THETA))
    wavelen = 2.0 * math.pi / frequency
    smooth = (8192.0 / wavelen - 1.0) / 3.0
    scaled = jnp.where(
        wavelen < 2048.0,
        frequency,
        jnp.where(
            wavelen > 8192.0,
            frequency / 32.0,
            (1.0 - smooth) * frequency / 32.0 + smooth * frequency,
        ),
    )
    angles = positions.astype(jnp.float32)[:, None] * scaled[None, :]
    cosine = jnp.cos(angles)
    sine_part = jnp.sin(angles)
    return (jnp.concatenate([cosine, cosine], 1), jnp.concatenate([sine_part, sine_part], 1))


def adamw(weight, gradient, states, step_rate, decay_rate):
    first_mom = BETA_ONE * states[0] + (1.0 - BETA_ONE) * gradient
    root_mom = jnp.sqrt(BETA_TWO * states[1] * states[1] + (1.0 - BETA_TWO) * gradient * gradient)
    first_hat = first_mom / (1.0 - BETA_ONE**3)
    root_hat = root_mom / math.sqrt(1.0 - BETA_TWO**3)
    updated = weight - step_rate * (first_hat / (root_hat + ADAM_EPS) + decay_rate * weight)
    return (updated, jnp.stack([first_mom, root_mom]))


def contract_rows(left_arr, right_arr):
    return lax.dot_general(
        left_arr, right_arr, (((0,), (0,)), ((), ())), preferred_element_type=jnp.float32
    )


def contract_cols(left_arr, right_arr):
    return lax.dot_general(
        left_arr, right_arr, (((1,), (1,)), ((), ())), preferred_element_type=jnp.float32
    )


def wrap(value, size):
    return lax.rem(value + size, size)


def remote(src, dst, send_sem, recv_sem, **where):
    return pltpu.make_async_remote_copy(
        src_ref=src,
        dst_ref=dst,
        send_sem=send_sem,
        recv_sem=recv_sem,
        device_id=where,
        device_id_type=MESH,
    )


def greet(places):
    barrier = pltpu.get_barrier_semaphore()
    for where in places:
        pl.semaphore_signal(barrier, inc=1, device_id=where, device_id_type=MESH)
    pl.semaphore_wait(barrier, len(places))


def greet_line(line, pair):
    barrier = pltpu.get_barrier_semaphore()
    here = lax.axis_index("ctx")

    @pl.when(here > 0)
    def _():
        pl.semaphore_signal(barrier, inc=1, device_id={"ctx": here - 1}, device_id_type=MESH)

    @pl.when(here < line - 1)
    def _():
        pl.semaphore_signal(barrier, inc=1, device_id={"ctx": here + 1}, device_id_type=MESH)

    if pair > 1:
        pl.semaphore_signal(
            barrier, inc=1, device_id={"core": 1 - lax.axis_index("core")}, device_id_type=MESH
        )
    ends = (here == 0).astype(jnp.int32) + (here == line - 1).astype(jnp.int32)
    pl.semaphore_wait(barrier, 2 - ends + (1 if pair > 1 else 0))


class Travel:
    @staticmethod
    def sems(many, line):
        return [pltpu.SemaphoreType.DMA((many,))] + [pltpu.SemaphoreType.DMA((many, 2, line))] * 4

    def __init__(self, line, pair, ins, outs, own_sem, line_send, line_recv, core_send, core_recv):
        self.line, self.pair, self.ins, self.outs = line, pair, ins, outs
        self.own_sem, self.line_sems, self.core_sems = own_sem, (line_send, line_recv), (core_send, core_recv)
        self.here = lax.axis_index("ctx")
        self.core = lax.axis_index("core")

    def block(self, way, step):
        return self.here - 1 - step if way == 0 else self.here + 1 + step

    def copy(self, sems, at, source, place, **where):
        return remote(place if source is None else source, place, sems[0].at[at], sems[1].at[at], **where)

    def hop(self, item, way, step, source=None):
        place = self.outs[item](self.core, self.block(way, step - 1))
        target = self.here + 1 if way == 0 else self.here - 1
        return self.copy(self.line_sems, (item, way, step), source, place, ctx=target)

    def arrived(self, item, way, step):
        place = self.outs[item](self.core, self.block(way, step))
        return self.copy(self.line_sems, (item, way, step), None, place, ctx=self.here)

    def share(self, item, way, step, source=None):
        place = self.outs[item](self.core, self.block(way, step))
        return self.copy(self.core_sems, (item, way, step + 1), source, place, core=1 - self.core)

    def shared(self, item, way, step):
        place = self.outs[item](1 - self.core, self.block(way, step))
        return self.copy(self.core_sems, (item, way, step + 1), None, place, core=1 - self.core)

    def own(self, item):
        place = self.outs[item](self.core, self.here)
        return pltpu.make_async_copy(self.ins[item], place, self.own_sem.at[item])

    def sends(self, way):
        return self.here < self.line - 1 if way == 0 else self.here > 0

    def has(self, way, step):
        return self.block(way, step) >= 0 if way == 0 else self.block(way, step) <= self.line - 1

    def begin(self):
        for item in range(len(self.ins)):
            for way in range(2):

                @pl.when(self.sends(way))
                def _(item=item, way=way):
                    self.hop(item, way, 0, self.ins[item]).start()

            if self.pair > 1:
                self.share(item, 0, -1, self.ins[item]).start()
            if self.ins[item] is not None:
                self.own(item).start()

    def step(self, step):
        for item in range(len(self.ins)):
            for way in range(2):

                @pl.when(self.has(way, step))
                def _(item=item, way=way):
                    self.arrived(item, way, step).wait_recv()
                    if step + 1 < self.line - 1:

                        @pl.when(self.sends(way))
                        def _():
                            self.hop(item, way, step + 1).start()

                    if self.pair > 1:
                        self.share(item, way, step).start()

    def end(self):
        for item in range(len(self.ins)):
            if self.ins[item] is not None:
                self.own(item).wait()
            if self.pair > 1:
                self.share(item, 0, -1, self.ins[item]).wait_send()
                self.shared(item, 0, -1).wait_recv()
            for way in range(2):

                @pl.when(self.sends(way))
                def _(item=item, way=way):
                    self.hop(item, way, 0, self.ins[item]).wait_send()

                for step in range(self.line - 1):

                    @pl.when(self.has(way, step))
                    def _(item=item, way=way, step=step):
                        if step + 1 < self.line - 1:

                            @pl.when(self.sends(way))
                            def _():
                                self.hop(item, way, step + 1).wait_send()

                        if self.pair > 1:
                            self.share(item, way, step).wait_send()
                            self.shared(item, way, step).wait_recv()


def add_rows(rows, out_ref, *parts):
    def one(index, carry):
        at = pl.ds(pl.multiple_of(index * 16, 16), 16)
        total = parts[0][at, :].astype(F32)
        for part in parts[1:]:
            total = total + part[at, :].astype(F32)
        out_ref[at, :] = total.astype(out_ref.dtype)
        return carry

    lax.fori_loop(0, rows // 16, one, 0)


class Reduce:
    @staticmethod
    def sems(*outer):
        dma = pltpu.SemaphoreType.DMA
        return lambda line: [dma(outer), dma(outer), dma(outer + (2, line)), dma(outer + (2, line))]

    @staticmethod
    def room(line, pair, rows, columns, *outer):
        return [
            pltpu.VMEM(outer + (pair, line, rows, columns), BF),
            pltpu.VMEM(outer + (line, rows, columns), BF),
            pltpu.VMEM(outer + (line + 1, rows, columns), BF),
        ]

    def __init__(self, line, pair, part, near, landed, core_send, core_recv, line_send, line_recv, at, kind=None):
        self.line, self.pair, self.at = line, pair, at
        self.sem_at = at if kind is None else (kind, at[-1])
        self.part, self.near, self.landed = part, near, landed
        self.core_sems, self.line_sems = (core_send, core_recv), (line_send, line_recv)
        self.here, self.core = lax.axis_index("ctx"), lax.axis_index("core")
        self.rows = part.shape[-2]

    def mine(self, block):
        return self.part.at[self.at + (self.core, block)]

    def across(self):
        return remote(
            self.part.at[self.at + (1 - self.core,)],
            self.near.at[self.at],
            self.core_sems[0].at[self.sem_at],
            self.core_sems[1].at[self.sem_at],
            core=1 - self.core,
        )

    def slot(self, way, block):
        return self.landed.at[self.at + (block + 1 if way == 0 else block,)]

    def onward(self, way, block, here):
        index = self.sem_at + (way, block)
        return remote(
            self.mine(block),
            self.slot(way, block),
            self.line_sems[0].at[index],
            self.line_sems[1].at[index],
            ctx=here + 1 if way == 0 else here - 1,
        )

    def begin(self):
        if self.pair > 1:
            self.across().start()

    def settle(self):
        if self.pair > 1:
            self.across().wait_recv()

    def terms(self, block):
        return [self.mine(block)] + ([self.near.at[self.at + (block,)]] if self.pair > 1 else [])

    def relay(self, way, block, here):
        @pl.when(self.here == here)
        def _():
            terms = self.terms(block)
            if here != (0 if way == 0 else self.line - 1):
                self.onward(way, block, here).wait_recv()
                terms.append(self.slot(way, block))
            if len(terms) > 1:
                add_rows(self.rows, self.mine(block), *terms)
            self.onward(way, block, here).start()

    def finish(self, here, total_ref):
        @pl.when(self.here == here)
        def _():
            terms = self.terms(here)
            for way, has in ((0, here > 0), (1, here < self.line - 1)):
                if has:
                    self.onward(way, here, here).wait_recv()
                    terms.append(self.slot(way, here))
            add_rows(self.rows, total_ref, *terms)

    def drain(self):
        if self.pair > 1:
            self.across().wait_send()
        for here in range(self.line):

            @pl.when(self.here == here)
            def _(here=here):
                for block in range(self.line):
                    if block != here:
                        self.onward(0 if block > here else 1, block, here).wait_send()

    def plan(self, start, total_ref, after):
        ends, steps = self.line - 1, [(start, self.begin), (start + LAG, self.settle)]
        for way in range(2):
            for block in range(self.line):
                for here in range(self.line):
                    if here < block if way == 0 else here > block:
                        wait = ends - block if way == 0 else block
                        depth = here if way == 0 else ends - here
                        when = start + LAG + wait * SEND + depth * HOP
                        steps.append((when, functools.partial(self.relay, way, block, here)))
        finish = start + LAG + ends * HOP + 0.5
        for here in range(self.line):
            steps.append((finish, functools.partial(self.finish, here, total_ref)))
        steps.append((finish, after))
        return steps, finish


SEND, HOP, LAG = 4.0, 7.0, 5.0


def run_steps(steps):
    for _, step in sorted(steps, key=lambda item: item[0]):
        step()


def blocks_in_order(line, pair):
    away = sorted(range(line), key=lambda d: min(d, line - d))
    return [(dz, dc) for dz in away for dc in range(pair)]


def greet_all(sizes):
    names = ("dp", "ctx", "x", "core")
    at = {name: lax.axis_index(name) for name in names}
    places = []
    for dz, dc in blocks_in_order(sizes["ctx"], sizes["core"]):
        if dz or dc:
            places.append(
                {"ctx": wrap(at["ctx"] + dz, sizes["ctx"]), "core": wrap(at["core"] + dc, sizes["core"])}
            )
    for name in ("dp", "x"):
        for step in range(1, sizes[name]):
            places.append({name: wrap(at[name] + step, sizes[name])})
    greet(places)


class Spread:
    @staticmethod
    def sems(sizes):
        dma = pltpu.SemaphoreType.DMA
        group, steps = sizes["ctx"] * sizes["core"], max(sizes["dp"], sizes["x"])
        return [dma((1,))] + [dma((group,))] * 2 + [dma((group, steps))] * 2 + [dma((group, steps, steps))] * 2

    def __init__(self, sizes, pack, out, sems):
        self.sizes, self.pack, self.out = sizes, pack, out
        self.own_sem, *rest = sems
        self.f_sems, self.a_sems, self.b_sems = rest[0:2], rest[2:4], rest[4:6]
        self.line, self.pair = sizes["ctx"], sizes["core"]
        self.at = {name: lax.axis_index(name) for name in ("dp", "ctx", "x", "core")}
        self.order = blocks_in_order(self.line, self.pair)

    def spot(self, dp, z, x, c):
        return self.out.at[dp * self.line + z, x * self.pair + c]

    def mine(self):
        return self.spot(*[self.at[name] for name in ("dp", "ctx", "x", "core")])

    def copy(self, sems, at, source, target, **where):
        return remote(source, target, *[sem.at[at] for sem in sems], **where)

    def first(self, index):
        dz, dc = self.order[index]
        z, c = wrap(self.at["ctx"] + dz, self.line), wrap(self.at["core"] + dc, self.pair)
        return self.copy(self.f_sems, index, self.pack.at[z * self.pair + c], self.mine(), ctx=z, core=c)

    def place(self, index, moved):
        dz, dc = self.order[index]
        z, c = wrap(self.at["ctx"] - dz, self.line), wrap(self.at["core"] - dc, self.pair)
        dp, x = [wrap(self.at[name] - moved.get(name, 0), self.sizes[name]) for name in ("dp", "x")]
        return self.spot(dp, z, x, c)

    def axes(self, index):
        return ("x", "dp") if sum(self.order[index]) % 2 == 0 else ("dp", "x")

    def ahead(self, name, step):
        return {name: wrap(self.at[name] + step, self.sizes[name])}

    def came(self, index):
        spot = self.place(index, {})
        return self.copy(self.f_sems, index, spot, spot, core=self.at["core"])

    def hop_one(self, index, step):
        spot = self.place(index, {})
        return self.copy(self.a_sems, (index, step), spot, spot, **self.ahead(self.axes(index)[0], step))

    def one_came(self, index, step):
        spot = self.place(index, {self.axes(index)[0]: step})
        return self.copy(self.a_sems, (index, step), spot, spot, core=self.at["core"])

    def hop_two(self, index, step, far):
        name, other = self.axes(index)
        spot = self.place(index, {name: step})
        return self.copy(self.b_sems, (index, step, far), spot, spot, **self.ahead(other, far))

    def two_came(self, index, step, far):
        name, other = self.axes(index)
        spot = self.place(index, {name: step, other: far})
        return self.copy(self.b_sems, (index, step, far), spot, spot, core=self.at["core"])

    def own(self):
        source = self.pack.at[self.at["ctx"] * self.pair + self.at["core"]]
        return pltpu.make_async_copy(source, self.mine(), self.own_sem.at[0])

    def begin(self, *indices):
        for index in indices:
            if index == 0:
                self.own().start()
            elif index < len(self.order):
                self.first(index).start()

    def onward(self, index, *more):
        if index == 0:
            self.own().wait()
        else:
            self.came(index).wait_recv()
        self.begin(*more)
        name, other = self.axes(index)
        for step in range(1, self.sizes[name]):
            self.hop_one(index, step).start()
        for far in range(1, self.sizes[other]):
            self.hop_two(index, 0, far).start()

    def onward_two(self, index):
        name, other = self.axes(index)
        for step in range(1, self.sizes[name]):
            self.one_came(index, step).wait_recv()
            for far in range(1, self.sizes[other]):
                self.hop_two(index, step, far).start()

    def complete(self, *indices):
        for index in indices:
            name, other = self.axes(index)
            for step in range(self.sizes[name]):
                for far in range(1, self.sizes[other]):
                    self.two_came(index, step, far).wait_recv()

    def drain(self):
        for index in range(len(self.order)):
            name, other = self.axes(index)
            if index:
                self.first(index).wait_send()
            for step in range(self.sizes[name]):
                if step:
                    self.hop_one(index, step).wait_send()
                for far in range(1, self.sizes[other]):
                    self.hop_two(index, step, far).wait_send()


class Collect:
    AXES = (("dp", "x"), ("x", "dp"))

    @staticmethod
    def room(sizes, rows, width):
        room = [pltpu.VMEM((sizes["ctx"], sizes["dp"], sizes["x"], sizes["core"], rows, width), BF)]
        for parity, (name, other) in enumerate(Collect.AXES):
            count = sum((dz + dc) % 2 == parity for dz, dc in blocks_in_order(sizes["ctx"], sizes["core"]))
            room.append(pltpu.VMEM((max(1, count), (sizes[name] - 1) * sizes[other], rows, width), BF))
            room.append(pltpu.VMEM((max(1, count), sizes[other] - 1, rows, width), BF))
        return room

    @staticmethod
    def sems(sizes, pieces):
        dma = pltpu.SemaphoreType.DMA
        group, steps = sizes["ctx"] * sizes["core"], max(sizes["dp"], sizes["x"])
        return (
            [dma((pieces,))]
            + [dma((group, steps, steps))] * 2
            + [dma((group, steps))] * 2
            + [dma((group, pieces))] * 2
        )

    def __init__(self, sizes, widths, pieces, room, sems):
        self.sizes, self.widths, self.pieces = sizes, widths, pieces
        self.terms = room[0]
        self.near, self.far_in = room[1::2], room[2::2]
        self.own_sem, *rest = sems
        self.a_sems, self.b_sems, self.f_sems = rest[0:2], rest[2:4], rest[4:6]
        self.line, self.pair = sizes["ctx"], sizes["core"]
        self.rows = self.terms.shape[-2]
        self.at = {name: lax.axis_index(name) for name in ("dp", "ctx", "x", "core")}
        self.me = self.at["ctx"] * self.pair + self.at["core"]
        self.away = sorted(range(self.line), key=lambda d: (d != 0, -min(d, self.line - d)))
        self.order = [(dz, dc) for dz in self.away for dc in range(self.pair)]

    def spot_of(self, index, sign=1):
        dz, dc = self.order[index]
        return wrap(self.at["ctx"] + sign * dz, self.line), wrap(self.at["core"] + sign * dc, self.pair)

    def parity(self, index):
        return sum(self.order[index]) % 2

    def axes(self, index):
        return self.AXES[self.parity(index)]

    def slot(self, index):
        return sum(self.parity(before) == self.parity(index) for before in range(index))

    def indices(self, tick):
        return range(tick * self.pair, (tick + 1) * self.pair)

    def lanes(self, tick, dp):
        across = self.sizes["x"] * self.pair * self.rows
        z = wrap(self.at["ctx"] + self.away[tick], self.line)
        return pl.ds(pl.multiple_of((dp * self.line + z) * across, 128), across)

    def multiply(self, tick, item, left, right):
        start, width = sum(self.widths[:item]), self.widths[item]
        step = math.gcd(width, 512)

        @pl.loop(0, self.sizes["dp"])
        def _(dp):
            left_t = left[dp].T

            @pl.loop(0, width // step)
            def _(part):
                columns = pl.ds(pl.multiple_of(part * step, 128), step)
                into = pl.ds(pl.multiple_of(start + part * step, 128), step)
                product = dot(left_t, right[:, columns]).astype(BF)
                for x in range(self.sizes["x"]):
                    for core in range(self.pair):
                        low = (x * self.pair + core) * self.rows
                        self.terms[tick, dp, x, core, :, into] = product[low : low + self.rows]

    def block_terms(self, index, first_at, other_at):
        name, other = self.axes(index)
        spot = {name: first_at, other: other_at}
        return self.terms.at[index // self.pair, spot["dp"], spot["x"], self.spot_of(index)[1]]

    def landing(self, index, step, place):
        at = (step - 1) * self.sizes[self.axes(index)[1]] + place
        return self.near[self.parity(index)].at[self.slot(index), at]

    def far_landing(self, index, far):
        return self.far_in[self.parity(index)].at[self.slot(index), far - 1]

    def hop_one(self, index, step, place):
        name = self.axes(index)[0]
        to = wrap(self.at[name] + step, self.sizes[name])
        sems = [sem.at[index, step, place] for sem in self.a_sems]
        return remote(
            self.block_terms(index, to, place), self.landing(index, step, place), *sems, **{name: to}
        )

    def hop_two(self, index, far):
        name, other = self.axes(index)
        to = wrap(self.at[other] + far, self.sizes[other])
        sems = [sem.at[index, far] for sem in self.b_sems]
        return remote(
            self.block_terms(index, self.at[name], to), self.far_landing(index, far), *sems, **{other: to}
        )

    def done(self, index):
        name, other = self.axes(index)
        return self.block_terms(index, self.at[name], self.at[other])

    def stays(self, index):
        return self.order[index] == (0, 0)

    def piece_at(self, piece, member):
        out, width, _ = self.pieces[piece]
        return out.at[:, pl.ds(pl.multiple_of(member * width, 128), width)]

    def last(self, index, piece):
        z, c = self.spot_of(index)
        _, width, offset = self.pieces[piece]
        source = self.done(index).at[:, pl.ds(offset, width)]
        target = self.piece_at(piece, self.me)
        if self.stays(index):
            return pltpu.make_async_copy(source, target, self.own_sem.at[piece])
        return remote(source, target, *[sem.at[index, piece] for sem in self.f_sems], ctx=z, core=c)

    def last_came(self, index, piece):
        z, c = self.spot_of(index, -1)
        spot = self.piece_at(piece, z * self.pair + c)
        sems = [sem.at[index, piece] for sem in self.f_sems]
        return remote(spot, spot, *sems, core=self.at["core"])

    def places(self, index):
        other = self.axes(index)[1]
        size = self.sizes[other]
        return [(far, wrap(self.at[other] + far, size)) for far in list(range(1, size)) + [0]]

    def send_one(self, tick):
        for index in self.indices(tick):
            for _, place in self.places(index):
                for step in range(1, self.sizes[self.axes(index)[0]]):
                    self.hop_one(index, step, place).start()

    def sum_one(self, tick):
        for index in self.indices(tick):
            name = self.axes(index)[0]
            for far, place in self.places(index):
                steps = range(1, self.sizes[name])
                for step in steps:
                    self.hop_one(index, step, place).wait_recv()
                kept = self.block_terms(index, self.at[name], place)
                add_rows(self.rows, kept, kept, *[self.landing(index, step, place) for step in steps])
                if far:
                    self.hop_two(index, far).start()

    def sum_two(self, tick):
        for index in self.indices(tick):
            fars = range(1, self.sizes[self.axes(index)[1]])
            for far in fars:
                self.hop_two(index, far).wait_recv()
            done = self.done(index)
            add_rows(self.rows, done, done, *[self.far_landing(index, far) for far in fars])
            for piece in range(len(self.pieces)):
                self.last(index, piece).start()

    def drain(self):
        for index in range(len(self.order)):
            name, other = self.axes(index)
            for step in range(1, self.sizes[name]):
                for place in range(self.sizes[other]):
                    self.hop_one(index, step, place).wait_send()
            for far in range(1, self.sizes[other]):
                self.hop_two(index, far).wait_send()
            for piece in range(len(self.pieces)):
                if self.stays(index):
                    self.last(index, piece).wait()
                else:
                    self.last(index, piece).wait_send()
                    self.last_came(index, piece).wait_recv()


def lane_index(shape):
    return lax.broadcasted_iota(jnp.int32, shape, len(shape) - 1)


def turned(values):
    half, columns = HD // 2, values.shape[1]
    ahead = pltpu.roll(values, columns - half, 1)
    behind = pltpu.roll(values, half, 1)
    return jnp.where(lane_index(values.shape) % HD < half, ahead, behind)


def for_heads(table, columns):
    pair = 2 * HD
    return jnp.concatenate([table[:, :pair]] * ((columns - pair) // pair) + [table[:, pair:]], 1)


def only_head(values, head):
    return jnp.where(lane_index(values.shape) // HD == head, values, jnp.zeros_like(values))


def both_halves(values, head):
    wide = values.astype(F32)
    return jnp.where(lane_index(wide.shape) // HD == head, wide, pltpu.roll(wide, HD, 1)).astype(BF)


def softmax_rows(queries, keys, visible):
    scores = contract_cols(queries, keys) * HD ** (-0.5)
    scores = jnp.where(visible, scores, NEG_FILL)
    exponent = jnp.exp(scores - jnp.max(scores, -1, keepdims=True))
    return exponent / jnp.sum(exponent, -1, keepdims=True)


def query_rows(total_rows):
    return min(total_rows, 2**17 // total_rows)


def opening_kernel(sizes, chunks, *refs):
    line, pair = sizes["ctx"], sizes["core"]
    group = line * pair
    refs = list(refs)

    def take(count):
        taken, refs[:count] = refs[:count], []
        return taken

    qkv_in, out_in, gate_up_in, down_in, gain_in, hidden_ref, cot_ref, cos_ref, sin_ref, pos_col, pos_row = take(11)
    output_ref, middle, gains_ref = take(3)
    low_out, entry_one_out, qkv_out, heads_out, terms_out, entry_two_out, cots_out, act_out, dgu_out = take(9)
    stage, tall, wide, low_w, ffn_w, rows_in, cots, qkv, heads, act, dgu = take(11)
    part, near, landed, total = take(4)
    stage_sem, out_sem, slot_sem, terms_sem = take(4)
    tall_sems, wide_sems, reduce_sems, hidden_sems, travel_sems = take(7), take(7), take(4), take(5), take(5)

    rows, width = part.shape[-2:]
    own_rows = tall.shape[1]
    block_rows = rows * chunks
    tokens = group * rows
    total_rows = cos_ref.shape[0]
    qkv_cols, query_cols = qkv.shape[1], heads.shape[-1]
    units = ffn_w.shape[-1] // 3
    groups = ffn_w.shape[0]
    core, here = lax.axis_index("core"), lax.axis_index("ctx")
    steps, travels, sums = [], [], []
    low, high = Spread(sizes, tall, low_w, tall_sems), Spread(sizes, wide, ffn_w, wide_sems)
    gain_rows = [gains_ref.at[pl.ds(0, 1)], gains_ref.at[pl.ds(1, 1)]]

    def step(time, function, *values):
        steps.append((time, functools.partial(function, *values)))

    def chunk_rows(chunk):
        return slice(chunk * rows, (chunk + 1) * rows)

    def staged(member):
        slot = member % 2
        sources = (
            gate_up_in.at[:, pl.ds(member * units, units)],
            gate_up_in.at[:, pl.ds(FF + member * units, units)],
            down_in.at[:, pl.ds(member * units, units)],
        )
        return [
            pltpu.make_async_copy(
                source, stage.at[slot, :, pl.ds(index * units, units)], stage_sem.at[slot, index]
            )
            for index, source in enumerate(sources)
        ]

    def pack_low():
        keys = KV * HD // group
        heads_of = H * HD // group
        for member in range(group):
            key_at, value_at = H * HD + member * keys, (H + KV) * HD + member * keys
            tall[member, :, :heads_of] = qkv_in[:, member * heads_of : (member + 1) * heads_of].astype(BF)
            both = jnp.concatenate(
                [qkv_in[:, key_at : key_at + keys], qkv_in[:, value_at : value_at + keys]], 1
            )
            tall[member, :, heads_of:qkv_cols] = both.astype(BF)
            tall[member, :, qkv_cols : qkv_cols + heads_of] = out_in[
                :, member * heads_of : (member + 1) * heads_of
            ].astype(BF)
            tall[member, :, qkv_cols + heads_of :] = gain_in[...].astype(BF)

    def pack_high():
        for member in range(group):
            for load in staged(member):
                load.wait()
            wide[member] = stage[member % 2].astype(BF)
            if member + 2 < group:
                for load in staged(member + 2):
                    load.start()

    def columns_of(weight, first, size):
        return weight[:, :, :, first : first + size].reshape(width, size)

    def rows_of(weight, index, count, first, size):
        each = groups // count
        return weight[index * each : (index + 1) * each, :, :, first : first + size].reshape(-1, size)

    def gains_to_rows():
        columns = columns_of(low_w, qkv_cols + query_cols, 128).astype(F32)
        gains_ref[...] = columns.T[:8, :]

    def project(sequence):
        weight = columns_of(low_w, 0, qkv_cols)

        @pl.loop(0, line)
        def _(z):
            values = rows_in[:, sequence, z].reshape(block_rows, width).astype(F32)
            inverse = lax.rsqrt(jnp.mean(values * values, -1, keepdims=True) + EPS_NORM)
            entry = (values * inverse * gain_rows[0][...]).astype(BF)
            rows_in[:, sequence, z] = entry.reshape(chunks, rows, width)
            projected = dot(entry, weight)
            table_at = pl.ds(pl.multiple_of(z * block_rows, block_rows), block_rows)
            cosine, sine = for_heads(cos_ref[table_at, :], qkv_cols), for_heads(sin_ref[table_at, :], qkv_cols)
            rotated = projected * cosine + turned(projected) * sine
            at = pl.ds(pl.multiple_of((sequence * line + z) * block_rows, block_rows), block_rows)
            qkv[at, :] = rotated.astype(BF)

    def attention(sequence, first, size, lane):
        start = sequence * total_rows
        both = qkv[start : start + total_rows, query_cols:]
        keys, values = both_halves(both, 0), both_halves(both, 1)
        visible = pos_row[...] <= pos_col[first : first + size, :]
        queries = qkv[start + first : start + first + size, lane : lane + 2 * HD]
        two = [
            dot(softmax_rows(only_head(queries, head), keys, visible).astype(BF), values)
            for head in range(2)
        ]
        merged = jnp.where(lane_index(two[0].shape) < HD, two[0], two[1]).astype(BF)
        from_z, to_z = first // block_rows, (first + size) // block_rows
        heads[sequence, from_z:to_z, :, lane : lane + 2 * HD] = merged.reshape(-1, block_rows, 2 * HD)

    def entry_one_copies():
        return [
            pltpu.make_async_copy(rows_in.at[:, c, z], entry_one_out.at[c, z], out_sem.at[3 + c * line + z])
            for c in range(pair)
            for z in range(line)
        ]

    whole_copies = [
        pltpu.make_async_copy(low_w, low_out, out_sem.at[0]),
        pltpu.make_async_copy(qkv, qkv_out, out_sem.at[1]),
        pltpu.make_async_copy(heads, heads_out, out_sem.at[2]),
    ]

    def chunk_copies(chunk):
        return [
            pltpu.make_async_copy(source, target.at[chunk], slot_sem.at[chunk, index])
            for index, (source, target) in enumerate(
                (
                    (act.at[chunk % 2], act_out),
                    (dgu.at[chunk % 2], dgu_out),
                    (rows_in.at[chunk], entry_two_out),
                    (cots.at[chunk], cots_out),
                )
            )
        ]

    def start_all(copies):
        for copy in copies:
            copy.start()

    def wait_all(copies):
        for copy in copies:
            copy.wait()

    def reducer(kind, chunk):
        one = Reduce(line, pair, part, near, landed, *reduce_sems, (kind // 2, chunk), kind)
        sums.append(one)
        return one

    def traveller(sems, source, place, start, hop):
        one = Travel(line, pair, [source], [place], *sems)
        steps.append((start, one.begin))
        for index in range(line - 1):
            steps.append((start + (index + 1) * hop, functools.partial(one.step, index)))
        finish = start + line * hop - 1.0
        steps.append((finish, one.end))
        return finish

    def product(chunk):
        mine = heads[:, :, chunk_rows(chunk), :].reshape(tokens, query_cols)
        for index in range(4):
            at = slice(index * (width // 4), (index + 1) * (width // 4))
            term = contract_cols(mine, rows_of(low_w, index, 4, qkv_cols, query_cols)).astype(BF)
            part[0, chunk, :, :, :, at] = term.reshape(pair, line, rows, -1)

    def norm_rows(chunk):
        mid = hidden_ref[chunk].astype(F32) + total[...]
        middle[chunk_rows(chunk), :] = mid
        inverse = lax.rsqrt(jnp.mean(mid * mid, -1, keepdims=True) + EPS_NORM)
        rows_in[chunk, core, here] = (mid * inverse * gain_rows[1][...]).astype(BF)

    def units_part(chunk, index, count):
        size = units // count
        slot = chunk % 2
        entry = rows_in[chunk].reshape(tokens, width)
        first, last = index * size, (index + 1) * size
        gate = dot(entry, columns_of(ffn_w, first, size))
        up = dot(entry, columns_of(ffn_w, units + first, size))
        grad_act = dot(cots[chunk].reshape(tokens, width), columns_of(ffn_w, 2 * units + first, size))
        sigmoid = 1.0 / (1.0 + jnp.exp(-gate))
        silu = gate * sigmoid
        act[slot, :, first:last] = (silu * up).astype(BF)
        dgu[slot, :, first:last] = (grad_act * up * sigmoid * (1.0 + gate * (1.0 - sigmoid))).astype(BF)
        dgu[slot, :, units + first : units + last] = (grad_act * silu).astype(BF)

    def back_part(chunk, index, count):
        size = width // count
        at = slice(index * size, (index + 1) * size)
        term = contract_cols(dgu[chunk % 2], rows_of(ffn_w, index, count, 0, 2 * units)).astype(BF)
        part[0, chunk, :, :, :, at] = term.reshape(pair, line, rows, size)

    def down_part(chunk, index, count):
        size = width // count
        at = slice(index * size, (index + 1) * size)
        term = contract_cols(act[chunk % 2], rows_of(ffn_w, index, count, 2 * units, units)).astype(BF)
        part[1, chunk, :, :, :, at] = term.reshape(pair, line, rows, size)

    def terms_copy(chunk):
        return pltpu.make_async_copy(part.at[0, chunk], terms_out.at[chunk], terms_sem.at[chunk])

    def write_output(chunk):
        output_ref[chunk_rows(chunk), :] = (middle[chunk_rows(chunk), :] + total[...]).astype(BF)

    for member in range(2):
        start_all(staged(member))
    greet_all(sizes)

    step(0.0, pack_low)
    hidden_done = traveller(
        hidden_sems, hidden_ref, lambda c, z: rows_in.at[:, c, z], 0.0, T_HIDDEN
    )
    step(0.1, low.begin, *range(group))
    step(0.2, pack_high)
    step(0.3, high.begin, *range(min(group, 4)))
    for index in range(group):
        when = 1.0 + T_LOW * (index // 2)
        step(when, low.onward, index)
        step(when + T_LOW + 1.0, low.onward_two, index)
        when = 1.0 + T_HIGH * (index // 2)
        step(when, high.onward, index, *([index + 2] if index >= 2 else []))
        step(when + T_HIGH * 0.6, high.onward_two, index)
    weights_there = 1.0 + T_HIGH * (group // 2) + 8.0

    now = max(hidden_done + 0.2, 1.0 + T_LOW * (group // 2) + 6.0)
    step(now, low.complete, *range(group))
    step(now, gains_to_rows)
    step(now, whole_copies[0].start)
    for sequence in range(pair * line * block_rows // total_rows):
        step(now + 0.1, project, sequence)
        now += 2.5
    step(now, start_all, entry_one_copies())
    step(now, whole_copies[1].start)
    size = query_rows(total_rows)
    for sequence in range(pair * line * block_rows // total_rows):
        for first in range(0, total_rows, size):
            for lane in range(0, query_cols, 2 * HD):
                step(now + 0.1, attention, sequence, first, size, lane)
                now += 1.0
    step(now, whole_copies[2].start)
    step(now, wait_all, entry_one_copies())

    span = (line - 1) * SEND
    ready_ffn, ready_back, base = weights_there, 0.0, now + 0.5
    count = 4
    for chunk in range(chunks):
        cot_done = traveller(
            [sem.at[0, chunk] for sem in travel_sems],
            cot_ref.at[chunk],
            lambda c, z, k=chunk: cots.at[k, c, z],
            base + chunk * span,
            HOP,
        )
        begin = base + 1.0 + chunk * span
        step(begin - 0.5, product, chunk)
        first_sum = reducer(0, chunk)
        more, finish = first_sum.plan(begin, total, functools.partial(norm_rows, chunk))
        steps.extend(more)
        arrived = traveller(
            [sem.at[1, chunk] for sem in travel_sems],
            None,
            lambda c, z, k=chunk: rows_in.at[k, c, z],
            finish,
            HOP,
        )
        begin = max(arrived, cot_done, ready_ffn) + 0.1
        if chunk == 0:
            step(begin, high.complete, *range(group))
        if chunk >= 2:
            step(begin, wait_all, chunk_copies(chunk - 2))
        step(begin, first_sum.drain)
        for index in range(count):
            step(begin + index, units_part, chunk, index, count)
        for index in range(count):
            step(begin + 4 + 0.5 * index, down_part, chunk, index, count)
        for index in range(count):
            step(begin + 6.3 + 0.8 * index, back_part, chunk, index, count)
        step(begin + 4.0, start_all, chunk_copies(chunk))
        step(begin + 9.4, terms_copy(chunk).start)
        ready_ffn = begin + 9.5
        begin = max(begin + 6.2, ready_back)
        ready_back = begin + span
        steps.extend(reducer(2, chunk).plan(begin, total, functools.partial(write_output, chunk))[0])
    run_steps(steps)
    for one in sums:
        if one.sem_at[0]:
            one.drain()
    low.drain()
    high.drain()
    wait_all(whole_copies)
    wait_all([terms_copy(chunk) for chunk in range(chunks)])
    for chunk in range(max(0, chunks - 2), chunks):
        wait_all(chunk_copies(chunk))


T_HIDDEN, T_LOW, T_HIGH = 14.0, 7.0, 28.0


def opening(sizes, collective_id, weights, gains, hidden, cot, tables):
    line, pair = sizes["ctx"], sizes["core"]
    group = line * pair
    block_rows, width = hidden.shape
    chunks = 4
    rows = block_rows // chunks
    tokens = group * rows
    own_rows = weights[0].shape[0]
    heads, keys, units = H * HD // group, KV * HD // group, FF // group
    qkv_cols = heads + 2 * keys
    tall, wide = qkv_cols + heads + 128, 3 * units
    blocks = (sizes["dp"] * line, sizes["x"] * pair, own_rows)
    gain_tile = jnp.pad(gains.T, ((0, 0), (0, 126)))
    any_spec = pl.BlockSpec(memory_space=pl.ANY)
    vmem = pl.BlockSpec(memory_space=pltpu.VMEM)
    shape = jax.ShapeDtypeStruct
    dma = pltpu.SemaphoreType.DMA
    by_chunk = (chunks, pair, line, rows, width)
    outs = pl.pallas_call(
        functools.partial(opening_kernel, sizes, chunks),
        out_shape=[
            shape((block_rows, width), BF),
            shape((block_rows, width), F32),
            shape((8, width), F32),
            shape(blocks + (tall,), BF),
            shape((pair, line, chunks, rows, width), BF),
            shape((group * block_rows, qkv_cols), BF),
            shape((pair, line, block_rows, heads), BF),
            shape(by_chunk, BF),
            shape(by_chunk, BF),
            shape(by_chunk, BF),
            shape((chunks, tokens, units), BF),
            shape((chunks, tokens, 2 * units), BF),
        ],
        in_specs=[vmem, vmem, any_spec, any_spec] + [vmem] * 7,
        out_specs=[vmem] * 3 + [any_spec] * 9,
        scratch_shapes=[
            pltpu.VMEM((2, own_rows, wide), F32),
            pltpu.VMEM((group, own_rows, tall), BF),
            pltpu.VMEM((group, own_rows, wide), BF),
            pltpu.VMEM(blocks + (tall,), BF),
            pltpu.VMEM(blocks + (wide,), BF),
            pltpu.VMEM(by_chunk, BF),
            pltpu.VMEM(by_chunk, BF),
            pltpu.VMEM((group * block_rows, qkv_cols), BF),
            pltpu.VMEM((pair, line, block_rows, heads), BF),
            pltpu.VMEM((2, tokens, units), BF),
            pltpu.VMEM((2, tokens, 2 * units), BF),
            *Reduce.room(line, pair, rows, width, 2, chunks),
            pltpu.VMEM((rows, width), F32),
            dma((2, 3)),
            dma((3 + group,)),
            dma((chunks, 4)),
            dma((chunks,)),
            *Spread.sems(sizes),
            *Spread.sems(sizes),
            *Reduce.sems(3, chunks)(line),
            *Travel.sems(1, line),
            dma((2, chunks, 1)),
            *[dma((2, chunks, 1, 2, line))] * 4,
        ],
        compiler_params=pltpu.CompilerParams(
            collective_id=collective_id, has_side_effects=True, vmem_limit_bytes=63 * 2**20
        ),
    )(*weights, gain_tile, hidden.reshape(chunks, rows, width), cot.reshape(chunks, rows, width), *tables)
    output, middle, gain_rows, low, entry_one, qkv, attended, terms, *rest = outs
    flat = [array.reshape(-1, array.shape[-1]) for array in (entry_one, qkv, attended, *rest)]
    return output, middle, gain_rows, low.reshape(width, tall), terms, flat


class GainSum:
    @staticmethod
    def room(sizes, width):
        group = sizes["ctx"] * sizes["core"]
        return [
            pltpu.VMEM((8, width), F32),
            pltpu.VMEM((sizes["x"] - 1, 8, width), F32),
            pltpu.VMEM((sizes["dp"] - 1, 8, width), F32),
            pltpu.VMEM((group, 8, 128), F32),
        ]

    @staticmethod
    def sems(sizes):
        group = sizes["ctx"] * sizes["core"]
        counts = (sizes["x"], sizes["x"], sizes["dp"], sizes["dp"], group, group)
        return [pltpu.SemaphoreType.DMA((count,)) for count in counts]

    def __init__(self, sizes, own_rows, out_ref, room, sems):
        self.sizes, self.own_rows, self.out_ref = sizes, own_rows, out_ref
        self.mine, self.over_x, self.over_dp, self.tiles = room
        self.sems_of = {"x": sems[0:2], "dp": sems[2:4], "group": sems[4:6]}
        self.at = {name: lax.axis_index(name) for name in ("dp", "ctx", "x", "core")}
        self.order = blocks_in_order(sizes["ctx"], sizes["core"])

    def hop(self, name, step):
        into = (self.over_x if name == "x" else self.over_dp).at[step - 1]
        sems = [sem.at[step] for sem in self.sems_of[name]]
        return remote(self.mine, into, *sems, **{name: wrap(self.at[name] + step, self.sizes[name])})

    def tile(self, index):
        dz, dc = self.order[index]
        z, c = wrap(self.at["ctx"] + dz, self.sizes["ctx"]), wrap(self.at["core"] + dc, self.sizes["core"])
        place = (self.at["dp"] * self.sizes["ctx"] + z) * self.sizes["x"] + self.at["x"]
        first = (place * self.sizes["core"] + c) * self.own_rows
        source = self.mine.at[:, pl.ds(pl.multiple_of(first // 128 * 128, 128), 128)]
        sems = [sem.at[index] for sem in self.sems_of["group"]]
        if index == 0:
            return source
        return remote(source, self.tiles.at[index], *sems, ctx=z, core=c)

    def begin(self, first, second):
        self.mine[...] = jnp.zeros_like(self.mine)
        self.mine[0:1, :] = first[...]
        self.mine[1:2, :] = second[...]
        self.send("x")

    def send(self, name):
        for step in range(1, self.sizes[name]):
            self.hop(name, step).start()

    def add(self, name):
        for step in range(1, self.sizes[name]):
            self.hop(name, step).wait()
        for step in range(1, self.sizes[name]):
            self.mine[...] += (self.over_x if name == "x" else self.over_dp)[step - 1]

    def second(self):
        self.add("x")
        self.send("dp")

    def third(self):
        self.add("dp")
        for index in range(1, len(self.order)):
            self.tile(index).start()

    def end(self):
        total = self.tile(0)[...]
        for index in range(1, len(self.order)):
            self.tile(index).wait()
            total = total + self.tiles[index]
        self.out_ref[...] = total


def closing_kernel(sizes, chunks, *refs):
    refs = list(refs)

    def take(count):
        taken, refs[:count] = refs[:count], []
        return taken

    entry_two, dgu_ref, cots_ref, act_ref, entry_one, heads_ref, low_ref, terms_ref = take(8)
    qkv_ref, hidden_ref, cot_ref, middle_ref, gains_ref, cos_ref, sin_ref, pos_col, pos_row = take(9)
    piece_refs, (branch_ref, grad_hidden_ref, gain_sum_ref) = take(6), take(3)
    left_slots, dgu, part, act, dqkv, heads, branch_slots, low_w, grad_heads, grad_proj, key_acc, value_acc = take(12)
    near, landed, total, grad_mid, branch, load_sem, left_sem, branch_sem = take(8)
    ffn_room, att_room = take(5), take(5)
    ffn_sems, att_sems, reduce_sems = take(7), take(7), take(4)
    gain_grad, gain_room, gain_sems = take(2), take(4), take(6)
    travel_sems = take(5)
    line, pair = sizes["ctx"], sizes["core"]
    rows = part.shape[-2]
    block_rows, width = hidden_ref.shape
    tokens, total_rows = qkv_ref.shape[0], cos_ref.shape[0]
    query_cols = heads.shape[1]
    qkv_cols = dqkv.shape[1]
    loads = {
        "dgu": pltpu.make_async_copy(dgu_ref, dgu, load_sem.at[0]),
        "act": pltpu.make_async_copy(act_ref, act, load_sem.at[1]),
        "heads": pltpu.make_async_copy(heads_ref, heads, load_sem.at[2]),
        "low": pltpu.make_async_copy(low_ref.at[:, pl.ds(0, low_w.shape[1])], low_w, load_sem.at[3]),
    }
    names = grad_pieces(sizes)
    shift = names[3][2]
    ffn_pieces = [(ref, w, o) for ref, (_, w, o) in zip(piece_refs[:3], names[:3])]
    att_pieces = [(ref, w, o - shift) for ref, (_, w, o) in zip(piece_refs[3:], names[3:])]
    ffn = Collect(sizes, (2 * act.shape[1], act.shape[1]), ffn_pieces, ffn_room, ffn_sems)
    att = Collect(sizes, (qkv_cols, query_cols), att_pieces, att_room, att_sems)
    entry_sums, sums = [
        [Reduce(line, pair, part, near, landed, *reduce_sems, (chunk,), kind) for chunk in range(chunks)]
        for kind in range(2)
    ]
    term_loads = [
        pltpu.make_async_copy(terms_ref.at[chunk], part.at[chunk], load_sem.at[4 + chunk])
        for chunk in range(chunks)
    ]
    gain_sum = GainSum(sizes, ffn.rows, gain_sum_ref, gain_room, gain_sems)

    def left_loads(turn, item):
        one, sources = (ffn, (entry_two, cots_ref)) if turn < line else (att, (entry_one, branch_ref))
        return [
            pltpu.make_async_copy(
                sources[item].at[:, one.lanes(turn % line, dp)], left_slots.at[item, dp], left_sem.at[item, dp]
            )
            for dp in range(sizes["dp"])
        ]

    def branch_load(index):
        size = branch_slots.shape[1]
        return pltpu.make_async_copy(
            branch_ref.at[pl.ds(index * size, size)], branch_slots.at[index % 2], branch_sem.at[index % 2]
        )

    for load in term_loads + left_loads(0, 0) + list(loads.values()) + left_loads(0, 1):
        load.start()
    greet_all(sizes)

    def multiply(turn):
        one, rights = (ffn, (dgu, act)) if turn < line else (att, (dqkv, heads))
        for item in range(2):
            for load in left_loads(turn, item):
                load.wait()
            one.multiply(turn % line, item, left_slots.at[item], rights[item])
            if turn % line < line - 1:
                for load in left_loads(turn + 1, item):
                    load.start()

    def later_loads():
        for load in left_loads(line, 0) + left_loads(line, 1):
            load.start()

    def back_to_heads():
        loads["low"].wait()
        size = branch_slots.shape[1]
        branch_load(0).start()
        for index in range(tokens // size):
            if index + 1 < tokens // size:
                branch_load(index + 1).start()
            branch_load(index).wait()
            grad_heads[index * size : (index + 1) * size, :] = dot(
                branch_slots[index % 2], low_w[:, qkv_cols:]
            ).astype(BF)

    def attention_part(sequence, low, size, lane):
        start = sequence * total_rows
        span = slice(start, start + total_rows)
        at = slice(start + low, start + low + size)
        both = qkv_ref[span, query_cols:]
        keys, values = both_halves(both, 0), both_halves(both, 1)
        visible = pos_row[...] <= pos_col[low : low + size, :]
        queries = qkv_ref[at, lane : lane + 2 * HD]
        grads = grad_heads[at, lane : lane + 2 * HD]
        grad_queries = []
        key_term = value_term = None
        for head in range(2):
            query, grad = only_head(queries, head), only_head(grads, head)
            probability = softmax_rows(query, keys, visible)
            grad_prob = contract_cols(grad, values)
            delta = jnp.sum(probability * grad_prob, -1, keepdims=True)
            grad_scores = jnp.where(visible, probability * (grad_prob - delta), 0.0).astype(BF)
            grad_queries.append(dot(grad_scores, keys))
            key_more = contract_rows(grad_scores, query)
            value_more = contract_rows(probability.astype(BF), grad)
            key_term = key_more if key_term is None else key_term + key_more
            value_term = value_more if value_term is None else value_term + value_more
        scale = HD ** (-0.5)
        grad_proj[low : low + size, lane : lane + 2 * HD] = scale * jnp.where(
            lane_index(grad_queries[0].shape) < HD, grad_queries[0], grad_queries[1]
        )
        if low == 0 and lane == 0:
            key_acc[...] = key_term * scale
            value_acc[...] = value_term
        else:
            key_acc[...] += key_term * scale
            value_acc[...] += value_term

    def rotate_back(sequence):
        keys, values = key_acc[...], value_acc[...]
        grad_proj[:, query_cols:] = jnp.where(
            lane_index(keys.shape) < HD, keys + pltpu.roll(keys, HD, 1), values + pltpu.roll(values, HD, 1)
        )
        for low in range(0, total_rows, 256):
            size = min(256, total_rows - low)
            grads = grad_proj[low : low + size, :]
            cosine = for_heads(cos_ref[low : low + size, :], qkv_cols)
            sine = for_heads(sin_ref[low : low + size, :], qkv_cols)
            back = grads * cosine + turned(grads * sine)
            at = sequence * total_rows + low
            dqkv[at : at + size, :] = back.astype(BF)

    def entry_terms(chunk):
        mine = jnp.concatenate(
            [
                dqkv[(c * line + z) * block_rows + chunk * rows : (c * line + z) * block_rows + (chunk + 1) * rows, :]
                for c in range(pair)
                for z in range(line)
            ],
            0,
        )
        for low in range(0, width, 512):
            term = contract_cols(mine, low_w[low : low + 512, :qkv_cols]).astype(BF)
            part[chunk, :, :, :, low : low + 512] = term.reshape(pair, line, rows, 512)

    def norm_back(values, which, chunk):
        inverse = lax.rsqrt(jnp.mean(values * values, -1, keepdims=True) + EPS_NORM)
        normed = values * inverse
        grad_entry = total[...]
        gain_term = jnp.sum(grad_entry * normed, 0, keepdims=True)
        if chunk == 0:
            gain_grad[which][...] = gain_term
        else:
            gain_grad[which][...] += gain_term
        grad_normed = grad_entry * gains_ref[which : which + 1, :]
        return inverse * (grad_normed - normed * jnp.mean(grad_normed * normed, -1, keepdims=True))

    def middle_back(chunk):
        at = slice(chunk * rows, (chunk + 1) * rows)
        grad = cot_ref[at, :].astype(F32) + norm_back(middle_ref[at, :], 1, chunk)
        grad_mid[at, :] = grad
        branch[chunk] = grad.astype(BF)

    def hidden_back(chunk):
        at = slice(chunk * rows, (chunk + 1) * rows)
        grad = grad_mid[at, :] + norm_back(hidden_ref[at, :].astype(F32), 0, chunk)
        grad_hidden_ref[at, :] = grad.astype(BF)

    steps = []

    def step(time, function, *values):
        steps.append((time, functools.partial(function, *values)))

    step(0.0, loads["dgu"].wait)
    step(0.0, loads["act"].wait)
    span = (line - 1) * SEND
    gathered = 0.0
    for chunk, one in enumerate(entry_sums):
        start = 1.0 + chunk * span
        step(start - 0.1, term_loads[chunk].wait)
        more, finish = one.plan(start, total, functools.partial(middle_back, chunk))
        steps += more
        travel = Travel(
            line,
            pair,
            [branch.at[chunk]],
            [lambda c, z, k=chunk: branch_ref.at[pl.ds(((c * line + z) * chunks + k) * rows, rows)]],
            *[sem.at[chunk] for sem in travel_sems],
        )
        step(finish, travel.begin)
        for index in range(line - 1):
            step(finish + (index + 1) * HOP, travel.step, index)
        gathered = finish + line * HOP - 1.0
        step(gathered, travel.end)
    period, before = PERIOD, BEFORE
    for tick in range(line):
        arrived = before + period * tick
        issued = 5.5 * (tick + 1) if tick < 2 else before + period * (tick - 2) + 0.5
        step(issued - 5.0 if tick < 2 else issued - 5.5, multiply, tick)
        step(issued, ffn.send_one, tick)
        step(arrived, ffn.sum_one, tick)
        step(arrived + 18.0, ffn.sum_two, tick)
    now = gathered + 0.1
    step(now, back_to_heads)
    last_multiply = max(5.5 * 2, before + period * (line - 3)) + 0.6
    step(max(now, last_multiply), later_loads)
    now += 3.0
    for sequence in range(tokens // total_rows):
        size = query_rows(total_rows)
        for low in range(0, total_rows, size):
            for lane in range(0, query_cols, 2 * HD):
                step(now, attention_part, sequence, low, size, lane)
                now += 3.0
        step(now, rotate_back, sequence)
        now += 0.5
    step(now, loads["heads"].wait)
    begin = now + 1.0
    for chunk, one in enumerate(sums):
        step(now + 0.5 + chunk, entry_sums[chunk].drain)
        step(now + 0.5 + chunk, entry_terms, chunk)
        start = begin + chunk * span
        more, finish = one.plan(start, total, functools.partial(hidden_back, chunk))
        steps += more
    step(finish + 0.2, gain_sum.begin, *gain_grad)
    step(finish + 4.0, gain_sum.second)
    step(finish + 8.0, gain_sum.third)
    step(finish + 12.0, gain_sum.end)
    now = max(now + 1.0 + chunks, last_multiply + 1.0)
    for tick in range(line):
        step(now + tick, multiply, line + tick)
        step(now + tick + 0.5, att.send_one, tick)
        arrived = now + ATT_WAIT + 2.0 * tick
        step(arrived, att.sum_one, tick)
        step(arrived + 12.5, att.sum_two, tick)
    run_steps(steps)
    for one in sums + [ffn, att]:
        one.drain()


PERIOD, BEFORE, ATT_WAIT = 26.0, 40.0, 40.0


def closing(sizes, collective_id, factors, low, terms, hidden, cot, middle, gains, tables):
    line, pair = sizes["ctx"], sizes["core"]
    group = line * pair
    block_rows, width = hidden.shape
    tokens = block_rows * group
    chunks = 4
    rows = block_rows // chunks
    own_rows = width // (group * sizes["dp"] * sizes["x"])
    units = factors[3].shape[1]
    qkv_cols, query_cols = factors[6].shape[1], factors[5].shape[1]
    total_rows = tables[0].shape[0]
    pieces = grad_pieces(sizes)
    any_spec = pl.BlockSpec(memory_space=pl.ANY)
    vmem = pl.BlockSpec(memory_space=pltpu.VMEM)
    dma = pltpu.SemaphoreType.DMA
    shape = jax.ShapeDtypeStruct
    across = sizes["x"] * pair * own_rows
    branch_rows = 128
    part_shape = (chunks, pair, line, rows, width)
    return pl.pallas_call(
        functools.partial(closing_kernel, sizes, chunks),
        out_shape=[shape((own_rows, group * w), BF) for _, w, _ in pieces]
        + [shape((tokens, width), BF), shape((block_rows, width), BF), shape((8, 128), F32)],
        in_specs=[any_spec] * 8 + [vmem] * 9,
        out_specs=[any_spec] * (len(pieces) + 1) + [vmem] * 2,
        scratch_shapes=[
            pltpu.VMEM((2, sizes["dp"], tokens, across), BF),
            pltpu.VMEM((tokens, 2 * units), BF),
            pltpu.VMEM(part_shape, BF),
            pltpu.VMEM((tokens, units), BF),
            pltpu.VMEM((tokens, qkv_cols), BF),
            pltpu.VMEM((tokens, query_cols), BF),
            pltpu.VMEM((2, branch_rows, width), BF),
            pltpu.VMEM((width, qkv_cols + query_cols), BF),
            pltpu.VMEM((tokens, query_cols), BF),
            pltpu.VMEM((total_rows, qkv_cols), F32),
            pltpu.VMEM((total_rows, 2 * HD), F32),
            pltpu.VMEM((total_rows, 2 * HD), F32),
            *Reduce.room(line, pair, rows, width, chunks)[1:],
            pltpu.VMEM((rows, width), F32),
            pltpu.VMEM((block_rows, width), F32),
            pltpu.VMEM((chunks, rows, width), BF),
            dma((4 + chunks,)),
            dma((2, sizes["dp"])),
            dma((2,)),
            *Collect.room(sizes, own_rows, 3 * units),
            *Collect.room(sizes, own_rows, qkv_cols + query_cols),
            *Collect.sems(sizes, 3),
            *Collect.sems(sizes, 3),
            *Reduce.sems(2, chunks)(line),
            pltpu.VMEM((1, width), F32),
            pltpu.VMEM((1, width), F32),
            *GainSum.room(sizes, width),
            *GainSum.sems(sizes),
            dma((chunks, 1)),
            *[dma((chunks, 1, 2, line))] * 4,
        ],
        compiler_params=pltpu.CompilerParams(
            collective_id=collective_id, has_side_effects=True, vmem_limit_bytes=63 * 2**20
        ),
    )(*factors[:6], low, terms, factors[6], hidden, cot, middle, gains, *tables)


def grad_pieces(sizes):
    group = sizes["ctx"] * sizes["core"]
    heads, keys, units = H * HD // group, KV * HD // group, FF // group
    pieces, offset = [], 0
    for name, width in (
        ("gate", units),
        ("up", units),
        ("down", units),
        ("query", heads),
        ("key_value", 2 * keys),
        ("out", heads),
    ):
        pieces.append((name, width, offset))
        offset += width
    return pieces


def adamw_kernel(step_rate, decay_rate, grad_ref, weight_ref, state_ref, grad_out, weight_out, state_out):
    gradient = grad_ref[...].astype(F32)
    grad_out[...] = gradient
    updated, states = adamw(weight_ref[...], gradient, state_ref[...], step_rate, decay_rate)
    weight_out[...] = updated
    state_out[...] = states


def adamw_columns(gradient, weight, states, step_rate, decay_rate):
    rows, columns = weight.shape
    step = math.gcd(columns, 4096)
    while rows * step > 2**18 and step % 256 == 0:
        step //= 2
    flat = pl.BlockSpec((rows, step), lambda i: (0, i))
    deep = pl.BlockSpec((2, rows, step), lambda i: (0, 0, i))
    return pl.pallas_call(
        functools.partial(adamw_kernel, step_rate, decay_rate),
        grid=(columns // step,),
        out_shape=[
            jax.ShapeDtypeStruct(weight.shape, F32),
            jax.ShapeDtypeStruct(weight.shape, F32),
            jax.ShapeDtypeStruct(states.shape, F32),
        ],
        in_specs=[flat, flat, deep],
        out_specs=[flat, flat, deep],
        compiler_params=pltpu.CompilerParams(vmem_limit_bytes=40 * 2**20),
    )(gradient, weight, states)


def dot(left, right):
    return jnp.dot(left, right, preferred_element_type=F32)


def shards(
    sizes,
    hidden,
    cotangent,
    span_order,
    norm_gains,
    w_qkv,
    w_out,
    w_gate_up,
    w_down,
    mom_gains,
    mom_qkv,
    mom_out,
    mom_gate_up,
    mom_down,
):
    everyone = ("dp", "ctx", "x", "core")
    line, pair = sizes["ctx"], sizes["core"]
    group = line * pair
    block_rows, width = hidden.shape[1:]
    total_rows = block_rows * line
    span_rows = total_rows // span_order.shape[0]
    heads, kv_heads = H // group, KV // group
    query_cols, kv_cols = heads * HD, kv_heads * HD
    key_pos = (
        span_order[:, None] * span_rows + jnp.arange(span_rows, dtype=jnp.int32)[None, :]
    ).reshape(-1)
    cos_tab, sin_tab = rope_table(key_pos)
    signs = jnp.where(jnp.arange(HD) < HD // 2, -1.0, 1.0)
    cosines = jnp.concatenate([cos_tab] * 3 + [jnp.ones_like(cos_tab)], 1)
    sines = jnp.concatenate(
        [sin_tab * signs] * 3 + [jnp.zeros_like(sin_tab)], 1
    )
    tables = (cosines, sines, key_pos[:, None], key_pos[None, :])
    weights = (w_qkv, w_out, w_gate_up, w_down)
    output, middle, gains, low, terms, flat = opening(
        sizes, 0, weights, norm_gains, hidden[0], cotangent[0], tables
    )
    entry_one, qkv, attended, entry_two, cot, activated, grad_gu = flat
    factors = (entry_two, grad_gu, cot, activated, entry_one, attended, qkv)
    *pieces, _, grad_hidden, gain_sums = closing(
        sizes, 1, factors, low, terms, hidden[0], cotangent[0], middle, gains, tables
    )
    grad_gate, grad_up, grad_down, grad_query, grad_key_value, grad_out = pieces
    output, grad_hidden = output[None], grad_hidden[None]
    rows = w_qkv.shape[0]
    place = lax.axis_index(everyone) * rows
    grad_gains = lax.dynamic_slice(gain_sums, (0, lax.rem(place, 128)), (2, rows))
    grad_key_value = grad_key_value.reshape(rows, group, 2, kv_cols).transpose(0, 2, 1, 3)
    grad_qkv = jnp.concatenate([grad_query, grad_key_value.reshape(rows, -1)], 1)
    grad_gate_up = jnp.concatenate([grad_gate, grad_up], 1)
    new_gains, new_mom_gains = adamw(norm_gains, grad_gains, mom_gains, LR_GAIN, 0.0)
    grad_qkv, new_qkv, new_mom_qkv = adamw_columns(grad_qkv, w_qkv, mom_qkv, LR_MATRIX, DECAY_MATRIX)
    grad_out, new_out, new_mom_out = adamw_columns(grad_out, w_out, mom_out, LR_OUTPUT, DECAY_MATRIX)
    grad_gate_up, new_gate_up, new_mom_gate_up = adamw_columns(
        grad_gate_up, w_gate_up, mom_gate_up, LR_MATRIX, DECAY_MATRIX
    )
    grad_down, new_down, new_mom_down = adamw_columns(
        grad_down, w_down, mom_down, LR_MATRIX, DECAY_MATRIX
    )
    return (
        output,
        grad_hidden,
        grad_gains,
        grad_qkv,
        grad_out,
        grad_gate_up,
        grad_down,
        new_gains,
        new_qkv,
        new_out,
        new_gate_up,
        new_down,
        new_mom_gains,
        new_mom_qkv,
        new_mom_out,
        new_mom_gate_up,
        new_mom_down,
    )


def solution(mesh):
    shape = dict(mesh.shape)
    pair = 2 if shape["ctx"] * 2 <= KV and shape["fsdp"] % 2 == 0 else 1
    sizes = {"dp": shape["dp"], "ctx": shape["ctx"], "x": shape["fsdp"] // pair, "core": pair}
    finer = Mesh(mesh.devices.reshape(tuple(sizes.values())), tuple(sizes))
    tokens = P(("dp", "x", "core"), "ctx", None)
    everyone = ("dp", "ctx", "x", "core")
    rows, gains = P(everyone, None), P(None, everyone)
    row_moments, gain_moments = P(None, everyone, None), P(None, None, everyone)
    weights = (gains, rows, rows, rows, rows)
    moments = (gain_moments, row_moments, row_moments, row_moments, row_moments)
    return jax.shard_map(
        functools.partial(shards, sizes),
        mesh=finer,
        in_specs=(tokens, tokens, P()) + weights + moments,
        out_specs=(tokens, tokens) + weights + weights + moments,
        check_vma=False,
    )
```

```python
import functools
import math

import jax
import jax.numpy as jnp
from jax import lax
from jax.experimental import pallas as pl
from jax.experimental.pallas import tpu as pltpu
from jax.sharding import Mesh
from jax.sharding import PartitionSpec as P

MESH = pl.DeviceIdType.MESH
BF = jnp.bfloat16
F32 = jnp.float32
H = 32
KV = 8
HD = 64
FF = 8192


EPS_NORM = 1e-05
NEG_FILL = -1000000000.0
THETA = 500000.0
BETA_ONE = 0.9
BETA_TWO = 0.95
ADAM_EPS = 1e-08
DECAY_MATRIX = 0.1
LR_MATRIX = 0.01
LR_OUTPUT = 0.06
LR_GAIN = 0.3


def rope_rates():
    half_dim = HD // 2
    index_row = jnp.arange(half_dim, dtype=jnp.float32)
    frequency = jnp.exp(-(2.0 * index_row / HD) * math.log(THETA))
    wavelen = 2.0 * math.pi / frequency
    smooth = (8192.0 / wavelen - 1.0) / 3.0
    return jnp.where(
        wavelen < 2048.0,
        frequency,
        jnp.where(
            wavelen > 8192.0,
            frequency / 32.0,
            (1.0 - smooth) * frequency / 32.0 + smooth * frequency,
        ),
    )


def adamw(weight, gradient, states, step_rate, decay_rate):
    first_mom = BETA_ONE * states[0] + (1.0 - BETA_ONE) * gradient
    root_mom = jnp.sqrt(BETA_TWO * states[1] * states[1] + (1.0 - BETA_TWO) * gradient * gradient)
    first_hat = first_mom / (1.0 - BETA_ONE**3)
    root_hat = root_mom / math.sqrt(1.0 - BETA_TWO**3)
    updated = weight - step_rate * (first_hat / (root_hat + ADAM_EPS) + decay_rate * weight)
    return (updated, jnp.stack([first_mom, root_mom]))


def contract_rows(left_arr, right_arr):
    return lax.dot_general(
        left_arr, right_arr, (((0,), (0,)), ((), ())), preferred_element_type=jnp.float32
    )


def contract_cols(left_arr, right_arr):
    return lax.dot_general(
        left_arr, right_arr, (((1,), (1,)), ((), ())), preferred_element_type=jnp.float32
    )


def wrap(value, size):
    return lax.rem(value + size, size)


def remote(src, dst, send_sem, recv_sem, **where):
    return pltpu.make_async_remote_copy(
        src_ref=src,
        dst_ref=dst,
        send_sem=send_sem,
        recv_sem=recv_sem,
        device_id=where,
        device_id_type=MESH,
    )


def greet(places):
    barrier = pltpu.get_barrier_semaphore()
    for where in places:
        pl.semaphore_signal(barrier, inc=1, device_id=where, device_id_type=MESH)
    pl.semaphore_wait(barrier, len(places))


def greet_line(line, pair):
    barrier = pltpu.get_barrier_semaphore()
    here = lax.axis_index("ctx")

    @pl.when(here > 0)
    def _():
        pl.semaphore_signal(barrier, inc=1, device_id={"ctx": here - 1}, device_id_type=MESH)

    @pl.when(here < line - 1)
    def _():
        pl.semaphore_signal(barrier, inc=1, device_id={"ctx": here + 1}, device_id_type=MESH)

    if pair > 1:
        pl.semaphore_signal(
            barrier, inc=1, device_id={"core": 1 - lax.axis_index("core")}, device_id_type=MESH
        )
    ends = (here == 0).astype(jnp.int32) + (here == line - 1).astype(jnp.int32)
    pl.semaphore_wait(barrier, 2 - ends + (1 if pair > 1 else 0))


class Travel:
    @staticmethod
    def sems(many, line):
        return [pltpu.SemaphoreType.DMA((many,))] + [pltpu.SemaphoreType.DMA((many, 2, line))] * 4

    def __init__(self, line, pair, ins, outs, own_sem, line_send, line_recv, core_send, core_recv):
        self.line, self.pair, self.ins, self.outs = line, pair, ins, outs
        self.own_sem, self.line_sems, self.core_sems = own_sem, (line_send, line_recv), (core_send, core_recv)
        self.here = lax.axis_index("ctx")
        self.core = lax.axis_index("core")

    def block(self, way, step):
        return self.here - 1 - step if way == 0 else self.here + 1 + step

    def copy(self, sems, at, source, place, **where):
        return remote(place if source is None else source, place, sems[0].at[at], sems[1].at[at], **where)

    def hop(self, item, way, step, source=None):
        place = self.outs[item](self.core, self.block(way, step - 1))
        target = self.here + 1 if way == 0 else self.here - 1
        return self.copy(self.line_sems, (item, way, step), source, place, ctx=target)

    def arrived(self, item, way, step):
        place = self.outs[item](self.core, self.block(way, step))
        return self.copy(self.line_sems, (item, way, step), None, place, ctx=self.here)

    def share(self, item, way, step, source=None):
        place = self.outs[item](self.core, self.block(way, step))
        return self.copy(self.core_sems, (item, way, step + 1), source, place, core=1 - self.core)

    def shared(self, item, way, step):
        place = self.outs[item](1 - self.core, self.block(way, step))
        return self.copy(self.core_sems, (item, way, step + 1), None, place, core=1 - self.core)

    def own(self, item):
        place = self.outs[item](self.core, self.here)
        return pltpu.make_async_copy(self.ins[item], place, self.own_sem.at[item])

    def sends(self, way):
        return self.here < self.line - 1 if way == 0 else self.here > 0

    def has(self, way, step):
        return self.block(way, step) >= 0 if way == 0 else self.block(way, step) <= self.line - 1

    def begin(self):
        for item in range(len(self.ins)):
            for way in range(2):

                @pl.when(self.sends(way))
                def _(item=item, way=way):
                    self.hop(item, way, 0, self.ins[item]).start()

            if self.pair > 1:
                self.share(item, 0, -1, self.ins[item]).start()
            if self.ins[item] is not None:
                self.own(item).start()

    def step(self, step):
        for item in range(len(self.ins)):
            for way in range(2):

                @pl.when(self.has(way, step))
                def _(item=item, way=way):
                    self.arrived(item, way, step).wait_recv()
                    if step + 1 < self.line - 1:

                        @pl.when(self.sends(way))
                        def _():
                            self.hop(item, way, step + 1).start()

                    if self.pair > 1:
                        self.share(item, way, step).start()

    def end(self):
        for item in range(len(self.ins)):
            if self.ins[item] is not None:
                self.own(item).wait()
            if self.pair > 1:
                self.share(item, 0, -1, self.ins[item]).wait_send()
                self.shared(item, 0, -1).wait_recv()
            for way in range(2):

                @pl.when(self.sends(way))
                def _(item=item, way=way):
                    self.hop(item, way, 0, self.ins[item]).wait_send()

                for step in range(self.line - 1):

                    @pl.when(self.has(way, step))
                    def _(item=item, way=way, step=step):
                        if step + 1 < self.line - 1:

                            @pl.when(self.sends(way))
                            def _():
                                self.hop(item, way, step + 1).wait_send()

                        if self.pair > 1:
                            self.share(item, way, step).wait_send()
                            self.shared(item, way, step).wait_recv()


def add_rows(rows, out_ref, *parts):
    def one(index, carry):
        at = pl.ds(pl.multiple_of(index * 16, 16), 16)
        total = parts[0][at, :].astype(F32)
        for part in parts[1:]:
            total = total + part[at, :].astype(F32)
        out_ref[at, :] = total.astype(out_ref.dtype)
        return carry

    lax.fori_loop(0, rows // 16, one, 0)


class Reduce:
    @staticmethod
    def sems(*outer):
        dma = pltpu.SemaphoreType.DMA
        return lambda line: [dma(outer), dma(outer), dma(outer + (2, line)), dma(outer + (2, line))]

    @staticmethod
    def room(line, pair, rows, columns, *outer):
        return [
            pltpu.VMEM(outer + (pair, line, rows, columns), BF),
            pltpu.VMEM(outer + (line, rows, columns), BF),
            pltpu.VMEM(outer + (line + 1, rows, columns), BF),
        ]

    def __init__(self, line, pair, part, near, landed, core_send, core_recv, line_send, line_recv, at, kind=None):
        self.line, self.pair, self.at = line, pair, at
        self.sem_at = at if kind is None else (kind, at[-1])
        self.part, self.near, self.landed = part, near, landed
        self.core_sems, self.line_sems = (core_send, core_recv), (line_send, line_recv)
        self.here, self.core = lax.axis_index("ctx"), lax.axis_index("core")
        self.rows = part.shape[-2]

    def mine(self, block):
        return self.part.at[self.at + (self.core, block)]

    def across(self):
        return remote(
            self.part.at[self.at + (1 - self.core,)],
            self.near.at[self.at],
            self.core_sems[0].at[self.sem_at],
            self.core_sems[1].at[self.sem_at],
            core=1 - self.core,
        )

    def slot(self, way, block):
        return self.landed.at[self.at + (block + 1 if way == 0 else block,)]

    def onward(self, way, block, here):
        index = self.sem_at + (way, block)
        return remote(
            self.mine(block),
            self.slot(way, block),
            self.line_sems[0].at[index],
            self.line_sems[1].at[index],
            ctx=here + 1 if way == 0 else here - 1,
        )

    def begin(self):
        if self.pair > 1:
            self.across().start()

    def settle(self):
        if self.pair > 1:
            self.across().wait_recv()

    def terms(self, block):
        return [self.mine(block)] + ([self.near.at[self.at + (block,)]] if self.pair > 1 else [])

    def relay(self, way, block, here):
        @pl.when(self.here == here)
        def _():
            terms = self.terms(block)
            if here != (0 if way == 0 else self.line - 1):
                self.onward(way, block, here).wait_recv()
                terms.append(self.slot(way, block))
            if len(terms) > 1:
                add_rows(self.rows, self.mine(block), *terms)
            self.onward(way, block, here).start()

    def finish(self, here, total_ref):
        @pl.when(self.here == here)
        def _():
            terms = self.terms(here)
            for way, has in ((0, here > 0), (1, here < self.line - 1)):
                if has:
                    self.onward(way, here, here).wait_recv()
                    terms.append(self.slot(way, here))
            add_rows(self.rows, total_ref, *terms)

    def drain(self):
        if self.pair > 1:
            self.across().wait_send()
        for here in range(self.line):

            @pl.when(self.here == here)
            def _(here=here):
                for block in range(self.line):
                    if block != here:
                        self.onward(0 if block > here else 1, block, here).wait_send()

    def plan(self, start, total_ref, after):
        ends, steps = self.line - 1, [(start, self.begin), (start + LAG, self.settle)]
        for way in range(2):
            for block in range(self.line):
                for here in range(self.line):
                    if here < block if way == 0 else here > block:
                        wait = ends - block if way == 0 else block
                        depth = here if way == 0 else ends - here
                        when = start + LAG + wait * SEND + depth * HOP
                        steps.append((when, functools.partial(self.relay, way, block, here)))
        finish = start + LAG + ends * HOP + 0.5
        for here in range(self.line):
            steps.append((finish, functools.partial(self.finish, here, total_ref)))
        steps.append((finish, after))
        return steps, finish


SEND, HOP, LAG = 4.0, 7.0, 5.0


def run_steps(steps):
    for _, step in sorted(steps, key=lambda item: item[0]):
        step()


def blocks_in_order(line, pair):
    away = sorted(range(line), key=lambda d: min(d, line - d))
    return [(dz, dc) for dz in away for dc in range(pair)]


def greet_all(sizes):
    names = ("dp", "ctx", "x", "core")
    at = {name: lax.axis_index(name) for name in names}
    places = []
    for dz, dc in blocks_in_order(sizes["ctx"], sizes["core"]):
        if dz or dc:
            places.append(
                {"ctx": wrap(at["ctx"] + dz, sizes["ctx"]), "core": wrap(at["core"] + dc, sizes["core"])}
            )
    for name in ("dp", "x"):
        for step in range(1, sizes[name]):
            places.append({name: wrap(at[name] + step, sizes[name])})
    greet(places)


class Spread:
    @staticmethod
    def sems(sizes):
        dma = pltpu.SemaphoreType.DMA
        group, steps = sizes["ctx"] * sizes["core"], max(sizes["dp"], sizes["x"])
        return [dma((1,))] + [dma((group,))] * 2 + [dma((group, steps))] * 2 + [dma((group, steps, steps))] * 2

    def __init__(self, sizes, pack, out, sems):
        self.sizes, self.pack, self.out = sizes, pack, out
        self.own_sem, *rest = sems
        self.f_sems, self.a_sems, self.b_sems = rest[0:2], rest[2:4], rest[4:6]
        self.line, self.pair = sizes["ctx"], sizes["core"]
        self.at = {name: lax.axis_index(name) for name in ("dp", "ctx", "x", "core")}
        self.order = blocks_in_order(self.line, self.pair)

    def spot(self, dp, z, x, c):
        return self.out.at[dp * self.line + z, x * self.pair + c]

    def mine(self):
        return self.spot(*[self.at[name] for name in ("dp", "ctx", "x", "core")])

    def copy(self, sems, at, source, target, **where):
        return remote(source, target, *[sem.at[at] for sem in sems], **where)

    def first(self, index):
        dz, dc = self.order[index]
        z, c = wrap(self.at["ctx"] + dz, self.line), wrap(self.at["core"] + dc, self.pair)
        return self.copy(self.f_sems, index, self.pack.at[z * self.pair + c], self.mine(), ctx=z, core=c)

    def place(self, index, moved):
        dz, dc = self.order[index]
        z, c = wrap(self.at["ctx"] - dz, self.line), wrap(self.at["core"] - dc, self.pair)
        dp, x = [wrap(self.at[name] - moved.get(name, 0), self.sizes[name]) for name in ("dp", "x")]
        return self.spot(dp, z, x, c)

    def axes(self, index):
        return ("x", "dp") if sum(self.order[index]) % 2 == 0 else ("dp", "x")

    def ahead(self, name, step):
        return {name: wrap(self.at[name] + step, self.sizes[name])}

    def came(self, index):
        spot = self.place(index, {})
        return self.copy(self.f_sems, index, spot, spot, core=self.at["core"])

    def hop_one(self, index, step):
        spot = self.place(index, {})
        return self.copy(self.a_sems, (index, step), spot, spot, **self.ahead(self.axes(index)[0], step))

    def one_came(self, index, step):
        spot = self.place(index, {self.axes(index)[0]: step})
        return self.copy(self.a_sems, (index, step), spot, spot, core=self.at["core"])

    def hop_two(self, index, step, far):
        name, other = self.axes(index)
        spot = self.place(index, {name: step})
        return self.copy(self.b_sems, (index, step, far), spot, spot, **self.ahead(other, far))

    def two_came(self, index, step, far):
        name, other = self.axes(index)
        spot = self.place(index, {name: step, other: far})
        return self.copy(self.b_sems, (index, step, far), spot, spot, core=self.at["core"])

    def own(self):
        source = self.pack.at[self.at["ctx"] * self.pair + self.at["core"]]
        return pltpu.make_async_copy(source, self.mine(), self.own_sem.at[0])

    def begin(self, *indices):
        for index in indices:
            if index == 0:
                self.own().start()
            elif index < len(self.order):
                self.first(index).start()

    def onward(self, index, *more):
        if index == 0:
            self.own().wait()
        else:
            self.came(index).wait_recv()
        self.begin(*more)
        name, other = self.axes(index)
        for step in range(1, self.sizes[name]):
            self.hop_one(index, step).start()
        for far in range(1, self.sizes[other]):
            self.hop_two(index, 0, far).start()

    def onward_two(self, index):
        name, other = self.axes(index)
        for step in range(1, self.sizes[name]):
            self.one_came(index, step).wait_recv()
            for far in range(1, self.sizes[other]):
                self.hop_two(index, step, far).start()

    def complete(self, *indices):
        for index in indices:
            name, other = self.axes(index)
            for step in range(self.sizes[name]):
                for far in range(1, self.sizes[other]):
                    self.two_came(index, step, far).wait_recv()

    def drain(self):
        for index in range(len(self.order)):
            name, other = self.axes(index)
            if index:
                self.first(index).wait_send()
            for step in range(self.sizes[name]):
                if step:
                    self.hop_one(index, step).wait_send()
                for far in range(1, self.sizes[other]):
                    self.hop_two(index, step, far).wait_send()


class Collect:
    AXES = (("dp", "x"), ("x", "dp"))

    @staticmethod
    def room(sizes, rows, width):
        room = [pltpu.VMEM((sizes["ctx"], sizes["dp"], sizes["x"], sizes["core"], rows, width), BF)]
        for parity, (name, other) in enumerate(Collect.AXES):
            count = sum((dz + dc) % 2 == parity for dz, dc in blocks_in_order(sizes["ctx"], sizes["core"]))
            room.append(pltpu.VMEM((max(1, count), (sizes[name] - 1) * sizes[other], rows, width), BF))
            room.append(pltpu.VMEM((max(1, count), sizes[other] - 1, rows, width), BF))
        return room

    @staticmethod
    def sems(sizes, pieces):
        dma = pltpu.SemaphoreType.DMA
        group, steps = sizes["ctx"] * sizes["core"], max(sizes["dp"], sizes["x"])
        return (
            [dma((pieces,))]
            + [dma((group, steps, steps))] * 2
            + [dma((group, steps))] * 2
            + [dma((group, pieces))] * 2
        )

    def __init__(self, sizes, widths, pieces, room, sems):
        self.sizes, self.widths, self.pieces = sizes, widths, pieces
        self.terms = room[0]
        self.near, self.far_in = room[1::2], room[2::2]
        self.own_sem, *rest = sems
        self.a_sems, self.b_sems, self.f_sems = rest[0:2], rest[2:4], rest[4:6]
        self.line, self.pair = sizes["ctx"], sizes["core"]
        self.rows = self.terms.shape[-2]
        self.at = {name: lax.axis_index(name) for name in ("dp", "ctx", "x", "core")}
        self.me = self.at["ctx"] * self.pair + self.at["core"]
        self.away = sorted(range(self.line), key=lambda d: (d != 0, -min(d, self.line - d)))
        self.order = [(dz, dc) for dz in self.away for dc in range(self.pair)]

    def spot_of(self, index, sign=1):
        dz, dc = self.order[index]
        return wrap(self.at["ctx"] + sign * dz, self.line), wrap(self.at["core"] + sign * dc, self.pair)

    def parity(self, index):
        return sum(self.order[index]) % 2

    def axes(self, index):
        return self.AXES[self.parity(index)]

    def slot(self, index):
        return sum(self.parity(before) == self.parity(index) for before in range(index))

    def indices(self, tick):
        return range(tick * self.pair, (tick + 1) * self.pair)

    def lanes(self, tick, dp):
        across = self.sizes["x"] * self.pair * self.rows
        z = wrap(self.at["ctx"] + self.away[tick], self.line)
        return pl.ds(pl.multiple_of((dp * self.line + z) * across, 128), across)

    def multiply(self, tick, item, left, right):
        start, width = sum(self.widths[:item]), self.widths[item]
        step = math.gcd(width, 512)

        @pl.loop(0, self.sizes["dp"])
        def _(dp):
            left_t = left[dp].T

            @pl.loop(0, width // step)
            def _(part):
                columns = pl.ds(pl.multiple_of(part * step, 128), step)
                into = pl.ds(pl.multiple_of(start + part * step, 128), step)
                product = dot(left_t, right[:, columns]).astype(BF)
                for x in range(self.sizes["x"]):
                    for core in range(self.pair):
                        low = (x * self.pair + core) * self.rows
                        self.terms[tick, dp, x, core, :, into] = product[low : low + self.rows]

    def block_terms(self, index, first_at, other_at):
        name, other = self.axes(index)
        spot = {name: first_at, other: other_at}
        return self.terms.at[index // self.pair, spot["dp"], spot["x"], self.spot_of(index)[1]]

    def landing(self, index, step, place):
        at = (step - 1) * self.sizes[self.axes(index)[1]] + place
        return self.near[self.parity(index)].at[self.slot(index), at]

    def far_landing(self, index, far):
        return self.far_in[self.parity(index)].at[self.slot(index), far - 1]

    def hop_one(self, index, step, place):
        name = self.axes(index)[0]
        to = wrap(self.at[name] + step, self.sizes[name])
        sems = [sem.at[index, step, place] for sem in self.a_sems]
        return remote(
            self.block_terms(index, to, place), self.landing(index, step, place), *sems, **{name: to}
        )

    def hop_two(self, index, far):
        name, other = self.axes(index)
        to = wrap(self.at[other] + far, self.sizes[other])
        sems = [sem.at[index, far] for sem in self.b_sems]
        return remote(
            self.block_terms(index, self.at[name], to), self.far_landing(index, far), *sems, **{other: to}
        )

    def done(self, index):
        name, other = self.axes(index)
        return self.block_terms(index, self.at[name], self.at[other])

    def stays(self, index):
        return self.order[index] == (0, 0)

    def piece_at(self, piece, member):
        out, width, _ = self.pieces[piece]
        return out.at[:, pl.ds(pl.multiple_of(member * width, 128), width)]

    def last(self, index, piece):
        z, c = self.spot_of(index)
        _, width, offset = self.pieces[piece]
        source = self.done(index).at[:, pl.ds(offset, width)]
        target = self.piece_at(piece, self.me)
        if self.stays(index):
            return pltpu.make_async_copy(source, target, self.own_sem.at[piece])
        return remote(source, target, *[sem.at[index, piece] for sem in self.f_sems], ctx=z, core=c)

    def last_came(self, index, piece):
        z, c = self.spot_of(index, -1)
        spot = self.piece_at(piece, z * self.pair + c)
        sems = [sem.at[index, piece] for sem in self.f_sems]
        return remote(spot, spot, *sems, core=self.at["core"])

    def places(self, index):
        other = self.axes(index)[1]
        size = self.sizes[other]
        return [(far, wrap(self.at[other] + far, size)) for far in list(range(1, size)) + [0]]

    def send_one(self, tick):
        for index in self.indices(tick):
            for _, place in self.places(index):
                for step in range(1, self.sizes[self.axes(index)[0]]):
                    self.hop_one(index, step, place).start()

    def sum_one(self, tick):
        for index in self.indices(tick):
            name = self.axes(index)[0]
            for far, place in self.places(index):
                steps = range(1, self.sizes[name])
                for step in steps:
                    self.hop_one(index, step, place).wait_recv()
                kept = self.block_terms(index, self.at[name], place)
                add_rows(self.rows, kept, kept, *[self.landing(index, step, place) for step in steps])
                if far:
                    self.hop_two(index, far).start()

    def sum_two(self, tick):
        for index in self.indices(tick):
            fars = range(1, self.sizes[self.axes(index)[1]])
            for far in fars:
                self.hop_two(index, far).wait_recv()
            done = self.done(index)
            add_rows(self.rows, done, done, *[self.far_landing(index, far) for far in fars])
            for piece in range(len(self.pieces)):
                self.last(index, piece).start()

    def drain(self):
        for index in range(len(self.order)):
            name, other = self.axes(index)
            for step in range(1, self.sizes[name]):
                for place in range(self.sizes[other]):
                    self.hop_one(index, step, place).wait_send()
            for far in range(1, self.sizes[other]):
                self.hop_two(index, far).wait_send()
            for piece in range(len(self.pieces)):
                if self.stays(index):
                    self.last(index, piece).wait()
                else:
                    self.last(index, piece).wait_send()
                    self.last_came(index, piece).wait_recv()


def lane_index(shape):
    return lax.broadcasted_iota(jnp.int32, shape, len(shape) - 1)


def turned(values):
    half, columns = HD // 2, values.shape[1]
    ahead = pltpu.roll(values, columns - half, 1)
    behind = pltpu.roll(values, half, 1)
    return jnp.where(lane_index(values.shape) % HD < half, ahead, behind)


def for_heads(table, columns):
    pair = 2 * HD
    return jnp.concatenate([table[:, :pair]] * ((columns - pair) // pair) + [table[:, pair:]], 1)


def only_head(values, head):
    return jnp.where(lane_index(values.shape) // HD == head, values, jnp.zeros_like(values))


def both_halves(values, head):
    wide = values.astype(F32)
    return jnp.where(lane_index(wide.shape) // HD == head, wide, pltpu.roll(wide, HD, 1)).astype(BF)


def softmax_rows(queries, keys, visible):
    scores = contract_cols(queries, keys) * HD ** (-0.5)
    scores = jnp.where(visible, scores, NEG_FILL)
    exponent = jnp.exp(scores - jnp.max(scores, -1, keepdims=True))
    return exponent / jnp.sum(exponent, -1, keepdims=True)


def query_rows(total_rows):
    return min(total_rows, 2**17 // total_rows)


def opening_kernel(sizes, chunks, *refs):
    line, pair = sizes["ctx"], sizes["core"]
    group = line * pair
    refs = list(refs)

    def take(count):
        taken, refs[:count] = refs[:count], []
        return taken

    qkv_in, out_in, gate_up_in, down_in, gain_in, hidden_ref, cot_ref, rate_ref, pos_col, pos_row = take(10)
    output_ref, middle, gains_ref, cos_ref, sin_ref = take(5)
    low_out, entry_one_out, qkv_out, heads_out, terms_out, entry_two_out, cots_out, act_out, dgu_out = take(9)
    stage, tall, wide, low_w, ffn_w, rows_in, cots, qkv, heads, act, dgu = take(11)
    part, near, landed, total = take(4)
    stage_sem, out_sem, slot_sem, terms_sem = take(4)
    tall_sems, wide_sems, reduce_sems, hidden_sems, travel_sems = take(7), take(7), take(4), take(5), take(5)

    rows, width = part.shape[-2:]
    own_rows = tall.shape[1]
    block_rows = rows * chunks
    tokens = group * rows
    total_rows = cos_ref.shape[0]
    qkv_cols, query_cols = qkv.shape[1], heads.shape[-1]
    units = ffn_w.shape[-1] // 3
    groups = ffn_w.shape[0]
    core, here = lax.axis_index("core"), lax.axis_index("ctx")
    steps, travels, sums = [], [], []
    low, high = Spread(sizes, tall, low_w, tall_sems), Spread(sizes, wide, ffn_w, wide_sems)
    gain_rows = [gains_ref.at[pl.ds(0, 1)], gains_ref.at[pl.ds(1, 1)]]

    def step(time, function, *values):
        steps.append((time, functools.partial(function, *values)))

    def chunk_rows(chunk):
        return slice(chunk * rows, (chunk + 1) * rows)

    def staged(member):
        slot = member % 2
        sources = (
            gate_up_in.at[:, pl.ds(member * units, units)],
            gate_up_in.at[:, pl.ds(FF + member * units, units)],
            down_in.at[:, pl.ds(member * units, units)],
        )
        return [
            pltpu.make_async_copy(
                source, stage.at[slot, :, pl.ds(index * units, units)], stage_sem.at[slot, index]
            )
            for index, source in enumerate(sources)
        ]

    def pack_low():
        keys = KV * HD // group
        heads_of = H * HD // group
        for member in range(group):
            key_at, value_at = H * HD + member * keys, (H + KV) * HD + member * keys
            tall[member, :, :heads_of] = qkv_in[:, member * heads_of : (member + 1) * heads_of].astype(BF)
            both = jnp.concatenate(
                [qkv_in[:, key_at : key_at + keys], qkv_in[:, value_at : value_at + keys]], 1
            )
            tall[member, :, heads_of:qkv_cols] = both.astype(BF)
            tall[member, :, qkv_cols : qkv_cols + heads_of] = out_in[
                :, member * heads_of : (member + 1) * heads_of
            ].astype(BF)
            tall[member, :, qkv_cols + heads_of :] = gain_in[...].astype(BF)

    def pack_high():
        for member in range(group):
            for load in staged(member):
                load.wait()
            wide[member] = stage[member % 2].astype(BF)
            if member + 2 < group:
                for load in staged(member + 2):
                    load.start()

    def columns_of(weight, first, size):
        return weight[:, :, :, first : first + size].reshape(width, size)

    def rows_of(weight, index, count, first, size):
        each = groups // count
        return weight[index * each : (index + 1) * each, :, :, first : first + size].reshape(-1, size)

    def rotary_tables():
        @pl.loop(0, total_rows // block_rows)
        def _(index):
            at = pl.ds(pl.multiple_of(index * block_rows, block_rows), block_rows)
            angle = pos_col[at, :].astype(F32) * rate_ref[...]
            sine = jnp.sin(angle)
            cos_ref[at, :] = jnp.cos(angle)
            sin_ref[at, :] = jnp.where(lane_index(sine.shape) % HD < HD // 2, -sine, sine)

    def gains_to_rows():
        columns = columns_of(low_w, qkv_cols + query_cols, 128).astype(F32)
        gains_ref[...] = columns.T[:8, :]

    def project(sequence):
        weight = columns_of(low_w, 0, qkv_cols)

        @pl.loop(0, line)
        def _(z):
            values = rows_in[:, sequence, z].reshape(block_rows, width).astype(F32)
            inverse = lax.rsqrt(jnp.mean(values * values, -1, keepdims=True) + EPS_NORM)
            entry = (values * inverse * gain_rows[0][...]).astype(BF)
            rows_in[:, sequence, z] = entry.reshape(chunks, rows, width)
            projected = dot(entry, weight)
            table_at = pl.ds(pl.multiple_of(z * block_rows, block_rows), block_rows)
            cosine, sine = for_heads(cos_ref[table_at, :], qkv_cols), for_heads(sin_ref[table_at, :], qkv_cols)
            rotated = projected * cosine + turned(projected) * sine
            at = pl.ds(pl.multiple_of((sequence * line + z) * block_rows, block_rows), block_rows)
            qkv[at, :] = rotated.astype(BF)

    def attention(sequence, first, size, lane):
        start = sequence * total_rows
        both = qkv[start : start + total_rows, query_cols:]
        keys, values = both_halves(both, 0), both_halves(both, 1)
        visible = pos_row[...] <= pos_col[first : first + size, :]
        queries = qkv[start + first : start + first + size, lane : lane + 2 * HD]
        two = [
            dot(softmax_rows(only_head(queries, head), keys, visible).astype(BF), values)
            for head in range(2)
        ]
        merged = jnp.where(lane_index(two[0].shape) < HD, two[0], two[1]).astype(BF)
        from_z, to_z = first // block_rows, (first + size) // block_rows
        heads[sequence, from_z:to_z, :, lane : lane + 2 * HD] = merged.reshape(-1, block_rows, 2 * HD)

    def entry_one_copies():
        return [
            pltpu.make_async_copy(rows_in.at[:, c, z], entry_one_out.at[c, z], out_sem.at[3 + c * line + z])
            for c in range(pair)
            for z in range(line)
        ]

    whole_copies = [
        pltpu.make_async_copy(low_w, low_out, out_sem.at[0]),
        pltpu.make_async_copy(qkv, qkv_out, out_sem.at[1]),
        pltpu.make_async_copy(heads, heads_out, out_sem.at[2]),
    ]

    def chunk_copies(chunk):
        return [
            pltpu.make_async_copy(source, target.at[chunk], slot_sem.at[chunk, index])
            for index, (source, target) in enumerate(
                (
                    (act.at[chunk % 2], act_out),
                    (dgu.at[chunk % 2], dgu_out),
                    (rows_in.at[chunk], entry_two_out),
                    (cots.at[chunk], cots_out),
                )
            )
        ]

    def start_all(copies):
        for copy in copies:
            copy.start()

    def wait_all(copies):
        for copy in copies:
            copy.wait()

    def reducer(kind, chunk):
        one = Reduce(line, pair, part, near, landed, *reduce_sems, (kind // 2, chunk), kind)
        sums.append(one)
        return one

    def traveller(sems, source, place, start, hop):
        one = Travel(line, pair, [source], [place], *sems)
        steps.append((start, one.begin))
        for index in range(line - 1):
            steps.append((start + (index + 1) * hop, functools.partial(one.step, index)))
        finish = start + line * hop - 1.0
        steps.append((finish, one.end))
        return finish

    def product(chunk):
        mine = heads[:, :, chunk_rows(chunk), :].reshape(tokens, query_cols)
        for index in range(4):
            at = slice(index * (width // 4), (index + 1) * (width // 4))
            term = contract_cols(mine, rows_of(low_w, index, 4, qkv_cols, query_cols)).astype(BF)
            part[0, chunk, :, :, :, at] = term.reshape(pair, line, rows, -1)

    def norm_rows(chunk):
        mid = hidden_ref[chunk].astype(F32) + total[...]
        middle[chunk_rows(chunk), :] = mid
        inverse = lax.rsqrt(jnp.mean(mid * mid, -1, keepdims=True) + EPS_NORM)
        rows_in[chunk, core, here] = (mid * inverse * gain_rows[1][...]).astype(BF)

    def units_part(chunk, index, count):
        size = units // count
        slot = chunk % 2
        entry = rows_in[chunk].reshape(tokens, width)
        first, last = index * size, (index + 1) * size
        gate = dot(entry, columns_of(ffn_w, first, size))
        up = dot(entry, columns_of(ffn_w, units + first, size))
        grad_act = dot(cots[chunk].reshape(tokens, width), columns_of(ffn_w, 2 * units + first, size))
        sigmoid = 1.0 / (1.0 + jnp.exp(-gate))
        silu = gate * sigmoid
        act[slot, :, first:last] = (silu * up).astype(BF)
        dgu[slot, :, first:last] = (grad_act * up * sigmoid * (1.0 + gate * (1.0 - sigmoid))).astype(BF)
        dgu[slot, :, units + first : units + last] = (grad_act * silu).astype(BF)

    def back_part(chunk, index, count):
        size = width // count
        at = slice(index * size, (index + 1) * size)
        term = contract_cols(dgu[chunk % 2], rows_of(ffn_w, index, count, 0, 2 * units)).astype(BF)
        part[0, chunk, :, :, :, at] = term.reshape(pair, line, rows, size)

    def down_part(chunk, index, count):
        size = width // count
        at = slice(index * size, (index + 1) * size)
        term = contract_cols(act[chunk % 2], rows_of(ffn_w, index, count, 2 * units, units)).astype(BF)
        part[1, chunk, :, :, :, at] = term.reshape(pair, line, rows, size)

    def terms_copy(chunk):
        return pltpu.make_async_copy(part.at[0, chunk], terms_out.at[chunk], terms_sem.at[chunk])

    def write_output(chunk):
        output_ref[chunk_rows(chunk), :] = (middle[chunk_rows(chunk), :] + total[...]).astype(BF)

    for member in range(2):
        start_all(staged(member))
    greet_all(sizes)

    step(0.0, pack_low)
    hidden_done = traveller(
        hidden_sems, hidden_ref, lambda c, z: rows_in.at[:, c, z], 0.0, T_HIDDEN
    )
    step(0.1, low.begin, *range(group))
    step(0.2, pack_high)
    step(0.3, high.begin, *range(min(group, 4)))
    step(9.0, rotary_tables)
    for index in range(group):
        when = 1.0 + T_LOW * (index // 2)
        step(when, low.onward, index)
        step(when + T_LOW + 1.0, low.onward_two, index)
        when = 1.0 + T_HIGH * (index // 2)
        step(when, high.onward, index, *([index + 2] if index >= 2 else []))
        step(when + T_HIGH * 0.6, high.onward_two, index)
    weights_there = 1.0 + T_HIGH * (group // 2) + 8.0

    now = max(hidden_done + 0.2, 1.0 + T_LOW * (group // 2) + 6.0)
    step(now, low.complete, *range(group))
    step(now, gains_to_rows)
    step(now, whole_copies[0].start)
    for sequence in range(pair * line * block_rows // total_rows):
        step(now + 0.1, project, sequence)
        now += 2.5
    step(now, start_all, entry_one_copies())
    step(now, whole_copies[1].start)
    size = query_rows(total_rows)
    for sequence in range(pair * line * block_rows // total_rows):
        for first in range(0, total_rows, size):
            for lane in range(0, query_cols, 2 * HD):
                step(now + 0.1, attention, sequence, first, size, lane)
                now += 1.0
    step(now, whole_copies[2].start)
    step(now, wait_all, entry_one_copies())

    span = (line - 1) * SEND
    ready_ffn, ready_back, base = weights_there, 0.0, now + 0.5
    count = 4
    for chunk in range(chunks):
        cot_done = traveller(
            [sem.at[0, chunk] for sem in travel_sems],
            cot_ref.at[chunk],
            lambda c, z, k=chunk: cots.at[k, c, z],
            base + chunk * span,
            HOP,
        )
        begin = base + 1.0 + chunk * span
        step(begin - 0.5, product, chunk)
        first_sum = reducer(0, chunk)
        more, finish = first_sum.plan(begin, total, functools.partial(norm_rows, chunk))
        steps.extend(more)
        arrived = traveller(
            [sem.at[1, chunk] for sem in travel_sems],
            None,
            lambda c, z, k=chunk: rows_in.at[k, c, z],
            finish,
            HOP,
        )
        begin = max(arrived, cot_done, ready_ffn) + 0.1
        if chunk == 0:
            step(begin, high.complete, *range(group))
        if chunk >= 2:
            step(begin, wait_all, chunk_copies(chunk - 2))
        step(begin, first_sum.drain)
        for index in range(count):
            step(begin + index, units_part, chunk, index, count)
        for index in range(count):
            step(begin + 4 + 0.5 * index, down_part, chunk, index, count)
        for index in range(count):
            step(begin + 6.3 + 0.8 * index, back_part, chunk, index, count)
        step(begin + 4.0, start_all, chunk_copies(chunk))
        step(begin + 9.4, terms_copy(chunk).start)
        ready_ffn = begin + 9.5
        begin = max(begin + 6.2, ready_back)
        ready_back = begin + span
        steps.extend(reducer(2, chunk).plan(begin, total, functools.partial(write_output, chunk))[0])
    run_steps(steps)
    for one in sums:
        if one.sem_at[0]:
            one.drain()
    low.drain()
    high.drain()
    wait_all(whole_copies)
    wait_all([terms_copy(chunk) for chunk in range(chunks)])
    for chunk in range(max(0, chunks - 2), chunks):
        wait_all(chunk_copies(chunk))


T_HIDDEN, T_LOW, T_HIGH = 14.0, 7.0, 28.0


def opening(sizes, collective_id, weights, gains, hidden, cot, tables):
    line, pair = sizes["ctx"], sizes["core"]
    group = line * pair
    block_rows, width = hidden.shape
    chunks = 4
    rows = block_rows // chunks
    tokens = group * rows
    own_rows = weights[0].shape[0]
    heads, keys, units = H * HD // group, KV * HD // group, FF // group
    qkv_cols = heads + 2 * keys
    tall, wide = qkv_cols + heads + 128, 3 * units
    blocks = (sizes["dp"] * line, sizes["x"] * pair, own_rows)
    gain_tile = jnp.pad(gains.T, ((0, 0), (0, 126)))
    any_spec = pl.BlockSpec(memory_space=pl.ANY)
    vmem = pl.BlockSpec(memory_space=pltpu.VMEM)
    shape = jax.ShapeDtypeStruct
    dma = pltpu.SemaphoreType.DMA
    by_chunk = (chunks, pair, line, rows, width)
    outs = pl.pallas_call(
        functools.partial(opening_kernel, sizes, chunks),
        out_shape=[
            shape((block_rows, width), BF),
            shape((block_rows, width), F32),
            shape((8, width), F32),
            shape((tables[1].shape[0], 4 * HD), F32),
            shape((tables[1].shape[0], 4 * HD), F32),
            shape(blocks + (tall,), BF),
            shape((pair, line, chunks, rows, width), BF),
            shape((group * block_rows, qkv_cols), BF),
            shape((pair, line, block_rows, heads), BF),
            shape(by_chunk, BF),
            shape(by_chunk, BF),
            shape(by_chunk, BF),
            shape((chunks, tokens, units), BF),
            shape((chunks, tokens, 2 * units), BF),
        ],
        in_specs=[vmem, vmem, any_spec, any_spec] + [vmem] * 6,
        out_specs=[vmem] * 5 + [any_spec] * 9,
        scratch_shapes=[
            pltpu.VMEM((2, own_rows, wide), F32),
            pltpu.VMEM((group, own_rows, tall), BF),
            pltpu.VMEM((group, own_rows, wide), BF),
            pltpu.VMEM(blocks + (tall,), BF),
            pltpu.VMEM(blocks + (wide,), BF),
            pltpu.VMEM(by_chunk, BF),
            pltpu.VMEM(by_chunk, BF),
            pltpu.VMEM((group * block_rows, qkv_cols), BF),
            pltpu.VMEM((pair, line, block_rows, heads), BF),
            pltpu.VMEM((2, tokens, units), BF),
            pltpu.VMEM((2, tokens, 2 * units), BF),
            *Reduce.room(line, pair, rows, width, 2, chunks),
            pltpu.VMEM((rows, width), F32),
            dma((2, 3)),
            dma((3 + group,)),
            dma((chunks, 4)),
            dma((chunks,)),
            *Spread.sems(sizes),
            *Spread.sems(sizes),
            *Reduce.sems(3, chunks)(line),
            *Travel.sems(1, line),
            dma((2, chunks, 1)),
            *[dma((2, chunks, 1, 2, line))] * 4,
        ],
        compiler_params=pltpu.CompilerParams(
            collective_id=collective_id, has_side_effects=True, vmem_limit_bytes=63 * 2**20
        ),
    )(*weights, gain_tile, hidden.reshape(chunks, rows, width), cot.reshape(chunks, rows, width), *tables)
    output, middle, gain_rows, cosines, sines, low, entry_one, qkv, attended, terms, *rest = outs
    flat = [array.reshape(-1, array.shape[-1]) for array in (entry_one, qkv, attended, *rest)]
    return output, middle, gain_rows, (cosines, sines), low.reshape(width, tall), terms, flat


class GainSum:
    @staticmethod
    def room(sizes, width):
        group = sizes["ctx"] * sizes["core"]
        return [
            pltpu.VMEM((8, width), F32),
            pltpu.VMEM((sizes["x"] - 1, 8, width), F32),
            pltpu.VMEM((sizes["dp"] - 1, 8, width), F32),
            pltpu.VMEM((group, 8, 128), F32),
        ]

    @staticmethod
    def sems(sizes):
        group = sizes["ctx"] * sizes["core"]
        counts = (sizes["x"], sizes["x"], sizes["dp"], sizes["dp"], group, group)
        return [pltpu.SemaphoreType.DMA((count,)) for count in counts]

    def __init__(self, sizes, own_rows, out_ref, room, sems):
        self.sizes, self.own_rows, self.out_ref = sizes, own_rows, out_ref
        self.mine, self.over_x, self.over_dp, self.tiles = room
        self.sems_of = {"x": sems[0:2], "dp": sems[2:4], "group": sems[4:6]}
        self.at = {name: lax.axis_index(name) for name in ("dp", "ctx", "x", "core")}
        self.order = blocks_in_order(sizes["ctx"], sizes["core"])

    def hop(self, name, step):
        into = (self.over_x if name == "x" else self.over_dp).at[step - 1]
        sems = [sem.at[step] for sem in self.sems_of[name]]
        return remote(self.mine, into, *sems, **{name: wrap(self.at[name] + step, self.sizes[name])})

    def tile(self, index):
        dz, dc = self.order[index]
        z, c = wrap(self.at["ctx"] + dz, self.sizes["ctx"]), wrap(self.at["core"] + dc, self.sizes["core"])
        place = (self.at["dp"] * self.sizes["ctx"] + z) * self.sizes["x"] + self.at["x"]
        first = (place * self.sizes["core"] + c) * self.own_rows
        source = self.mine.at[:, pl.ds(pl.multiple_of(first // 128 * 128, 128), 128)]
        sems = [sem.at[index] for sem in self.sems_of["group"]]
        if index == 0:
            return source
        return remote(source, self.tiles.at[index], *sems, ctx=z, core=c)

    def begin(self, first, second):
        self.mine[...] = jnp.zeros_like(self.mine)
        self.mine[0:1, :] = first[...]
        self.mine[1:2, :] = second[...]
        self.send("x")

    def send(self, name):
        for step in range(1, self.sizes[name]):
            self.hop(name, step).start()

    def add(self, name):
        for step in range(1, self.sizes[name]):
            self.hop(name, step).wait()
        for step in range(1, self.sizes[name]):
            self.mine[...] += (self.over_x if name == "x" else self.over_dp)[step - 1]

    def second(self):
        self.add("x")
        self.send("dp")

    def third(self):
        self.add("dp")
        for index in range(1, len(self.order)):
            self.tile(index).start()

    def end(self):
        total = self.tile(0)[...]
        for index in range(1, len(self.order)):
            self.tile(index).wait()
            total = total + self.tiles[index]
        self.out_ref[...] = total


def closing_kernel(sizes, chunks, *refs):
    refs = list(refs)

    def take(count):
        taken, refs[:count] = refs[:count], []
        return taken

    entry_two, dgu_ref, cots_ref, act_ref, entry_one, heads_ref, low_ref, terms_ref = take(8)
    qkv_ref, hidden_ref, cot_ref, middle_ref, gains_ref, cos_ref, sin_ref, pos_col, pos_row = take(9)
    piece_refs, (branch_ref, grad_hidden_ref, gain_sum_ref) = take(6), take(3)
    left_slots, dgu, part, act, dqkv, heads, branch_slots, low_w, grad_heads, grad_proj, key_acc, value_acc = take(12)
    near, landed, total, grad_mid, branch, load_sem, left_sem, branch_sem = take(8)
    ffn_room, att_room = take(5), take(5)
    ffn_sems, att_sems, reduce_sems = take(7), take(7), take(4)
    gain_grad, gain_room, gain_sems = take(2), take(4), take(6)
    travel_sems = take(5)
    line, pair = sizes["ctx"], sizes["core"]
    rows = part.shape[-2]
    block_rows, width = hidden_ref.shape
    tokens, total_rows = qkv_ref.shape[0], cos_ref.shape[0]
    query_cols = heads.shape[1]
    qkv_cols = dqkv.shape[1]
    loads = {
        "dgu": pltpu.make_async_copy(dgu_ref, dgu, load_sem.at[0]),
        "act": pltpu.make_async_copy(act_ref, act, load_sem.at[1]),
        "heads": pltpu.make_async_copy(heads_ref, heads, load_sem.at[2]),
        "low": pltpu.make_async_copy(low_ref.at[:, pl.ds(0, low_w.shape[1])], low_w, load_sem.at[3]),
    }
    names = grad_pieces(sizes)
    shift = names[3][2]
    ffn_pieces = [(ref, w, o) for ref, (_, w, o) in zip(piece_refs[:3], names[:3])]
    att_pieces = [(ref, w, o - shift) for ref, (_, w, o) in zip(piece_refs[3:], names[3:])]
    ffn = Collect(sizes, (2 * act.shape[1], act.shape[1]), ffn_pieces, ffn_room, ffn_sems)
    att = Collect(sizes, (qkv_cols, query_cols), att_pieces, att_room, att_sems)
    entry_sums, sums = [
        [Reduce(line, pair, part, near, landed, *reduce_sems, (chunk,), kind) for chunk in range(chunks)]
        for kind in range(2)
    ]
    term_loads = [
        pltpu.make_async_copy(terms_ref.at[chunk], part.at[chunk], load_sem.at[4 + chunk])
        for chunk in range(chunks)
    ]
    gain_sum = GainSum(sizes, ffn.rows, gain_sum_ref, gain_room, gain_sems)

    def left_loads(turn, item):
        one, sources = (ffn, (entry_two, cots_ref)) if turn < line else (att, (entry_one, branch_ref))
        return [
            pltpu.make_async_copy(
                sources[item].at[:, one.lanes(turn % line, dp)], left_slots.at[item, dp], left_sem.at[item, dp]
            )
            for dp in range(sizes["dp"])
        ]

    def branch_load(index):
        size = branch_slots.shape[1]
        return pltpu.make_async_copy(
            branch_ref.at[pl.ds(index * size, size)], branch_slots.at[index % 2], branch_sem.at[index % 2]
        )

    for load in term_loads + left_loads(0, 0) + list(loads.values()) + left_loads(0, 1):
        load.start()
    greet_all(sizes)

    def multiply(turn):
        one, rights = (ffn, (dgu, act)) if turn < line else (att, (dqkv, heads))
        for item in range(2):
            for load in left_loads(turn, item):
                load.wait()
            one.multiply(turn % line, item, left_slots.at[item], rights[item])
            if turn % line < line - 1:
                for load in left_loads(turn + 1, item):
                    load.start()

    def later_loads():
        for load in left_loads(line, 0) + left_loads(line, 1):
            load.start()

    def back_to_heads():
        loads["low"].wait()
        size = branch_slots.shape[1]
        branch_load(0).start()
        for index in range(tokens // size):
            if index + 1 < tokens // size:
                branch_load(index + 1).start()
            branch_load(index).wait()
            grad_heads[index * size : (index + 1) * size, :] = dot(
                branch_slots[index % 2], low_w[:, qkv_cols:]
            ).astype(BF)

    def attention_part(sequence, low, size, lane):
        start = sequence * total_rows
        span = slice(start, start + total_rows)
        at = slice(start + low, start + low + size)
        both = qkv_ref[span, query_cols:]
        keys, values = both_halves(both, 0), both_halves(both, 1)
        visible = pos_row[...] <= pos_col[low : low + size, :]
        queries = qkv_ref[at, lane : lane + 2 * HD]
        grads = grad_heads[at, lane : lane + 2 * HD]
        grad_queries = []
        key_term = value_term = None
        for head in range(2):
            query, grad = only_head(queries, head), only_head(grads, head)
            probability = softmax_rows(query, keys, visible)
            grad_prob = contract_cols(grad, values)
            delta = jnp.sum(probability * grad_prob, -1, keepdims=True)
            grad_scores = jnp.where(visible, probability * (grad_prob - delta), 0.0).astype(BF)
            grad_queries.append(dot(grad_scores, keys))
            key_more = contract_rows(grad_scores, query)
            value_more = contract_rows(probability.astype(BF), grad)
            key_term = key_more if key_term is None else key_term + key_more
            value_term = value_more if value_term is None else value_term + value_more
        scale = HD ** (-0.5)
        grad_proj[low : low + size, lane : lane + 2 * HD] = scale * jnp.where(
            lane_index(grad_queries[0].shape) < HD, grad_queries[0], grad_queries[1]
        )
        if low == 0 and lane == 0:
            key_acc[...] = key_term * scale
            value_acc[...] = value_term
        else:
            key_acc[...] += key_term * scale
            value_acc[...] += value_term

    def rotate_back(sequence):
        keys, values = key_acc[...], value_acc[...]
        grad_proj[:, query_cols:] = jnp.where(
            lane_index(keys.shape) < HD, keys + pltpu.roll(keys, HD, 1), values + pltpu.roll(values, HD, 1)
        )
        for low in range(0, total_rows, 256):
            size = min(256, total_rows - low)
            grads = grad_proj[low : low + size, :]
            cosine = for_heads(cos_ref[low : low + size, :], qkv_cols)
            sine = for_heads(sin_ref[low : low + size, :], qkv_cols)
            back = grads * cosine + turned(grads * sine)
            at = sequence * total_rows + low
            dqkv[at : at + size, :] = back.astype(BF)

    def entry_terms(chunk):
        mine = jnp.concatenate(
            [
                dqkv[(c * line + z) * block_rows + chunk * rows : (c * line + z) * block_rows + (chunk + 1) * rows, :]
                for c in range(pair)
                for z in range(line)
            ],
            0,
        )
        for low in range(0, width, 512):
            term = contract_cols(mine, low_w[low : low + 512, :qkv_cols]).astype(BF)
            part[chunk, :, :, :, low : low + 512] = term.reshape(pair, line, rows, 512)

    def norm_back(values, which, chunk):
        inverse = lax.rsqrt(jnp.mean(values * values, -1, keepdims=True) + EPS_NORM)
        normed = values * inverse
        grad_entry = total[...]
        gain_term = jnp.sum(grad_entry * normed, 0, keepdims=True)
        if chunk == 0:
            gain_grad[which][...] = gain_term
        else:
            gain_grad[which][...] += gain_term
        grad_normed = grad_entry * gains_ref[which : which + 1, :]
        return inverse * (grad_normed - normed * jnp.mean(grad_normed * normed, -1, keepdims=True))

    def middle_back(chunk):
        at = slice(chunk * rows, (chunk + 1) * rows)
        grad = cot_ref[at, :].astype(F32) + norm_back(middle_ref[at, :], 1, chunk)
        grad_mid[at, :] = grad
        branch[chunk] = grad.astype(BF)

    def hidden_back(chunk):
        at = slice(chunk * rows, (chunk + 1) * rows)
        grad = grad_mid[at, :] + norm_back(hidden_ref[at, :].astype(F32), 0, chunk)
        grad_hidden_ref[at, :] = grad.astype(BF)

    steps = []

    def step(time, function, *values):
        steps.append((time, functools.partial(function, *values)))

    step(0.0, loads["dgu"].wait)
    step(0.0, loads["act"].wait)
    span = (line - 1) * SEND
    gathered = 0.0
    for chunk, one in enumerate(entry_sums):
        start = 1.0 + chunk * span
        step(start - 0.1, term_loads[chunk].wait)
        more, finish = one.plan(start, total, functools.partial(middle_back, chunk))
        steps += more
        travel = Travel(
            line,
            pair,
            [branch.at[chunk]],
            [lambda c, z, k=chunk: branch_ref.at[pl.ds(((c * line + z) * chunks + k) * rows, rows)]],
            *[sem.at[chunk] for sem in travel_sems],
        )
        step(finish, travel.begin)
        for index in range(line - 1):
            step(finish + (index + 1) * HOP, travel.step, index)
        gathered = finish + line * HOP - 1.0
        step(gathered, travel.end)
    period, before = PERIOD, BEFORE
    for tick in range(line):
        arrived = before + period * tick
        issued = 5.5 * (tick + 1) if tick < 2 else before + period * (tick - 2) + 0.5
        step(issued - 5.0 if tick < 2 else issued - 5.5, multiply, tick)
        step(issued, ffn.send_one, tick)
        step(arrived, ffn.sum_one, tick)
        step(arrived + 18.0, ffn.sum_two, tick)
    now = gathered + 0.1
    step(now, back_to_heads)
    last_multiply = max(5.5 * 2, before + period * (line - 3)) + 0.6
    step(max(now, last_multiply), later_loads)
    now += 3.0
    for sequence in range(tokens // total_rows):
        size = query_rows(total_rows)
        for low in range(0, total_rows, size):
            for lane in range(0, query_cols, 2 * HD):
                step(now, attention_part, sequence, low, size, lane)
                now += 3.0
        step(now, rotate_back, sequence)
        now += 0.5
    step(now, loads["heads"].wait)
    begin = now + 1.0
    for chunk, one in enumerate(sums):
        step(now + 0.5 + chunk, entry_sums[chunk].drain)
        step(now + 0.5 + chunk, entry_terms, chunk)
        start = begin + chunk * span
        more, finish = one.plan(start, total, functools.partial(hidden_back, chunk))
        steps += more
    step(finish + 0.2, gain_sum.begin, *gain_grad)
    step(finish + 4.0, gain_sum.second)
    step(finish + 8.0, gain_sum.third)
    step(finish + 12.0, gain_sum.end)
    now = max(now + 1.0 + chunks, last_multiply + 1.0)
    for tick in range(line):
        step(now + tick, multiply, line + tick)
        step(now + tick + 0.5, att.send_one, tick)
        arrived = now + ATT_WAIT + 2.0 * tick
        step(arrived, att.sum_one, tick)
        step(arrived + 12.5, att.sum_two, tick)
    run_steps(steps)
    for one in sums + [ffn, att]:
        one.drain()


PERIOD, BEFORE, ATT_WAIT = 26.0, 40.0, 40.0


def closing(sizes, collective_id, factors, low, terms, hidden, cot, middle, gains, tables):
    line, pair = sizes["ctx"], sizes["core"]
    group = line * pair
    block_rows, width = hidden.shape
    tokens = block_rows * group
    chunks = 4
    rows = block_rows // chunks
    own_rows = width // (group * sizes["dp"] * sizes["x"])
    units = factors[3].shape[1]
    qkv_cols, query_cols = factors[6].shape[1], factors[5].shape[1]
    total_rows = tables[0].shape[0]
    pieces = grad_pieces(sizes)
    any_spec = pl.BlockSpec(memory_space=pl.ANY)
    vmem = pl.BlockSpec(memory_space=pltpu.VMEM)
    dma = pltpu.SemaphoreType.DMA
    shape = jax.ShapeDtypeStruct
    across = sizes["x"] * pair * own_rows
    branch_rows = 128
    part_shape = (chunks, pair, line, rows, width)
    return pl.pallas_call(
        functools.partial(closing_kernel, sizes, chunks),
        out_shape=[shape((own_rows, group * w), BF) for _, w, _ in pieces]
        + [shape((tokens, width), BF), shape((block_rows, width), BF), shape((8, 128), F32)],
        in_specs=[any_spec] * 8 + [vmem] * 9,
        out_specs=[any_spec] * (len(pieces) + 1) + [vmem] * 2,
        scratch_shapes=[
            pltpu.VMEM((2, sizes["dp"], tokens, across), BF),
            pltpu.VMEM((tokens, 2 * units), BF),
            pltpu.VMEM(part_shape, BF),
            pltpu.VMEM((tokens, units), BF),
            pltpu.VMEM((tokens, qkv_cols), BF),
            pltpu.VMEM((tokens, query_cols), BF),
            pltpu.VMEM((2, branch_rows, width), BF),
            pltpu.VMEM((width, qkv_cols + query_cols), BF),
            pltpu.VMEM((tokens, query_cols), BF),
            pltpu.VMEM((total_rows, qkv_cols), F32),
            pltpu.VMEM((total_rows, 2 * HD), F32),
            pltpu.VMEM((total_rows, 2 * HD), F32),
            *Reduce.room(line, pair, rows, width, chunks)[1:],
            pltpu.VMEM((rows, width), F32),
            pltpu.VMEM((block_rows, width), F32),
            pltpu.VMEM((chunks, rows, width), BF),
            dma((4 + chunks,)),
            dma((2, sizes["dp"])),
            dma((2,)),
            *Collect.room(sizes, own_rows, 3 * units),
            *Collect.room(sizes, own_rows, qkv_cols + query_cols),
            *Collect.sems(sizes, 3),
            *Collect.sems(sizes, 3),
            *Reduce.sems(2, chunks)(line),
            pltpu.VMEM((1, width), F32),
            pltpu.VMEM((1, width), F32),
            *GainSum.room(sizes, width),
            *GainSum.sems(sizes),
            dma((chunks, 1)),
            *[dma((chunks, 1, 2, line))] * 4,
        ],
        compiler_params=pltpu.CompilerParams(
            collective_id=collective_id, has_side_effects=True, vmem_limit_bytes=63 * 2**20
        ),
    )(*factors[:6], low, terms, factors[6], hidden, cot, middle, gains, *tables)


def grad_pieces(sizes):
    group = sizes["ctx"] * sizes["core"]
    heads, keys, units = H * HD // group, KV * HD // group, FF // group
    pieces, offset = [], 0
    for name, width in (
        ("gate", units),
        ("up", units),
        ("down", units),
        ("query", heads),
        ("key_value", 2 * keys),
        ("out", heads),
    ):
        pieces.append((name, width, offset))
        offset += width
    return pieces


def adamw_kernel(step_rate, decay_rate, grad_ref, weight_ref, state_ref, grad_out, weight_out, state_out):
    gradient = grad_ref[...].astype(F32)
    grad_out[...] = gradient
    updated, states = adamw(weight_ref[...], gradient, state_ref[...], step_rate, decay_rate)
    weight_out[...] = updated
    state_out[...] = states


def adamw_columns(gradient, weight, states, step_rate, decay_rate):
    rows, columns = weight.shape
    step = math.gcd(columns, 4096)
    while rows * step > 2**18 and step % 256 == 0:
        step //= 2
    flat = pl.BlockSpec((rows, step), lambda i: (0, i))
    deep = pl.BlockSpec((2, rows, step), lambda i: (0, 0, i))
    return pl.pallas_call(
        functools.partial(adamw_kernel, step_rate, decay_rate),
        grid=(columns // step,),
        out_shape=[
            jax.ShapeDtypeStruct(weight.shape, F32),
            jax.ShapeDtypeStruct(weight.shape, F32),
            jax.ShapeDtypeStruct(states.shape, F32),
        ],
        in_specs=[flat, flat, deep],
        out_specs=[flat, flat, deep],
        compiler_params=pltpu.CompilerParams(vmem_limit_bytes=40 * 2**20),
    )(gradient, weight, states)


def dot(left, right):
    return jnp.dot(left, right, preferred_element_type=F32)


def shards(
    sizes,
    hidden,
    cotangent,
    span_order,
    norm_gains,
    w_qkv,
    w_out,
    w_gate_up,
    w_down,
    mom_gains,
    mom_qkv,
    mom_out,
    mom_gate_up,
    mom_down,
):
    everyone = ("dp", "ctx", "x", "core")
    line, pair = sizes["ctx"], sizes["core"]
    group = line * pair
    block_rows, width = hidden.shape[1:]
    total_rows = block_rows * line
    span_rows = total_rows // span_order.shape[0]
    heads, kv_heads = H // group, KV // group
    query_cols, kv_cols = heads * HD, kv_heads * HD
    key_pos = (
        span_order[:, None] * span_rows + jnp.arange(span_rows, dtype=jnp.int32)[None, :]
    ).reshape(-1)
    positions = (key_pos[:, None], key_pos[None, :])
    rates = jnp.concatenate([rope_rates()] * 6 + [jnp.zeros(HD, jnp.float32)])[None]
    weights = (w_qkv, w_out, w_gate_up, w_down)
    output, middle, gains, turns, low, terms, flat = opening(
        sizes, 0, weights, norm_gains, hidden[0], cotangent[0], (rates,) + positions
    )
    entry_one, qkv, attended, entry_two, cot, activated, grad_gu = flat
    factors = (entry_two, grad_gu, cot, activated, entry_one, attended, qkv)
    *pieces, _, grad_hidden, gain_sums = closing(
        sizes, 1, factors, low, terms, hidden[0], cotangent[0], middle, gains, turns + positions
    )
    grad_gate, grad_up, grad_down, grad_query, grad_key_value, grad_out = pieces
    output, grad_hidden = output[None], grad_hidden[None]
    rows = w_qkv.shape[0]
    place = lax.axis_index(everyone) * rows
    grad_gains = lax.dynamic_slice(gain_sums, (0, lax.rem(place, 128)), (2, rows))
    grad_key_value = grad_key_value.reshape(rows, group, 2, kv_cols).transpose(0, 2, 1, 3)
    grad_qkv = jnp.concatenate([grad_query, grad_key_value.reshape(rows, -1)], 1)
    grad_gate_up = jnp.concatenate([grad_gate, grad_up], 1)
    new_gains, new_mom_gains = adamw(norm_gains, grad_gains, mom_gains, LR_GAIN, 0.0)
    grad_qkv, new_qkv, new_mom_qkv = adamw_columns(grad_qkv, w_qkv, mom_qkv, LR_MATRIX, DECAY_MATRIX)
    grad_out, new_out, new_mom_out = adamw_columns(grad_out, w_out, mom_out, LR_OUTPUT, DECAY_MATRIX)
    grad_gate_up, new_gate_up, new_mom_gate_up = adamw_columns(
        grad_gate_up, w_gate_up, mom_gate_up, LR_MATRIX, DECAY_MATRIX
    )
    grad_down, new_down, new_mom_down = adamw_columns(
        grad_down, w_down, mom_down, LR_MATRIX, DECAY_MATRIX
    )
    return (
        output,
        grad_hidden,
        grad_gains,
        grad_qkv,
        grad_out,
        grad_gate_up,
        grad_down,
        new_gains,
        new_qkv,
        new_out,
        new_gate_up,
        new_down,
        new_mom_gains,
        new_mom_qkv,
        new_mom_out,
        new_mom_gate_up,
        new_mom_down,
    )


def solution(mesh):
    shape = dict(mesh.shape)
    pair = 2 if shape["ctx"] * 2 <= KV and shape["fsdp"] % 2 == 0 else 1
    sizes = {"dp": shape["dp"], "ctx": shape["ctx"], "x": shape["fsdp"] // pair, "core": pair}
    finer = Mesh(mesh.devices.reshape(tuple(sizes.values())), tuple(sizes))
    tokens = P(("dp", "x", "core"), "ctx", None)
    everyone = ("dp", "ctx", "x", "core")
    rows, gains = P(everyone, None), P(None, everyone)
    row_moments, gain_moments = P(None, everyone, None), P(None, None, everyone)
    weights = (gains, rows, rows, rows, rows)
    moments = (gain_moments, row_moments, row_moments, row_moments, row_moments)
    return jax.shard_map(
        functools.partial(shards, sizes),
        mesh=finer,
        in_specs=(tokens, tokens, P()) + weights + moments,
        out_specs=(tokens, tokens) + weights + weights + moments,
        check_vma=False,
    )
```
